512 devices in a mesh: lon: 32 (over z, x_hi), lat: 16 (over y, x_lo, core).
Axes of the slice: x: 4 (x_hi: 2, x_lo: 2; x = x_hi * 2 + x_lo), y: 4, z: 16, core: 2. Of those that a mesh axis runs over, the one named last changes fastest.
Arguments:
- features: bfloat16 [256, 512, 180], P('lat', 'lon'), may hold values from -6 to 6
- cotangent: bfloat16 [256, 512, 180], P('lat', 'lon'), may hold values from -6 to 6
- first_gain: float32 [180], replicated, may hold values from 0.25 to 1.75
- window_qkv: bfloat16 [180, 540], replicated, may hold values from -0.4375 to 0.4375
- window_proj: bfloat16 [180, 180], replicated, may hold values from -0.4375 to 0.4375
- window_table: float32 [6, 961], replicated, may hold values from -3 to 300
- second_gain: float32 [180], replicated, may hold values from 0.25 to 1.75
- cross_qkv: bfloat16 [180, 540], replicated, may hold values from -0.4375 to 0.4375
- cross_proj: bfloat16 [180, 180], replicated, may hold values from -0.4375 to 0.4375
- cross_table: float32 [6, 1521], replicated, may hold values from -3 to 300
Outputs:
- grad_features: float32 [256, 512, 180], P('lat', 'lon')
- grad_window_table: float32 [6, 961], replicated
- grad_cross_table: float32 [6, 1521], replicated
The draws below stay inside these ranges and needn't reach their ends.
All inputs are finite; a program needn't handle non-finite values.
Results may differ from the reference program's by a relative error of at most 0.017.
Values may be sent and summed in bfloat16 or wider, within the bound.
A program may use at most 192 MiB of HBM per device.

```python
import jax
import jax.numpy as jnp
from jax import lax

CHANNELS = 180
NUM_HEADS = 6
WINDOW = 16
KEY_WINDOW = 24
WIN_SHIFT = 8
KEY_RIM = 4
WINDOW_SPAN = 31
CROSS_SPAN = 39
LAT_ALL = 256
LON_ALL = 512


def draw_window_table(key, part):
    key = jax.random.fold_in(key, 11)
    entry_count = WINDOW_SPAN * WINDOW_SPAN
    return jnp.clip(jax.random.normal(key, (NUM_HEADS, entry_count), jnp.float32), -3.0, 3.0)


def draw_cross_table(key, part):
    key = jax.random.fold_in(key, 23)
    entry_count = CROSS_SPAN * CROSS_SPAN
    return jnp.clip(jax.random.normal(key, (NUM_HEADS, entry_count), jnp.float32), -3.0, 3.0)


def shard_levels(rng, shape, split, smallest, top_value):
    factor_of = 1.0
    for axis_at, shards_of in split:
        draws = jax.random.uniform(jax.random.fold_in(jax.random.fold_in(rng, 6), axis_at), (shards_of,), jnp.float32, smallest / len(split), top_value / len(split))
        factor_of = factor_of * jnp.repeat(jnp.exp(draws), shape[axis_at] // shards_of).reshape((-1,) + (1,) * (len(shape) - 1 - axis_at))
    return factor_of


def scatter_about(own_key, extent, width, reach, cuts=(), kind=jnp.bfloat16):
    gain = shard_levels(own_key, extent, cuts, -0.22, 0.18) if cuts else 1.0
    array = jax.random.normal(own_key, extent, jnp.float32) * width * gain
    return jnp.minimum(jnp.maximum(array, -reach), reach).astype(kind)


def setup_inputs(seed: int = 0) -> dict:
    seeds = jax.random.split(jax.random.key(seed), 11)
    features = scatter_about(seeds[0], (LAT_ALL, LON_ALL, CHANNELS), 1.0, 6.0, ((0, 16), (1, 32)))
    cotangent = scatter_about(seeds[1], (LAT_ALL, LON_ALL, CHANNELS), 1.0, 6.0, ((0, 16), (1, 32)))
    first_gain = jnp.clip(1.0 + 0.15 * jax.random.normal(seeds[2], (CHANNELS,), jnp.float32), 0.25, 1.75)
    window_qkv = scatter_about(seeds[3], (CHANNELS, 3 * CHANNELS), CHANNELS ** -0.5, 0.4375)
    window_proj = scatter_about(seeds[4], (CHANNELS, CHANNELS), CHANNELS ** -0.5, 0.4375)
    window_table = draw_window_table(jax.random.fold_in(seeds[10], 71), 0)
    second_gain = jnp.clip(1.0 + 0.15 * jax.random.normal(seeds[6], (CHANNELS,), jnp.float32), 0.25, 1.75)
    cross_qkv = scatter_about(seeds[7], (CHANNELS, 3 * CHANNELS), CHANNELS ** -0.5, 0.4375)
    cross_proj = scatter_about(seeds[8], (CHANNELS, CHANNELS), CHANNELS ** -0.5, 0.4375)
    cross_table = draw_cross_table(jax.random.fold_in(seeds[10], 71), 0)
    return {"features": features, "cotangent": cotangent, "first_gain": first_gain, "window_qkv": window_qkv, "window_proj": window_proj, "window_table": window_table, "second_gain": second_gain, "cross_qkv": cross_qkv, "cross_proj": cross_proj, "cross_table": cross_table}


EPSILON = 1e-05
NEGATIVE = -1e+30

def layer_norm(values, norm_gain):
    centre = lax.optimization_barrier(jnp.mean(values, axis=-1, keepdims=True))
    offset = values - centre
    spread = lax.optimization_barrier(jnp.mean(offset * offset, axis=-1, keepdims=True))
    return offset * lax.rsqrt(spread + EPSILON) * norm_gain

def to_windows(values):
    row_total, col_total, chan_total = values.shape
    blocks = values.reshape(row_total // WINDOW, WINDOW, col_total // WINDOW, WINDOW, chan_total)
    return blocks.transpose(0, 2, 1, 3, 4).reshape(row_total // WINDOW, col_total // WINDOW, WINDOW * WINDOW, chan_total)

def from_windows(blocks):
    row_blocks, col_blocks, cell_count, chan_total = blocks.shape
    shaped = blocks.reshape(row_blocks, col_blocks, WINDOW, WINDOW, chan_total)
    return shaped.transpose(0, 2, 1, 3, 4).reshape(row_blocks * WINDOW, col_blocks * WINDOW, chan_total)

def wide_windows(values, row_blocks, col_blocks):
    extra_rows = WINDOW - 2 * KEY_RIM
    chan_total = values.shape[-1]
    padded = jnp.pad(values, ((0, extra_rows), (0, extra_rows), (0, 0)))
    col_total = padded.shape[1]
    upper_part = padded[:WINDOW * row_blocks].reshape(row_blocks, WINDOW, col_total, chan_total)
    lower_part = padded[WINDOW:].reshape(row_blocks, WINDOW, col_total, chan_total)[:, :2 * KEY_RIM]
    tall_part = jnp.concatenate([upper_part, lower_part], axis=1)
    left_part = tall_part[:, :, :WINDOW * col_blocks].reshape(row_blocks, KEY_WINDOW, col_blocks, WINDOW, chan_total)
    right_part = tall_part[:, :, WINDOW:].reshape(row_blocks, KEY_WINDOW, col_blocks, WINDOW, chan_total)[:, :, :, :2 * KEY_RIM]
    square_part = jnp.concatenate([left_part, right_part], axis=3)
    return square_part.transpose(0, 2, 1, 3, 4).reshape(row_blocks, col_blocks, KEY_WINDOW * KEY_WINDOW, chan_total)

def attend(queries, key_cells, values, position_bias, visible):
    win_count, query_len, chan_total = queries.shape
    key_len = key_cells.shape[1]
    head_size = chan_total // NUM_HEADS
    query_heads = queries.reshape(win_count, query_len, NUM_HEADS, head_size).astype(jnp.float32)
    key_heads = key_cells.reshape(win_count, key_len, NUM_HEADS, head_size).astype(jnp.float32)
    value_heads = values.reshape(win_count, key_len, NUM_HEADS, head_size).astype(jnp.float32)
    scores = jnp.einsum('wnhd,wmhd->whnm', query_heads, key_heads) * head_size ** (-0.5) + position_bias[None]
    if visible is not None:
        scores = jnp.where(visible[None, None], scores, NEGATIVE)
    row_peak = lax.stop_gradient(lax.optimization_barrier(jnp.max(scores, axis=-1, keepdims=True)))
    raised = jnp.exp(scores - row_peak)
    attn_probs = (raised / lax.optimization_barrier(jnp.sum(raised, axis=-1, keepdims=True))).astype(jnp.bfloat16)
    head_out = jnp.einsum('whnm,wmhd->wnhd', attn_probs.astype(jnp.float32), value_heads)
    return head_out.reshape(win_count, query_len, chan_total).astype(jnp.bfloat16)

def window_index():
    cells = jnp.arange(WINDOW * WINDOW)
    rows_of = cells // WINDOW
    cols_of = cells % WINDOW
    return ((rows_of[:, None] - rows_of[None, :] + WINDOW - 1) * WINDOW_SPAN + cols_of[:, None] - cols_of[None, :] + WINDOW - 1).astype(jnp.int32)

def cross_index():
    query_pos = jnp.arange(WINDOW * WINDOW)
    key_pos = jnp.arange(KEY_WINDOW * KEY_WINDOW)
    row_part = key_pos[None, :] // KEY_WINDOW - query_pos[:, None] // WINDOW + WINDOW - 1
    col_part = key_pos[None, :] % KEY_WINDOW - query_pos[:, None] % WINDOW + WINDOW - 1
    return (row_part * CROSS_SPAN + col_part).astype(jnp.int32)

def reference(features, cotangent, first_gain, window_qkv, window_proj, window_table, second_gain, cross_qkv, cross_proj, cross_table):
    band_rows, band_cols, chan_total = features.shape

    def block_out(features_f32, window_bias_table, cross_bias_table):
        first_norm = layer_norm(features_f32, first_gain).astype(jnp.bfloat16)
        window_act = jnp.dot(first_norm, window_qkv, preferred_element_type=jnp.float32).astype(jnp.bfloat16)
        rolled = jnp.roll(window_act, (-WIN_SHIFT, -WIN_SHIFT), axis=(0, 1))
        blocks = to_windows(rolled)
        window_bias = window_bias_table[:, window_index()]
        row_ids = jnp.arange(band_rows) + WIN_SHIFT
        early_rows = row_ids % band_rows < WIN_SHIFT
        cell_early = jnp.repeat(early_rows.reshape(-1, WINDOW), WINDOW, axis=1)

        def window_row(pieces):
            row_blocks, row_early = pieces
            visible = row_early[:, None] == row_early[None, :]
            return attend(row_blocks[..., :chan_total], row_blocks[..., chan_total:2 * chan_total], row_blocks[..., 2 * chan_total:], window_bias, visible)
        mixed_out = from_windows(lax.map(jax.checkpoint(window_row), (blocks, cell_early)))
        mixed_out = jnp.roll(mixed_out, (WIN_SHIFT, WIN_SHIFT), axis=(0, 1))
        middle = features_f32 + jnp.dot(mixed_out, window_proj, preferred_element_type=jnp.float32)
        second_norm = layer_norm(middle, second_gain).astype(jnp.bfloat16)
        cross_act = jnp.dot(second_norm, cross_qkv, preferred_element_type=jnp.float32).astype(jnp.bfloat16)
        queries = cross_act[..., :chan_total]
        key_vals = cross_act[..., chan_total:].astype(jnp.float32)
        key_vals = jnp.concatenate([key_vals[:, band_cols - KEY_RIM:], key_vals, key_vals[:, :KEY_RIM]], axis=1)
        key_vals = jnp.pad(key_vals, ((KEY_RIM, KEY_RIM), (0, 0), (0, 0)))
        key_blocks = wide_windows(key_vals, band_rows // WINDOW, band_cols // WINDOW).astype(jnp.bfloat16)
        query_blocks = to_windows(queries)
        cross_bias = cross_bias_table[:, cross_index()]

        def cross_row(pieces):
            row_queries, row_keys = pieces
            return attend(row_queries, row_keys[..., :chan_total], row_keys[..., chan_total:], cross_bias, None)
        crossed = from_windows(lax.map(jax.checkpoint(cross_row), (query_blocks, key_blocks)))
        return middle + jnp.dot(crossed, cross_proj, preferred_element_type=jnp.float32)
    block_value, pullback = jax.vjp(block_out, features.astype(jnp.float32), window_table, cross_table)
    grad_features, grad_window_table, grad_cross_table = pullback(cotangent.astype(jnp.float32))
    return (grad_features, grad_window_table, grad_cross_table)
```

```python
import functools

import jax
import jax.numpy as jnp
from jax import lax
from jax.experimental import pallas as pl
from jax.experimental.pallas import tpu as pltpu
from jax.sharding import PartitionSpec as P

CHANNELS = 180
HEADS = 6
HEAD_SIZE = 30
HEAD_PAD = 32
WIDE = 256
CELLS = 256
KEYS = 576
KEY_SIDE = 24
SPAN = 31
CROSS = 39
EPSILON = 1e-05
NEGATIVE = -1e30
LOG2E = 1.4426950408889634
SCALE = HEAD_SIZE**-0.5
TILES_W = 8
TILES_C = 12
LANES_W = 1024
LANES_C = 1280
USED_W = 640
USED_C = 896
MESH = pl.DeviceIdType.MESH
F32 = jnp.float32
BF16 = jnp.bfloat16


def iota(shape, dim):
    return lax.broadcasted_iota(jnp.int32, shape, dim)


def dot(a, b):
    return jnp.dot(a, b, preferred_element_type=F32)


def dot_nt(a, b):
    return lax.dot_general(a, b, (((1,), (1,)), ((), ())), preferred_element_type=F32)


def one_hot(mask):
    return jnp.where(mask, 1.0, 0.0).astype(BF16)


def roll(x, shift):
    size = x.shape[-1]
    return pltpu.roll(x, shift % size, x.ndim - 1)


def norm_parts(values):
    centre = jnp.mean(values, axis=-1, keepdims=True)
    offset = values - centre
    spread = jnp.mean(offset * offset, axis=-1, keepdims=True)
    inverse = lax.rsqrt(spread + EPSILON)
    return offset * inverse, inverse


def norm_back(unit, inverse, gain, grads):
    scaled = grads * gain
    first = jnp.mean(scaled, axis=-1, keepdims=True)
    second = jnp.mean(scaled * unit, axis=-1, keepdims=True)
    return inverse * (scaled - first - unit * second)


def slot(a, b):
    return (a // 2 * 2 + b // 2) * 4 + a % 2 * 2 + b % 2


OWN = [(sy, sx, 2 * sy + sx, (1 - sy) * 2 + (1 - sx)) for sy in (0, 1) for sx in (0, 1)]


def spread_rows(base, stride, ways):
    rows = iota(base.shape, 0)
    for bit in (1, 2, 4):
        base = jnp.where((rows & bit) != 0, roll(base, stride * bit), base)
    upper = (iota(base.shape, 1) & 16) != 0
    base = jnp.where(upper, roll(base, -240), base)
    return [base if r == 0 else roll(base, -32 * r) for r in range(ways)]


def gather_rows(parts, stride):
    total = parts[0]
    for r in range(1, len(parts)):
        total = total + roll(parts[r], 32 * r)
    upper = (iota(total.shape, 1) & 16) != 0
    total = jnp.where(upper, 0.0, total) + roll(jnp.where(upper, total, 0.0), 240)
    rows = iota(total.shape, 0)
    for bit in (1, 2, 4):
        total = jnp.where((rows & bit) != 0, roll(total, -stride * bit), total)
    return jnp.sum(total.reshape(HEADS, 8, total.shape[1]), axis=1)


def kernel(
    n_lat,
    n_lon,
    feat_in,
    cot_in_hbm,
    gain1_in,
    qkv1_in,
    proj1_in,
    tab1_in,
    gain2_in,
    qkv2_in,
    proj2_in,
    tab2_in,
    out_ref,
    out1_ref,
    out2_ref,
    feat_ref,
    cot_ref,
    gain1_ref,
    qkv1_ref,
    proj1_ref,
    tab1_ref,
    gain2_ref,
    qkv2_ref,
    proj2_ref,
    tab2_ref,
    load_sem,
    region,
    flat1,
    flat2,
    wt1,
    wt2,
    pp1,
    pp2,
    turn,
    z1,
    z2,
    acc1,
    acc2,
    feats,
    middles,
    units,
    inverses,
    kk,
    vt,
    vv,
    kt,
    qm,
    dom,
    qmt,
    dmt,
    ot,
    p1,
    p2,
    ds1,
    ds2,
    k2,
    v2,
    k2t,
    lin,
    mid_out,
    mid_in,
    back_out,
    back_in,
    dense1,
    dense2,
    tiles1,
    tiles2,
    rs1,
    rs2,
    ag1,
    ag2,
    fin1,
    fin2,
    halo_send,
    halo_recv,
    mid_send,
    mid_recv,
    back_send,
    back_recv,
    sum_send,
    sum_recv,
):
    lat = lax.axis_index("lat")
    lon = lax.axis_index("lon")

    def wrapped(value, count):
        value = jnp.where(value >= count, value - count, value)
        return jnp.where(value < 0, value + count, value)

    def at(dy, dx):
        return (wrapped(lon + dx, n_lon), wrapped(lat + dy, n_lat))

    loads = [
        pltpu.make_async_copy(src, dst, load_sem.at[i])
        for i, (src, dst) in enumerate(
            (
                (feat_in, feat_ref),
                (qkv1_in, qkv1_ref),
                (proj1_in, proj1_ref),
                (gain1_in, gain1_ref),
                (tab1_in, tab1_ref),
                (tab2_in, tab2_ref),
                (qkv2_in, qkv2_ref),
                (gain2_in, gain2_ref),
                (proj2_in, proj2_ref),
                (cot_in_hbm, cot_ref),
            )
        )
    ]
    for load in loads:
        load.start()

    barrier = pltpu.get_barrier_semaphore()

    def greet(dy, dx):
        pl.semaphore_signal(barrier, inc=1, device_id=at(dy, dx), device_id_type=MESH)

    for dy in (-1, 1):
        for dx in (-1, 1):
            greet(dy, dx)
    for j in range(1, n_lat):
        greet(j, 0)
    for j in range(1, n_lon):
        greet(0, j)

    loads[0].wait()
    own = feat_ref[...].astype(F32)
    for sy, sx, w, s in OWN:
        quarter = own[8 * sy : 8 * sy + 8, 8 * sx : 8 * sx + 8, :].reshape(64, CHANNELS)
        region[w * 4 + s] = quarter.astype(BF16)

    for load in loads[1:5]:
        load.wait()

    row = iota((3 * WIDE, 1), 0)
    lane = row & 255
    real = (lane < 192) & ((lane & 31) < HEAD_SIZE)
    source = jnp.where(real, CHANNELS * (row >> 8) + lane - 2 * (lane >> 5), -1)
    pick = one_hot(iota((3 * WIDE, 3 * CHANNELS), 1) == source)
    wt1[...] = dot_nt(pick, qkv1_ref[...]).astype(BF16)
    pick_proj = pick[:WIDE, :CHANNELS]
    pp1[...] = dot(pick_proj, proj1_ref[...]).astype(BF16)

    pl.semaphore_wait(barrier, n_lat - 1 + n_lon - 1 + 4)

    halo = []
    for a in (1, 2):
        for b in (1, 2):
            for dy in (0, -1 if a == 1 else 1):
                for dx in (0, -1 if b == 1 else 1):
                    if dy == 0 and dx == 0:
                        continue
                    halo.append(
                        pltpu.make_async_remote_copy(
                            src_ref=region.at[slot(a, b)],
                            dst_ref=region.at[slot(a - 2 * dy, b - 2 * dx)],
                            send_sem=halo_send,
                            recv_sem=halo_recv,
                            device_id=at(dy, dx),
                            device_id_type=MESH,
                        )
                    )
    for copy in halo:
        copy.start()

    for load in loads[5:]:
        load.wait()
    wt2[...] = dot_nt(pick, qkv2_ref[...]).astype(BF16)
    pp2[...] = dot(pick_proj, proj2_ref[...]).astype(BF16)

    def turned(c):
        r = 255 - c
        return ((r >> 3) & 7) * 32 + ((r >> 7) & 1) * 16 + ((r >> 6) & 1) * 8 + (r & 7)

    turn[0] = one_hot(iota((CELLS, CELLS), 0) == turned(iota((1, CELLS), 1)))
    turn[1] = one_hot(iota((CELLS, CELLS), 1) == turned(iota((CELLS, 1), 0)))

    flat1[...] = jnp.zeros(flat1.shape, F32)
    flat2[...] = jnp.zeros(flat2.shape, F32)
    for dy in range(SPAN):
        flat1[:, dy * 32 : dy * 32 + SPAN] = tab1_ref[:, dy * SPAN : (dy + 1) * SPAN]
    for dy in range(CROSS):
        for s in range(3):
            start = dy * CROSS + 8 * s
            flat2[s, :, dy * 32 : dy * 32 + 23] = tab2_ref[:, start : start + 23]
    for s in range(2):
        base = jnp.broadcast_to(flat1[...][:, None, :] * LOG2E, (HEADS, 8, LANES_W))
        base = roll(base.reshape(HEADS * 8, LANES_W), 8 * s - 15)
        for r, part in enumerate(spread_rows(base, 1, 4)):
            z1[s, r] = part[:, :USED_W].reshape(HEADS, 8, USED_W)
    for s in range(3):
        base = jnp.broadcast_to(flat2[s][:, None, :] * LOG2E, (HEADS, 8, LANES_C))
        base = base.reshape(HEADS * 8, LANES_C)
        for r, part in enumerate(spread_rows(base, -1, 4)):
            z2[s, r] = part[:, :USED_C].reshape(HEADS, 8, USED_C)
    query_half = (iota((1, CELLS), 1) >> 4) & 1

    def window_bias(h, masks):
        pieces = []
        for y8 in range(8):
            for sy in range(2):
                t, r = divmod(15 - (8 * sy + y8), 4)
                for sx in range(2):
                    pieces.append(z1[sx, r, h, :, 128 * t : 128 * t + CELLS] + masks[sy])
        return jnp.concatenate(pieces, axis=0)

    def cross_bias(h):
        pieces = []
        for ky in range(KEY_SIDE):
            t, r = divmod(ky, 4)
            for s in range(3):
                pieces.append(z2[s, r, h, :, 128 * t : 128 * t + CELLS])
        return jnp.concatenate(pieces, axis=0)

    def collect(acc, h, s, count, group_of, slopes):
        for r in range(4):
            for t in range(count // 4 + 1):
                parts = []
                if t < count // 4:
                    group = group_of(4 * t + r)
                    parts.append(slopes[group : group + 8, 0:128])
                if t > 0:
                    group = group_of(4 * t - 4 + r)
                    parts.append(slopes[group : group + 8, 128:256])
                acc[s, r, h, :, 128 * t : 128 * t + 128] = sum(parts[1:], parts[0])

    def head_rows(values, h):
        before, rows = h % 4 * HEAD_PAD, values[h * HEAD_PAD : (h + 1) * HEAD_PAD, :]
        pieces = [rows]
        if before:
            pieces = [jnp.zeros((before, CELLS), values.dtype)] + pieces
        if before + HEAD_PAD < 128:
            pieces.append(jnp.zeros((128 - HEAD_PAD - before, CELLS), values.dtype))
        return jnp.concatenate(pieces, axis=0) if len(pieces) > 1 else rows

    every = region.at[pl.ds(0, 12)]
    pltpu.make_async_copy(every, every, halo_recv).wait()

    gain1 = gain1_ref[...]
    gain2 = gain2_ref[...]
    wide_lane = iota((CELLS, WIDE), 1) >> 5

    def window(w, _):
        parts = [
            region[w * 4 + s].astype(F32).reshape(8, 1, 8, CHANNELS) for s in range(4)
        ]
        values = jnp.concatenate(parts, axis=1).reshape(CELLS, CHANNELS)
        unit, _ = norm_parts(values)
        normed = (unit * gain1).astype(BF16)
        feats[...] = values
        queries = dot_nt(wt1[0:WIDE, :], normed).astype(BF16)
        kk[...] = dot_nt(normed, wt1[WIDE : 2 * WIDE, :]).astype(BF16)
        vt[...] = dot_nt(wt1[2 * WIDE :, :], normed).astype(BF16)
        edge = lat == jnp.where(w < 2, 0, n_lat - 1)
        floor = jnp.where(edge, NEGATIVE, 0.0)
        masks = [jnp.where(query_half != sy, floor, 0.0) for sy in range(2)]
        for h in range(HEADS):
            half = h // 4 * 128
            products = dot(kk[:, half : half + 128], head_rows(queries, h))
            scores = products * (SCALE * LOG2E) + window_bias(h, masks)
            peak = jnp.max(scores, axis=0, keepdims=True)
            raised = jnp.exp2(scores - peak)
            inverse = 1.0 / jnp.sum(raised, axis=0, keepdims=True)
            probs = (raised * inverse).astype(BF16)
            p1[:, h * CELLS : (h + 1) * CELLS] = probs
            ot[h * HEAD_PAD : (h + 1) * HEAD_PAD, :] = dot(
                vt[h * HEAD_PAD : (h + 1) * HEAD_PAD, :], probs
            )
        heads_out = jnp.transpose(ot[...]).astype(BF16)
        middle = values + dot(heads_out, pp1[...])
        middles[w] = middle.reshape(8, 2, 2, 8, CHANNELS)
        return 0

    ot[...] = jnp.zeros(ot.shape, F32)
    lax.fori_loop(0, 4, window, 0)

    y_runs = ((0, 0, 4, 8, 0), (0, 1, 0, 8, 4), (1, 0, 0, 8, 12), (1, 1, 0, 4, 20))
    for wy, sy, first, last, place in y_runs:
        for wx in range(2):
            for sx in range(2):
                start = (2 * wx + sx) * 8
                lin[place : place + last - first, start : start + 8, :] = middles[
                    2 * wy + wx, first:last, sy, sx
                ]
    unit2, inverse2 = norm_parts(lin[...].reshape(KEY_SIDE * 32, CHANNELS))
    units[...] = unit2
    inverses[...] = inverse2
    lin[...] = (unit2 * gain2).astype(BF16).astype(F32).reshape(KEY_SIDE, 32, CHANNELS)
    inside_low = jnp.where(lat > 0, 1.0, 0.0)
    inside_high = jnp.where(lat < n_lat - 1, 1.0, 0.0)
    lin[0:4] = lin[0:4] * inside_low
    lin[20:24] = lin[20:24] * inside_high
    keys_in = lin[:, 4:28, :].reshape(KEYS, CHANNELS).astype(BF16)
    k2[...] = dot_nt(keys_in, wt2[WIDE : 2 * WIDE, :]).astype(BF16)
    v2[...] = dot_nt(keys_in, wt2[2 * WIDE :, :]).astype(BF16)
    k2t[...] = dot_nt(wt2[WIDE : 2 * WIDE, :], keys_in).astype(BF16)

    def own_part(sy, sx):
        return slice(4 + 8 * sy, 12 + 8 * sy), slice(8 + 8 * sx, 16 + 8 * sx)

    own_second = jnp.concatenate(
        [lin[(*own_part(sy, sx), slice(None))].reshape(64, CHANNELS) for sy, sx, w, s in OWN],
        axis=0,
    )
    queries_in = dot(turn[0], own_second.astype(BF16)).astype(BF16)
    cot = cot_ref[...].astype(F32)
    cot_own = [
        cot[8 * sy : 8 * sy + 8, 8 * sx : 8 * sx + 8, :].reshape(64, CHANNELS)
        for sy, sx, w, s in OWN
    ]
    cot_in = dot(turn[0], jnp.concatenate(cot_own, axis=0).astype(BF16)).astype(BF16)
    queries_t = dot_nt(wt2[0:WIDE, :], queries_in).astype(BF16)
    grads_t = dot_nt(pp2[...], cot_in).astype(BF16)
    queries = dot_nt(queries_in, wt2[0:WIDE, :])
    grads = dot_nt(cot_in, pp2[...])
    for h in range(HEADS):
        qmt[h] = head_rows(queries_t, h)
        dmt[h] = head_rows(grads_t, h)
        qm[h * CELLS : (h + 1) * CELLS, :] = jnp.where(wide_lane == h, queries, 0.0).astype(BF16)
        dom[h * CELLS : (h + 1) * CELLS, :] = jnp.where(wide_lane == h, grads, 0.0).astype(BF16)

    def cross_pair(pair, _):
        half = pl.ds(pl.multiple_of(pair // 2 * 128, 128), 128)
        for i in range(2):
            h = 2 * pair + i
            scores = dot(k2[:, half], qmt[h]) * (SCALE * LOG2E) + cross_bias(h)
            peak = jnp.max(scores, axis=0, keepdims=True)
            raised = jnp.exp2(scores - peak)
            inverse = 1.0 / jnp.sum(raised, axis=0, keepdims=True)
            probs = raised * inverse
            columns = pl.ds(pl.multiple_of(h * CELLS, CELLS), CELLS)
            p2[:, columns] = probs.astype(BF16)
            weighted = probs * dot(v2[:, half], dmt[h])
            total = jnp.sum(weighted, axis=0, keepdims=True)
            slopes = weighted - probs * total
            for s in range(3):
                collect(acc2, h, s, KEY_SIDE, lambda m: (m * 3 + s) * 8, slopes)
            slopes_b = slopes.astype(BF16)
            ds2[:, columns] = slopes_b
            rows = pl.ds(pl.multiple_of(h * HEAD_PAD, HEAD_PAD), HEAD_PAD)
            ot[rows, :] = dot(k2t[rows, :], slopes_b)
        return 0

    lax.fori_loop(0, HEADS // 2, cross_pair, 0)
    grad_queries = (jnp.transpose(ot[...]) * SCALE).astype(BF16)
    grad_keys = (dot(ds2[...], qm[...]) * SCALE).astype(BF16)
    grad_values = dot(p2[...], dom[...]).astype(BF16)
    grad_second = dot(grad_keys, wt2[WIDE : 2 * WIDE, :]) + dot(grad_values, wt2[2 * WIDE :, :])
    grad_own = dot(turn[1], dot(grad_queries, wt2[0:WIDE, :]).astype(BF16))

    lin[...] = jnp.zeros(lin.shape, F32)
    lin[:, 4:28, :] = grad_second.reshape(KEY_SIDE, KEY_SIDE, CHANNELS)
    lin[0:4] = lin[0:4] * inside_low
    lin[20:24] = lin[20:24] * inside_high
    for i, (sy, sx, w, s) in enumerate(OWN):
        place = (*own_part(sy, sx), slice(None))
        lin[place] = lin[place] + grad_own[64 * i : 64 * i + 64, :].reshape(8, 8, CHANNELS)
    grad = norm_back(
        units[...], inverses[...], gain2, lin[...].reshape(KEY_SIDE * 32, CHANNELS)
    )
    lin[...] = grad.reshape(KEY_SIDE, 32, CHANNELS)
    for i, (sy, sx, w, s) in enumerate(OWN):
        place = (*own_part(sy, sx), slice(None))
        lin[place] = lin[place] + cot_own[i].reshape(8, 8, CHANNELS)
    for w in range(3):
        rows, cols = 12 * (w // 2), 16 * (w % 2)
        piece = lin[rows : rows + 12, cols : cols + 16, :]
        mid_out[w] = piece.reshape(192, CHANNELS).astype(BF16)
        pltpu.make_async_remote_copy(
            src_ref=mid_out.at[w],
            dst_ref=mid_in.at[w],
            send_sem=mid_send,
            recv_sem=mid_recv,
            device_id=at(w // 2 - 1, w % 2 - 1),
            device_id_type=MESH,
        ).start()

    def sum_scatter(kind, tiles, buffer):
        chunks, depth = buffer_plan(tiles, n_lat)
        for c in range(chunks):

            @pl.when(lat != c)
            def _():
                pltpu.make_async_remote_copy(
                    src_ref=tiles.at[pl.ds(c * depth, depth)],
                    dst_ref=buffer.at[wrapped(lat - c, n_lat) - 1],
                    send_sem=sum_send.at[kind],
                    recv_sem=sum_recv.at[kind],
                    device_id=(lon, c),
                    device_id_type=MESH,
                ).start()

    def drain(sem, ref):
        pltpu.make_async_copy(ref, ref, sem).wait()

    def sum_spread(kind, tiles, buffer, rows):
        chunks, depth = buffer_plan(tiles, n_lat)

        @pl.when(lat < chunks)
        def _():
            drain(sum_recv.at[kind], buffer)
            total = tiles[pl.ds(lat * depth, depth)]
            for i in range(n_lat - 1):
                total = total + buffer[i]
            rows[lon] = total

            for j in range(1, n_lon):
                pltpu.make_async_remote_copy(
                    src_ref=rows.at[lon],
                    dst_ref=rows.at[lon],
                    send_sem=sum_send.at[kind + 1],
                    recv_sem=sum_recv.at[kind + 1],
                    device_id=at(0, j),
                    device_id_type=MESH,
                ).start()

    def sum_gather(kind, tiles, rows, result):
        chunks, depth = buffer_plan(tiles, n_lat)

        @pl.when(lat < chunks)
        def _():
            drain(sum_recv.at[kind + 1], rows.at[pl.ds(0, n_lon - 1)])
            total = rows[0]
            for i in range(1, n_lon):
                total = total + rows[i]
            result[lat] = total

            for j in range(1, n_lat):
                pltpu.make_async_remote_copy(
                    src_ref=result.at[lat],
                    dst_ref=result.at[lat],
                    send_sem=sum_send.at[kind + 2],
                    recv_sem=sum_recv.at[kind + 2],
                    device_id=at(j, 0),
                    device_id_type=MESH,
                ).start()

    def sum_end(kind, tiles, buffer, rows, result):
        chunks, depth = buffer_plan(tiles, n_lat)

        @pl.when(lat < chunks)
        def _():
            if chunks > 1:
                drain(sum_recv.at[kind + 2], result.at[pl.ds(0, chunks - 1)])
                drain(sum_send.at[kind], result.at[pl.ds(0, chunks - 1)])
            drain(sum_send.at[kind + 1], rows.at[pl.ds(0, n_lon - 1)])
            drain(sum_send.at[kind + 2], buffer)

        @pl.when(lat >= chunks)
        def _():
            drain(sum_recv.at[kind + 2], result)
            drain(sum_send.at[kind], result)

    def joined(result, count):
        chunks, depth = result.shape[0], result.shape[1]
        whole = jnp.concatenate(
            [result[c, d] for c in range(chunks) for d in range(depth)], axis=1
        )
        return whole[:HEADS, :count]

    for s in range(3):
        parts = [
            jnp.concatenate(
                [
                    acc2[s, r].reshape(HEADS * 8, USED_C),
                    jnp.zeros((HEADS * 8, LANES_C - USED_C), F32),
                ],
                axis=1,
            )
            for r in range(4)
        ]
        flat2[s] = gather_rows(parts, -1)
    dense2[...] = jnp.zeros(dense2.shape, F32)
    for dy in range(CROSS):
        for s in range(3):
            start = dy * CROSS + 8 * s
            dense2[s, 0:HEADS, start : start + 23] = flat2[s, :, dy * 32 : dy * 32 + 23]
    for t in range(TILES_C):
        part = pl.ds(128 * t, 128)
        tiles2[t] = dense2[0, :, part] + dense2[1, :, part] + dense2[2, :, part]
    sum_scatter(0, tiles2, rs2)

    unit1, inverse1 = norm_parts(feats[...])
    normed1 = (unit1 * gain1).astype(BF16)
    vv[...] = dot_nt(normed1, wt1[2 * WIDE :, :]).astype(BF16)
    kt[...] = dot_nt(wt1[WIDE : 2 * WIDE, :], normed1).astype(BF16)
    queries = dot_nt(normed1, wt1[0:WIDE, :])
    for h in range(HEADS):
        qm[h * CELLS : (h + 1) * CELLS, :] = jnp.where(wide_lane == h, queries, 0.0).astype(BF16)

    drain(mid_recv, mid_in)
    total = lin[12:24, 16:32, :] + mid_in[2].astype(F32).reshape(12, 16, CHANNELS)
    below = (mid_in[0].astype(F32) + mid_in[1].astype(F32)).reshape(12, 16, CHANNELS)
    total = jnp.concatenate([total[0:4], total[4:12] + below[0:8], below[8:12]], axis=0)
    pair = [total[8 * sy : 8 * sy + 8].reshape(8, 1, 16, CHANNELS) for sy in range(2)]
    grad_middle = jnp.concatenate(pair, axis=1).reshape(CELLS, CHANNELS)
    sum_spread(0, tiles2, rs2, ag2)

    grad_in = grad_middle.astype(BF16)
    grads_t = dot_nt(pp1[...], grad_in).astype(BF16)
    grads = dot_nt(grad_in, pp1[...])
    for h in range(HEADS):
        dom[h * CELLS : (h + 1) * CELLS, :] = jnp.where(wide_lane == h, grads, 0.0).astype(BF16)
    for h in range(HEADS):
        half = h // 4 * 128
        probs = p1[:, h * CELLS : (h + 1) * CELLS].astype(F32)
        weighted = probs * dot(vv[:, half : half + 128], head_rows(grads_t, h))
        total = jnp.sum(weighted, axis=0, keepdims=True)
        slopes = weighted - probs * total
        for sx in range(2):

            def group_of(m):
                ky = 15 - m
                return (ky % 8 * 4 + ky // 8 * 2 + sx) * 8

            collect(acc1, h, sx, 16, group_of, slopes)
        slopes_b = slopes.astype(BF16)
        ds1[:, h * CELLS : (h + 1) * CELLS] = slopes_b
        ot[h * HEAD_PAD : (h + 1) * HEAD_PAD, :] = dot(
            kt[h * HEAD_PAD : (h + 1) * HEAD_PAD, :], slopes_b
        )
    sum_gather(0, tiles2, ag2, fin2)

    flat = None
    for s in range(2):
        parts = [
            jnp.concatenate(
                [
                    acc1[s, r].reshape(HEADS * 8, USED_W),
                    jnp.zeros((HEADS * 8, LANES_W - USED_W), F32),
                ],
                axis=1,
            )
            for r in range(4)
        ]
        piece = roll(gather_rows(parts, 1), 15 - 8 * s)
        flat = piece if flat is None else flat + piece
    flat1[...] = flat
    dense1[...] = jnp.zeros(dense1.shape, F32)
    for dy in range(SPAN):
        dense1[0:HEADS, dy * SPAN : (dy + 1) * SPAN] = flat1[:, dy * 32 : dy * 32 + SPAN]
    for t in range(TILES_W):
        tiles1[t] = dense1[:, 128 * t : 128 * t + 128]
    sum_scatter(3, tiles1, rs1)

    grad_queries = (jnp.transpose(ot[...]) * SCALE).astype(BF16)
    grad_keys = (dot(ds1[...], qm[...]) * SCALE).astype(BF16)
    grad_values = dot(p1[...], dom[...])
    grad_first = (
        dot(grad_queries, wt1[0:WIDE, :])
        + dot(grad_keys, wt1[WIDE : 2 * WIDE, :])
        + dot(grad_values.astype(BF16), wt1[2 * WIDE :, :])
    )
    grad_feats = grad_middle + norm_back(unit1, inverse1, gain1, grad_first)
    quarters = grad_feats.reshape(8, 2, 2, 8, CHANNELS)
    backs = []
    for s in (1, 2, 3):
        back_out[s - 1] = quarters[:, s // 2, s % 2].reshape(64, CHANNELS).astype(BF16)
        copy = pltpu.make_async_remote_copy(
            src_ref=back_out.at[s - 1],
            dst_ref=back_in.at[s - 1],
            send_sem=back_send,
            recv_sem=back_recv,
            device_id=at(s // 2, s % 2),
            device_id_type=MESH,
        )
        copy.start()
        backs.append(copy)
    out_ref[8:16, 8:16, :] = quarters[:, 0, 0]
    sum_spread(3, tiles1, rs1, ag1)
    drain(back_recv, back_in)
    out_ref[8:16, 0:8, :] = back_in[0].astype(F32).reshape(8, 8, CHANNELS)
    out_ref[0:8, 8:16, :] = back_in[1].astype(F32).reshape(8, 8, CHANNELS)
    out_ref[0:8, 0:8, :] = back_in[2].astype(F32).reshape(8, 8, CHANNELS)
    sum_gather(3, tiles1, ag1, fin1)
    sum_end(0, tiles2, rs2, ag2, fin2)
    out2_ref[...] = joined(fin2, CROSS * CROSS)
    sum_end(3, tiles1, rs1, ag1, fin1)
    pltpu.make_async_copy(every, every, halo_send).wait()
    drain(mid_send, mid_out)
    drain(back_send, back_out)
    out1_ref[...] = joined(fin1, SPAN * SPAN)


def buffer_plan(tiles, n_lat):
    count = tiles.shape[0]
    chunks = min(n_lat, count)
    return chunks, count // chunks


def body(n_lat, n_lon, *operands):
    vmem = pltpu.VMEM

    def sums(count):
        chunks = min(n_lat, count)
        depth = count // chunks
        return (
            vmem((count, 8, 128), F32),
            vmem((n_lat - 1, depth, 8, 128), F32),
            vmem((n_lon, depth, 8, 128), F32),
            vmem((chunks, depth, 8, 128), F32),
        )

    tiles1, rs1, ag1, fin1 = sums(TILES_W)
    tiles2, rs2, ag2, fin2 = sums(TILES_C)
    scratch = [
        vmem((16, 16, CHANNELS), BF16),
        vmem((16, 16, CHANNELS), BF16),
        vmem((1, CHANNELS), F32),
        vmem((CHANNELS, 3 * CHANNELS), BF16),
        vmem((CHANNELS, CHANNELS), BF16),
        vmem((HEADS, SPAN * SPAN), F32),
        vmem((1, CHANNELS), F32),
        vmem((CHANNELS, 3 * CHANNELS), BF16),
        vmem((CHANNELS, CHANNELS), BF16),
        vmem((HEADS, CROSS * CROSS), F32),
        pltpu.SemaphoreType.DMA((10,)),
        vmem((16, 64, CHANNELS), BF16),
        vmem((HEADS, LANES_W), F32),
        vmem((3, HEADS, LANES_C), F32),
        vmem((3 * WIDE, CHANNELS), BF16),
        vmem((3 * WIDE, CHANNELS), BF16),
        vmem((WIDE, CHANNELS), BF16),
        vmem((WIDE, CHANNELS), BF16),
        vmem((2, CELLS, CELLS), BF16),
        vmem((2, 4, HEADS, 8, USED_W), F32),
        vmem((3, 4, HEADS, 8, USED_C), F32),
        vmem((2, 4, HEADS, 8, USED_W), F32),
        vmem((3, 4, HEADS, 8, USED_C), F32),
        vmem((CELLS, CHANNELS), F32),
        vmem((4, 8, 2, 2, 8, CHANNELS), F32),
        vmem((KEY_SIDE * 32, CHANNELS), F32),
        vmem((KEY_SIDE * 32, 1), F32),
        vmem((CELLS, WIDE), BF16),
        vmem((WIDE, CELLS), BF16),
        vmem((CELLS, WIDE), BF16),
        vmem((WIDE, CELLS), BF16),
        vmem((HEADS * CELLS, WIDE), BF16),
        vmem((HEADS * CELLS, WIDE), BF16),
        vmem((HEADS, 128, CELLS), BF16),
        vmem((HEADS, 128, CELLS), BF16),
        vmem((WIDE, CELLS), F32),
        vmem((CELLS, HEADS * CELLS), BF16),
        vmem((KEYS, HEADS * CELLS), BF16),
        vmem((CELLS, HEADS * CELLS), BF16),
        vmem((KEYS, HEADS * CELLS), BF16),
        vmem((KEYS, WIDE), BF16),
        vmem((KEYS, WIDE), BF16),
        vmem((WIDE, KEYS), BF16),
        vmem((KEY_SIDE, 32, CHANNELS), F32),
        vmem((3, 192, CHANNELS), BF16),
        vmem((3, 192, CHANNELS), BF16),
        vmem((3, 64, CHANNELS), BF16),
        vmem((3, 64, CHANNELS), BF16),
        vmem((8, 128 * TILES_W), F32),
        vmem((3, 8, 128 * TILES_C), F32),
        tiles1,
        tiles2,
        rs1,
        rs2,
        ag1,
        ag2,
        fin1,
        fin2,
        pltpu.SemaphoreType.DMA,
        pltpu.SemaphoreType.DMA,
        pltpu.SemaphoreType.DMA,
        pltpu.SemaphoreType.DMA,
        pltpu.SemaphoreType.DMA,
        pltpu.SemaphoreType.DMA,
        pltpu.SemaphoreType.DMA((6,)),
        pltpu.SemaphoreType.DMA((6,)),
    ]
    whole = pl.BlockSpec(memory_space=pltpu.VMEM)
    return pl.pallas_call(
        functools.partial(kernel, n_lat, n_lon),
        out_shape=(
            jax.ShapeDtypeStruct((16, 16, CHANNELS), F32),
            jax.ShapeDtypeStruct((HEADS, SPAN * SPAN), F32),
            jax.ShapeDtypeStruct((HEADS, CROSS * CROSS), F32),
        ),
        in_specs=[pl.BlockSpec(memory_space=pltpu.HBM)] * 10,
        out_specs=(whole, whole, whole),
        scratch_shapes=scratch,
        compiler_params=pltpu.CompilerParams(
            collective_id=0, has_side_effects=True, vmem_limit_bytes=63 * 1024 * 1024
        ),
    )(*operands)


def solution(mesh):
    def local(
        features,
        cotangent,
        first_gain,
        window_qkv,
        window_proj,
        window_table,
        second_gain,
        cross_qkv,
        cross_proj,
        cross_table,
    ):
        return body(
            mesh.shape["lat"],
            mesh.shape["lon"],
            features,
            cotangent,
            first_gain.reshape(1, CHANNELS),
            window_qkv,
            window_proj,
            window_table,
            second_gain.reshape(1, CHANNELS),
            cross_qkv,
            cross_proj,
            cross_table,
        )

    return jax.shard_map(
        local,
        mesh=mesh,
        in_specs=(
            P("lat", "lon", None),
            P("lat", "lon", None),
            P(),
            P(),
            P(),
            P(),
            P(),
            P(),
            P(),
            P(),
        ),
        out_specs=(P("lat", "lon", None), P(), P()),
        check_vma=False,
    )
```

```python
import functools

import jax
import jax.numpy as jnp
from jax import lax
from jax.experimental import pallas as pl
from jax.experimental.pallas import tpu as pltpu
from jax.sharding import PartitionSpec as P

CHANNELS = 180
HEADS = 6
HEAD_SIZE = 30
HEAD_PAD = 32
WIDE = 256
CELLS = 256
KEYS = 576
KEY_SIDE = 24
SPAN = 31
CROSS = 39
EPSILON = 1e-05
NEGATIVE = -1e30
LOG2E = 1.4426950408889634
SCALE = HEAD_SIZE**-0.5
TILES_W = 8
TILES_C = 12
LANES_W = 1024
LANES_C = 1280
USED_W = 640
USED_C = 896
MESH = pl.DeviceIdType.MESH
F32 = jnp.float32
BF16 = jnp.bfloat16


def iota(shape, dim):
    return lax.broadcasted_iota(jnp.int32, shape, dim)


def dot(a, b):
    return jnp.dot(a, b, preferred_element_type=F32)


def dot_nt(a, b):
    return lax.dot_general(a, b, (((1,), (1,)), ((), ())), preferred_element_type=F32)


def one_hot(mask):
    return jnp.where(mask, 1.0, 0.0).astype(BF16)


def roll(x, shift):
    size = x.shape[-1]
    return pltpu.roll(x, shift % size, x.ndim - 1)


def norm_parts(values):
    centre = jnp.mean(values, axis=-1, keepdims=True)
    offset = values - centre
    spread = jnp.mean(offset * offset, axis=-1, keepdims=True)
    inverse = lax.rsqrt(spread + EPSILON)
    return offset * inverse, inverse


def norm_back(unit, inverse, gain, grads):
    scaled = grads * gain
    first = jnp.mean(scaled, axis=-1, keepdims=True)
    second = jnp.mean(scaled * unit, axis=-1, keepdims=True)
    return inverse * (scaled - first - unit * second)


def slot(a, b):
    return (a // 2 * 2 + b // 2) * 4 + a % 2 * 2 + b % 2


OWN = [(sy, sx, 2 * sy + sx, (1 - sy) * 2 + (1 - sx)) for sy in (0, 1) for sx in (0, 1)]


def spread_rows(base, stride, ways):
    rows = iota(base.shape, 0)
    for bit in (1, 2, 4):
        base = jnp.where((rows & bit) != 0, roll(base, stride * bit), base)
    upper = (iota(base.shape, 1) & 16) != 0
    base = jnp.where(upper, roll(base, -240), base)
    return [base if r == 0 else roll(base, -32 * r) for r in range(ways)]


def gather_rows(parts, stride):
    total = parts[0]
    for r in range(1, len(parts)):
        total = total + roll(parts[r], 32 * r)
    upper = (iota(total.shape, 1) & 16) != 0
    total = jnp.where(upper, 0.0, total) + roll(jnp.where(upper, total, 0.0), 240)
    rows = iota(total.shape, 0)
    for bit in (1, 2, 4):
        total = jnp.where((rows & bit) != 0, roll(total, -stride * bit), total)
    return jnp.sum(total, axis=0, keepdims=True)


def kernel(
    n_lat,
    n_lon,
    feat_in,
    cot_in_hbm,
    gain1_in,
    qkv1_in,
    proj1_in,
    tab1_in,
    gain2_in,
    qkv2_in,
    proj2_in,
    tab2_in,
    out_ref,
    out1_ref,
    out2_ref,
    feat_ref,
    cot_ref,
    gain1_ref,
    qkv1_ref,
    proj1_ref,
    tab1_ref,
    gain2_ref,
    qkv2_ref,
    proj2_ref,
    tab2_ref,
    load_sem,
    region,
    flat1,
    flat2,
    wt1,
    wt2,
    pp1,
    pp2,
    turn,
    z1,
    z2,
    acc1,
    acc2,
    feats,
    middles,
    units,
    inverses,
    kk,
    vt,
    vv,
    kt,
    qm,
    dom,
    qmt,
    gt,
    ot,
    normed,
    inverse1,
    s1,
    s2,
    g2,
    grad_mid,
    grad_first,
    p1,
    p2,
    ds1,
    ds2,
    k2,
    v2,
    k2t,
    lin,
    mid_out,
    mid_in,
    back_out,
    back_in,
    dense1,
    dense2,
    tiles1,
    tiles2,
    rs1,
    rs2,
    ag1,
    ag2,
    far1,
    far2,
    fin1,
    fin2,
    halo_send,
    halo_recv,
    mid_send,
    mid_recv,
    back_send,
    back_recv,
    sum_send,
    sum_recv,
):
    lat = lax.axis_index("lat")
    lon = lax.axis_index("lon")

    def wrapped(value, count):
        value = jnp.where(value >= count, value - count, value)
        return jnp.where(value < 0, value + count, value)

    def at(dy, dx):
        return (wrapped(lon + dx, n_lon), wrapped(lat + dy, n_lat))

    loads = [
        pltpu.make_async_copy(src, dst, load_sem.at[i])
        for i, (src, dst) in enumerate(
            (
                (feat_in, feat_ref),
                (qkv1_in, qkv1_ref),
                (proj1_in, proj1_ref),
                (qkv2_in, qkv2_ref),
                (proj2_in, proj2_ref),
                (tab1_in, tab1_ref),
                (tab2_in, tab2_ref),
                (gain1_in, gain1_ref),
                (gain2_in, gain2_ref),
                (cot_in_hbm, cot_ref),
            )
        )
    ]
    for load in loads:
        load.start()

    barrier = pltpu.get_barrier_semaphore()

    def greet(dy, dx):
        pl.semaphore_signal(barrier, inc=1, device_id=at(dy, dx), device_id_type=MESH)

    for dy in (-1, 1):
        for dx in (-1, 1):
            greet(dy, dx)
    for j in range(1, n_lat):
        greet(j, 0)
    greet(0, 1)
    greet(0, -1)
    inner, outer = lon_plan(n_lon)
    spot = lax.rem(lon, inner)

    def inner_peer(j):
        return (lon - spot + wrapped(spot + j, inner), lat)

    def greet_at(device):
        pl.semaphore_signal(barrier, inc=1, device_id=device, device_id_type=MESH)

    for j in range(1, inner):
        greet_at(inner_peer(j))
    for j in range(1, outer):
        greet(0, j * inner)

    loads[0].wait()
    own = feat_ref[...].astype(F32)
    for sy, sx, w, s in OWN:
        quarter = own[8 * sy : 8 * sy + 8, 8 * sx : 8 * sx + 8, :].reshape(64, CHANNELS)
        region[w * 4 + s] = quarter.astype(BF16)

    for load in loads[1:7]:
        load.wait()

    def pad_weights(i, _):
        lane = iota((WIDE, 1), 0)
        real = (lane < 192) & ((lane & 31) < HEAD_SIZE)
        source = jnp.where(real, CHANNELS * i + lane - 2 * (lane >> 5), -1)
        pick = one_hot(iota((WIDE, 3 * CHANNELS), 1) == source)
        rows = pl.ds(pl.multiple_of(i * WIDE, WIDE), WIDE)
        wt1[rows, :] = dot_nt(pick, qkv1_ref[...]).astype(BF16)
        wt2[rows, :] = dot_nt(pick, qkv2_ref[...]).astype(BF16)

        @pl.when(i == 0)
        def _():
            pick_proj = pick[:, :CHANNELS]
            pp1[...] = dot(pick_proj, proj1_ref[...]).astype(BF16)
            pp2[...] = dot(pick_proj, proj2_ref[...]).astype(BF16)

        return 0

    lax.fori_loop(0, 3, pad_weights, 0)

    pl.semaphore_wait(barrier, 4 + 2 + n_lat - 1 + inner - 1 + outer - 1)

    halo = []
    for a in (1, 2):
        for b in (1, 2):
            for dy in (0, -1 if a == 1 else 1):
                for dx in (0, -1 if b == 1 else 1):
                    if dy == 0 and dx == 0:
                        continue
                    halo.append(
                        pltpu.make_async_remote_copy(
                            src_ref=region.at[slot(a, b)],
                            dst_ref=region.at[slot(a - 2 * dy, b - 2 * dx)],
                            send_sem=halo_send,
                            recv_sem=halo_recv,
                            device_id=at(dy, dx),
                            device_id_type=MESH,
                        )
                    )
    for copy in halo:
        copy.start()

    for load in loads[7:]:
        load.wait()

    def turned(c):
        r = 255 - c
        return ((r >> 3) & 7) * 32 + ((r >> 7) & 1) * 16 + ((r >> 6) & 1) * 8 + (r & 7)

    turn[0] = one_hot(iota((CELLS, CELLS), 0) == turned(iota((1, CELLS), 1)))
    turn[1] = one_hot(iota((CELLS, CELLS), 1) == turned(iota((CELLS, 1), 0)))

    flat1[...] = jnp.zeros(flat1.shape, F32)
    flat2[...] = jnp.zeros(flat2.shape, F32)
    for dy in range(SPAN):
        flat1[:, dy * 32 : dy * 32 + SPAN] = tab1_ref[:, dy * SPAN : (dy + 1) * SPAN]
    for dy in range(CROSS):
        for s in range(3):
            start = dy * CROSS + 8 * s
            flat2[s, :, dy * 32 : dy * 32 + 23] = tab2_ref[:, start : start + 23]
    def spread(pair, _):
        for i in range(2):
            h = 2 * pair + i
            row = pl.ds(h, 1)
            for s in range(2):
                base = jnp.broadcast_to(flat1[row, :] * LOG2E, (8, LANES_W))
                for r, part in enumerate(spread_rows(roll(base, 8 * s - 15), 1, 4)):
                    z1[s, r, h] = part[:, :USED_W]
            for s in range(3):
                base = jnp.broadcast_to(flat2[s, row, :] * LOG2E, (8, LANES_C))
                for r, part in enumerate(spread_rows(base, -1, 4)):
                    z2[s, r, h] = part[:, :USED_C]
        return 0

    lax.fori_loop(0, HEADS // 2, spread, 0)
    query_half = (iota((1, CELLS), 1) >> 4) & 1

    def window_bias(h, y8):
        pieces = []
        for sy in range(2):
            t, r = divmod(15 - (8 * sy + y8), 4)
            for sx in range(2):
                pieces.append(z1[sx, r, h, :, 128 * t : 128 * t + CELLS])
        return jnp.concatenate(pieces, axis=0)

    def cross_bias(h, ky):
        t, r = divmod(ky, 4)
        pieces = [z2[s, r, h, :, 128 * t : 128 * t + CELLS] for s in range(3)]
        return jnp.concatenate(pieces, axis=0)

    def by_eight(values):
        return values.reshape(values.shape[0] // 8, 8, CELLS)

    def add_bias(scores, step, count, bias):
        peak = None
        for c in range(count):
            rows = slice(c * step, (c + 1) * step)
            part = scores[rows, :] * (SCALE * LOG2E) + bias(c)
            scores[rows, :] = part
            part = jnp.max(by_eight(part), axis=0)
            peak = part if peak is None else jnp.maximum(peak, part)
        return jnp.max(peak, axis=0, keepdims=True)

    def raise_all(scores, step, count, peak, probs, columns, keep):
        total = None
        for c in range(count):
            rows = slice(c * step, (c + 1) * step)
            part = jnp.exp2(scores[rows, :] - peak)
            probs[rows, columns] = part.astype(BF16)
            if keep:
                scores[rows, :] = part
            part = jnp.sum(by_eight(part), axis=0)
            total = part if total is None else total + part
        return 1.0 / jnp.sum(total, axis=0, keepdims=True)

    def weigh_all(raised, grads, step, count, inverse):
        total = None
        for c in range(count):
            rows = slice(c * step, (c + 1) * step)
            part = raised(rows) * grads[rows, :]
            grads[rows, :] = part
            part = jnp.sum(by_eight(part), axis=0)
            total = part if total is None else total + part
        return jnp.sum(total, axis=0, keepdims=True) * inverse

    def slope_all(raised, grads, step, count, total, slopes, packed, columns):
        for c in range(count):
            rows = slice(c * step, (c + 1) * step)
            part = grads[rows, :] - raised(rows) * total
            slopes[rows, :] = part
            packed[rows, columns] = part.astype(BF16)

    def collect(acc, h, s, count, group_of, slopes):
        for r in range(4):
            for t in range(count // 4 + 1):
                parts = []
                if t < count // 4:
                    group = group_of(4 * t + r)
                    parts.append(slopes[group : group + 8, 0:128])
                if t > 0:
                    group = group_of(4 * t - 4 + r)
                    parts.append(slopes[group : group + 8, 128:256])
                acc[s, r, h, :, 128 * t : 128 * t + 128] = sum(parts[1:], parts[0])

    def head_rows(rows, h):
        before = h % 4 * HEAD_PAD
        pieces = [rows]
        if before:
            pieces = [jnp.zeros((before, CELLS), rows.dtype)] + pieces
        if before + HEAD_PAD < 128:
            pieces.append(jnp.zeros((128 - HEAD_PAD - before, CELLS), rows.dtype))
        return jnp.concatenate(pieces, axis=0) if len(pieces) > 1 else rows

    def head_block(rows, h):
        four = jnp.concatenate([rows] * 4, axis=0)
        return jnp.where((iota((128, CELLS), 0) >> 5) == lax.rem(h, 4), four, 0.0).astype(BF16)

    def head_lanes(values, into):
        zeros = jnp.zeros((CELLS, 128), BF16)
        for h in range(HEADS):
            half = h // 4 * 128
            lanes = iota((CELLS, 128), 1) >> 5
            own_lanes = jnp.where(lanes == h % 4, values[:, half : half + 128], 0.0).astype(BF16)
            rows = slice(h * CELLS, (h + 1) * CELLS)
            into[rows, half : half + 128] = own_lanes
            into[rows, 128 - half : 256 - half] = zeros

    every = region.at[pl.ds(0, 12)]
    pltpu.make_async_copy(every, every, halo_recv).wait()

    gain1 = gain1_ref[...]
    gain2 = gain2_ref[...]

    key_half = 30 + ((iota((CELLS, 1), 0) >> 4) & 1)
    lane_row = iota((1, WIDE), 1)
    marks = key_half == jnp.where(lane_row < 192, lane_row & 31, 0)
    pad_row = iota((HEAD_PAD, CELLS), 0)

    def own_columns(h):
        return slice(h * CELLS, (h + 1) * CELLS)

    def own_rows(h):
        return slice(h * HEAD_PAD, (h + 1) * HEAD_PAD)

    def window_row(wy, _):
        for wx in range(2):
            w = 2 * wy + wx
            for c in range(4):
                parts = [
                    region[w * 4 + s, 16 * c : 16 * c + 16, :]
                    .astype(F32)
                    .reshape(2, 1, 8, CHANNELS)
                    for s in range(4)
                ]
                values = jnp.concatenate(parts, axis=1).reshape(64, CHANNELS)
                rows = slice(64 * c, 64 * c + 64)
                feats[wx, rows, :] = values
                unit, _ = norm_parts(values)
                normed[wx, rows, :] = (unit * gain1).astype(BF16)
        edge = lat == jnp.where(wy == 0, 0, n_lat - 1)
        floor = jnp.where(edge, NEGATIVE, 0.0)
        hidden = jnp.where(pad_row - 30 == 1 - query_half, floor, 0.0)
        hidden = jnp.where(pad_row >= 30, hidden, 0.0)
        for wx in range(2):
            queries = dot_nt(wt1[0:WIDE, :], normed[wx])
            for h in range(HEADS):
                qmt[wx, h] = head_rows((queries[own_rows(h), :] + hidden).astype(BF16), h)
            keys = dot_nt(normed[wx], wt1[WIDE : 2 * WIDE, :])
            kk[wx] = jnp.where(marks, 1.0, keys).astype(BF16)
            vt[wx] = dot_nt(wt1[2 * WIDE :, :], normed[wx]).astype(BF16)
        for wx in range(2):
            for h in range(HEADS):
                half = h // 4 * 128
                s1[wx, h] = dot(kk[wx, :, half : half + 128], qmt[wx, h])
        for wx in range(2):
            for h in range(HEADS):
                scores = s1.at[wx, h]
                peak = add_bias(scores, 32, 8, functools.partial(window_bias, h))
                inverse = raise_all(scores, 32, 8, peak, p1.at[wx], own_columns(h), False)
                inverse1[wx, h] = inverse
        for wx in range(2):
            for h in range(HEADS):
                rows = own_rows(h)
                heads_t = dot(vt[wx, rows, :], p1[wx, :, own_columns(h)])
                ot[wx, rows, :] = heads_t * inverse1[wx, h]
        for wx in range(2):
            heads_out = jnp.transpose(ot[wx]).astype(BF16)
            middle = feats[wx] + dot(heads_out, pp1[...])
            middles[2 * wy + wx] = middle.reshape(8, 2, 2, 8, CHANNELS)
        return 0

    ot[...] = jnp.zeros(ot.shape, F32)
    lax.fori_loop(0, 2, window_row, 0)

    y_runs = ((0, 0, 4, 8, 0), (0, 1, 0, 8, 4), (1, 0, 0, 8, 12), (1, 1, 0, 4, 20))
    for wy, sy, first, last, place in y_runs:
        for wx in range(2):
            for sx in range(2):
                start = (2 * wx + sx) * 8
                lin[place : place + last - first, start : start + 8, :] = middles[
                    2 * wy + wx, first:last, sy, sx
                ]

    def second_norm(step, _):
        for k in range(4):
            i = 4 * step + k
            lines, rows = pl.ds(2 * i, 2), pl.ds(pl.multiple_of(64 * i, 64), 64)
            unit, inverse = norm_parts(lin[lines].reshape(64, CHANNELS))
            units[rows, :] = unit
            inverses[rows, :] = inverse
            normal = (unit * gain2).astype(BF16).astype(F32)
            lin[lines] = normal.reshape(2, 32, CHANNELS)
        return 0

    lax.fori_loop(0, KEY_SIDE // 8, second_norm, 0)
    inside_low = jnp.where(lat > 0, 1.0, 0.0)
    inside_high = jnp.where(lat < n_lat - 1, 1.0, 0.0)
    lin[0:4] = lin[0:4] * inside_low
    lin[20:24] = lin[20:24] * inside_high
    keys_in = lin[:, 4:28, :].reshape(KEYS, CHANNELS).astype(BF16)
    k2[...] = dot_nt(keys_in, wt2[WIDE : 2 * WIDE, :]).astype(BF16)
    v2[...] = dot_nt(keys_in, wt2[2 * WIDE :, :]).astype(BF16)
    k2t[...] = dot_nt(wt2[WIDE : 2 * WIDE, :], keys_in).astype(BF16)

    def own_part(sy, sx):
        return slice(4 + 8 * sy, 12 + 8 * sy), slice(8 + 8 * sx, 16 + 8 * sx)

    own_second = jnp.concatenate(
        [lin[(*own_part(sy, sx), slice(None))].reshape(64, CHANNELS) for sy, sx, w, s in OWN],
        axis=0,
    )
    queries_in = dot(turn[0], own_second.astype(BF16)).astype(BF16)
    cot = cot_ref[...].astype(F32)
    cot_own = [
        cot[8 * sy : 8 * sy + 8, 8 * sx : 8 * sx + 8, :].reshape(64, CHANNELS)
        for sy, sx, w, s in OWN
    ]
    cot_in = dot(turn[0], jnp.concatenate(cot_own, axis=0).astype(BF16)).astype(BF16)
    queries_t = dot_nt(wt2[0:WIDE, :], queries_in).astype(BF16)
    gt[...] = dot_nt(pp2[...], cot_in)
    for h in range(HEADS):
        qmt[0, h] = head_rows(queries_t[h * HEAD_PAD : (h + 1) * HEAD_PAD, :], h)
    head_lanes(dot_nt(queries_in, wt2[0:WIDE, :]), qm)

    def cross_heads(group, _):
        heads = [3 * group + i for i in range(3)]

        def half(h):
            return pl.ds(pl.multiple_of(h // 4 * 128, 128), 128)

        def columns(h):
            return pl.ds(pl.multiple_of(h * CELLS, CELLS), CELLS)

        def rows(h):
            return pl.ds(pl.multiple_of(h * HEAD_PAD, HEAD_PAD), HEAD_PAD)

        def bias(h, c):
            return jnp.concatenate([cross_bias(h, 2 * c), cross_bias(h, 2 * c + 1)], axis=0)

        for i, h in enumerate(heads):
            s2[i] = dot(k2[:, half(h)], qmt[0, h])
        inverse = []
        for i, h in enumerate(heads):
            peak = add_bias(s2.at[i], 48, 12, functools.partial(bias, h))
            inverse.append(raise_all(s2.at[i], 48, 12, peak, p2, columns(h), True))
            scaled = gt[rows(h), :] * inverse[i]
            gt[rows(h), :] = scaled
            g2[i] = dot(v2[:, half(h)], head_block(scaled, h))
        for i, h in enumerate(heads):
            scores, grads = s2.at[i], g2.at[i]

            def raised(part):
                return scores[part, :]

            total = weigh_all(raised, grads, 48, 12, inverse[i])
            slope_all(raised, grads, 48, 12, total, scores, ds2, columns(h))
            for s in range(3):
                collect(acc2, h, s, KEY_SIDE, lambda m: (m * 3 + s) * 8, scores)
        for h in heads:
            ot[0, rows(h), :] = dot(k2t[rows(h), :], ds2[:, columns(h)])
        return 0

    lax.fori_loop(0, HEADS // 3, cross_heads, 0)
    head_lanes(jnp.transpose(gt[...]), dom)
    grad_queries = (jnp.transpose(ot[0]) * SCALE).astype(BF16)
    grad_keys = (dot(ds2[...], qm[...]) * SCALE).astype(BF16)
    grad_values = dot(p2[...], dom[...]).astype(BF16)
    grad_second = dot(grad_keys, wt2[WIDE : 2 * WIDE, :]) + dot(grad_values, wt2[2 * WIDE :, :])
    grad_own = dot(turn[1], dot(grad_queries, wt2[0:WIDE, :]).astype(BF16))

    lin[...] = jnp.zeros(lin.shape, F32)
    lin[:, 4:28, :] = grad_second.reshape(KEY_SIDE, KEY_SIDE, CHANNELS)
    lin[0:4] = lin[0:4] * inside_low
    lin[20:24] = lin[20:24] * inside_high
    for i, (sy, sx, w, s) in enumerate(OWN):
        place = (*own_part(sy, sx), slice(None))
        lin[place] = lin[place] + grad_own[64 * i : 64 * i + 64, :].reshape(8, 8, CHANNELS)

    def second_back(step, _):
        for k in range(4):
            i = 4 * step + k
            lines, rows = pl.ds(2 * i, 2), pl.ds(pl.multiple_of(64 * i, 64), 64)
            grad = lin[lines].reshape(64, CHANNELS)
            grad = norm_back(units[rows, :], inverses[rows, :], gain2, grad)
            lin[lines] = grad.reshape(2, 32, CHANNELS)
        return 0

    lax.fori_loop(0, KEY_SIDE // 8, second_back, 0)
    for i, (sy, sx, w, s) in enumerate(OWN):
        place = (*own_part(sy, sx), slice(None))
        lin[place] = lin[place] + cot_own[i].reshape(8, 8, CHANNELS)
    for w in range(3):
        rows, cols = 12 * (w // 2), 16 * (w % 2)
        piece = lin[rows : rows + 12, cols : cols + 16, :]
        mid_out[w] = piece.reshape(192, CHANNELS).astype(BF16)
        pltpu.make_async_remote_copy(
            src_ref=mid_out.at[w],
            dst_ref=mid_in.at[w],
            send_sem=mid_send,
            recv_sem=mid_recv,
            device_id=at(w // 2 - 1, w % 2 - 1),
            device_id_type=MESH,
        ).start()

    def sum_scatter(kind, tiles, buffer):
        chunks, depth = buffer_plan(tiles, n_lat)
        for c in range(chunks):

            @pl.when(lat != c)
            def _():
                pltpu.make_async_remote_copy(
                    src_ref=tiles.at[pl.ds(c * depth, depth)],
                    dst_ref=buffer.at[wrapped(lat - c, n_lat) - 1],
                    send_sem=sum_send.at[kind],
                    recv_sem=sum_recv.at[kind],
                    device_id=(lon, c),
                    device_id_type=MESH,
                ).start()

    def drain(sem, ref):
        pltpu.make_async_copy(ref, ref, sem).wait()

    def sum_spread(kind, tiles, buffer, rows):
        chunks, depth = buffer_plan(tiles, n_lat)

        @pl.when(lat < chunks)
        def _():
            drain(sum_recv.at[kind], buffer)
            total = tiles[pl.ds(lat * depth, depth)]
            for i in range(n_lat - 1):
                total = total + buffer[i]
            rows[spot] = total
            for j in range(1, inner):
                pltpu.make_async_remote_copy(
                    src_ref=rows.at[spot],
                    dst_ref=rows.at[spot],
                    send_sem=sum_send.at[kind + 1],
                    recv_sem=sum_recv.at[kind + 1],
                    device_id=inner_peer(j),
                    device_id_type=MESH,
                ).start()

    def sum_cross(kind, tiles, rows, far):
        chunks, depth = buffer_plan(tiles, n_lat)
        block = lax.div(lon, inner)

        @pl.when(lat < chunks)
        def _():
            drain(sum_recv.at[kind + 1], rows.at[pl.ds(0, inner - 1)])
            total = rows[0]
            for i in range(1, inner):
                total = total + rows[i]
            far[block] = total
            for j in range(1, outer):
                pltpu.make_async_remote_copy(
                    src_ref=far.at[block],
                    dst_ref=far.at[block],
                    send_sem=sum_send.at[kind + 2],
                    recv_sem=sum_recv.at[kind + 2],
                    device_id=at(0, j * inner),
                    device_id_type=MESH,
                ).start()

    def sum_gather(kind, tiles, far, result):
        chunks, depth = buffer_plan(tiles, n_lat)

        @pl.when(lat < chunks)
        def _():
            if outer > 1:
                drain(sum_recv.at[kind + 2], far.at[pl.ds(0, outer - 1)])
            total = far[0]
            for i in range(1, outer):
                total = total + far[i]
            result[lat] = total
            for j in range(1, n_lat):
                pltpu.make_async_remote_copy(
                    src_ref=result.at[lat],
                    dst_ref=result.at[lat],
                    send_sem=sum_send.at[kind + 3],
                    recv_sem=sum_recv.at[kind + 3],
                    device_id=at(j, 0),
                    device_id_type=MESH,
                ).start()

    def sum_end(kind, tiles, buffer, rows, far, result):
        chunks, depth = buffer_plan(tiles, n_lat)

        @pl.when(lat < chunks)
        def _():
            if chunks > 1:
                drain(sum_recv.at[kind + 3], result.at[pl.ds(0, chunks - 1)])
                drain(sum_send.at[kind], result.at[pl.ds(0, chunks - 1)])
            drain(sum_send.at[kind + 1], rows.at[pl.ds(0, inner - 1)])
            if outer > 1:
                drain(sum_send.at[kind + 2], far.at[pl.ds(0, outer - 1)])
            drain(sum_send.at[kind + 3], buffer)

        @pl.when(lat >= chunks)
        def _():
            drain(sum_recv.at[kind + 3], result)
            drain(sum_send.at[kind], result)

    def joined(result, count):
        chunks, depth = result.shape[0], result.shape[1]
        whole = jnp.concatenate(
            [result[c, d] for c in range(chunks) for d in range(depth)], axis=1
        )
        return whole[:, :count]

    def widened(part, width):
        return jnp.concatenate([part, jnp.zeros((8, width - part.shape[1]), F32)], axis=1)

    def gather_cross(pair, _):
        for i in range(2):
            h = 2 * pair + i
            for s in range(3):
                parts = [widened(acc2[s, r, h], LANES_C) for r in range(4)]
                flat2[s, pl.ds(h, 1), :] = gather_rows(parts, -1)
        return 0

    lax.fori_loop(0, HEADS // 2, gather_cross, 0)
    dense2[...] = jnp.zeros(dense2.shape, F32)
    for dy in range(CROSS):
        for s in range(3):
            start = dy * CROSS + 8 * s
            dense2[s, 0:HEADS, start : start + 23] = flat2[s, :, dy * 32 : dy * 32 + 23]
    for t in range(TILES_C):
        part = pl.ds(128 * t, 128)
        whole = dense2[0, :, part] + dense2[1, :, part] + dense2[2, :, part]
        tiles2[t] = whole[:HEADS]
    sum_scatter(0, tiles2, rs2)

    vv[...] = dot_nt(normed[1], wt1[2 * WIDE :, :]).astype(BF16)
    kt[...] = dot_nt(wt1[WIDE : 2 * WIDE, :], normed[1]).astype(BF16)
    head_lanes(dot_nt(normed[1], wt1[0:WIDE, :]), qm)

    drain(mid_recv, mid_in)
    total = lin[12:24, 16:32, :] + mid_in[2].astype(F32).reshape(12, 16, CHANNELS)
    below = (mid_in[0].astype(F32) + mid_in[1].astype(F32)).reshape(12, 16, CHANNELS)
    total = jnp.concatenate([total[0:4], total[4:12] + below[0:8], below[8:12]], axis=0)
    pair = [total[8 * sy : 8 * sy + 8].reshape(8, 1, 16, CHANNELS) for sy in range(2)]
    grad_mid[...] = jnp.concatenate(pair, axis=1).reshape(CELLS, CHANNELS)
    sum_spread(0, tiles2, rs2, ag2)

    grads_t = dot_nt(pp1[...], grad_mid[...].astype(BF16))
    for h in range(HEADS):
        scaled = grads_t[own_rows(h), :] * inverse1[1, h]
        gt[own_rows(h), :] = scaled
        half = h // 4 * 128
        s1[1, h] = dot(vv[:, half : half + 128], head_rows(scaled.astype(BF16), h))
    for h in range(HEADS):

        def raised(part):
            return p1[1, part, own_columns(h)].astype(F32)

        total = weigh_all(raised, s1.at[1, h], 32, 8, inverse1[1, h])
        slope_all(raised, s1.at[1, h], 32, 8, total, s1.at[0, h], ds1, own_columns(h))
        for sx in range(2):

            def group_of(m):
                ky = 15 - m
                return (ky % 8 * 4 + ky // 8 * 2 + sx) * 8

            collect(acc1, h, sx, 16, group_of, s1.at[0, h])
    sum_cross(0, tiles2, ag2, far2)

    for h in range(HEADS):
        total = None
        for s in range(2):
            parts = [widened(acc1[s, r, h], LANES_W) for r in range(4)]
            piece = roll(gather_rows(parts, 1), 15 - 8 * s)
            total = piece if total is None else total + piece
        flat1[h : h + 1, :] = total
    dense1[...] = jnp.zeros(dense1.shape, F32)
    for dy in range(SPAN):
        dense1[0:HEADS, dy * SPAN : (dy + 1) * SPAN] = flat1[:, dy * 32 : dy * 32 + SPAN]
    for t in range(TILES_W):
        tiles1[t] = dense1[:HEADS, 128 * t : 128 * t + 128]
    sum_scatter(4, tiles1, rs1)
    sum_gather(0, tiles2, far2, fin2)

    for h in range(HEADS):
        ot[0, own_rows(h), :] = dot(kt[own_rows(h), :], ds1[:, own_columns(h)])
    head_lanes(jnp.transpose(gt[...]), dom)
    grad_queries = (jnp.transpose(ot[0]) * SCALE).astype(BF16)
    grad_keys = (dot(ds1[...], qm[...]) * SCALE).astype(BF16)
    grad_values = dot(p1[1], dom[...])
    grad_first[...] = (
        dot(grad_queries, wt1[0:WIDE, :])
        + dot(grad_keys, wt1[WIDE : 2 * WIDE, :])
        + dot(grad_values.astype(BF16), wt1[2 * WIDE :, :])
    )
    for c in range(4):
        rows = slice(64 * c, 64 * c + 64)
        unit, inverse = norm_parts(feats[1, rows, :])
        grad = grad_mid[rows, :] + norm_back(unit, inverse, gain1, grad_first[rows, :])
        quarters = grad.reshape(2, 2, 2, 8, CHANNELS)
        out_ref[8 + 2 * c : 10 + 2 * c, 8:16, :] = quarters[:, 0, 0]
        for s in (1, 2, 3):
            piece = quarters[:, s // 2, s % 2].reshape(16, CHANNELS)
            back_out[s - 1, 16 * c : 16 * c + 16, :] = piece.astype(BF16)
    for s in (1, 2, 3):
        pltpu.make_async_remote_copy(
            src_ref=back_out.at[s - 1],
            dst_ref=back_in.at[s - 1],
            send_sem=back_send,
            recv_sem=back_recv,
            device_id=at(s // 2, s % 2),
            device_id_type=MESH,
        ).start()
    sum_spread(4, tiles1, rs1, ag1)
    drain(back_recv, back_in)
    out_ref[8:16, 0:8, :] = back_in[0].astype(F32).reshape(8, 8, CHANNELS)
    out_ref[0:8, 8:16, :] = back_in[1].astype(F32).reshape(8, 8, CHANNELS)
    out_ref[0:8, 0:8, :] = back_in[2].astype(F32).reshape(8, 8, CHANNELS)
    sum_cross(4, tiles1, ag1, far1)
    sum_gather(4, tiles1, far1, fin1)
    sum_end(0, tiles2, rs2, ag2, far2, fin2)
    out2_ref[...] = joined(fin2, CROSS * CROSS)
    sum_end(4, tiles1, rs1, ag1, far1, fin1)
    pltpu.make_async_copy(every, every, halo_send).wait()
    drain(mid_send, mid_out)
    drain(back_send, back_out)
    out1_ref[...] = joined(fin1, SPAN * SPAN)


def lon_plan(n_lon):
    inner = 8 if n_lon % 8 == 0 else 2 if n_lon % 2 == 0 else n_lon
    return inner, n_lon // inner


def buffer_plan(tiles, n_lat):
    count = tiles.shape[0]
    chunks = min(n_lat, count)
    return chunks, count // chunks


def body(n_lat, n_lon, *operands):
    vmem = pltpu.VMEM
    inner, outer = lon_plan(n_lon)

    def sums(count):
        chunks = min(n_lat, count)
        depth = count // chunks
        return (
            vmem((count, HEADS, 128), F32),
            vmem((n_lat - 1, depth, HEADS, 128), F32),
            vmem((inner, depth, HEADS, 128), F32),
            vmem((outer, depth, HEADS, 128), F32),
            vmem((chunks, depth, HEADS, 128), F32),
        )

    tiles1, rs1, ag1, far1, fin1 = sums(TILES_W)
    tiles2, rs2, ag2, far2, fin2 = sums(TILES_C)
    scratch = [
        vmem((16, 16, CHANNELS), BF16),
        vmem((16, 16, CHANNELS), BF16),
        vmem((1, CHANNELS), F32),
        vmem((CHANNELS, 3 * CHANNELS), BF16),
        vmem((CHANNELS, CHANNELS), BF16),
        vmem((HEADS, SPAN * SPAN), F32),
        vmem((1, CHANNELS), F32),
        vmem((CHANNELS, 3 * CHANNELS), BF16),
        vmem((CHANNELS, CHANNELS), BF16),
        vmem((HEADS, CROSS * CROSS), F32),
        pltpu.SemaphoreType.DMA((10,)),
        vmem((16, 64, CHANNELS), BF16),
        vmem((HEADS, LANES_W), F32),
        vmem((3, HEADS, LANES_C), F32),
        vmem((3 * WIDE, CHANNELS), BF16),
        vmem((3 * WIDE, CHANNELS), BF16),
        vmem((WIDE, CHANNELS), BF16),
        vmem((WIDE, CHANNELS), BF16),
        vmem((2, CELLS, CELLS), BF16),
        vmem((2, 4, HEADS, 8, USED_W), F32),
        vmem((3, 4, HEADS, 8, USED_C), F32),
        vmem((2, 4, HEADS, 8, USED_W), F32),
        vmem((3, 4, HEADS, 8, USED_C), F32),
        vmem((2, CELLS, CHANNELS), F32),
        vmem((4, 8, 2, 2, 8, CHANNELS), F32),
        vmem((KEY_SIDE * 32, CHANNELS), F32),
        vmem((KEY_SIDE * 32, 1), F32),
        vmem((2, CELLS, WIDE), BF16),
        vmem((2, WIDE, CELLS), BF16),
        vmem((CELLS, WIDE), BF16),
        vmem((WIDE, CELLS), BF16),
        vmem((HEADS * CELLS, WIDE), BF16),
        vmem((HEADS * CELLS, WIDE), BF16),
        vmem((2, HEADS, 128, CELLS), BF16),
        vmem((WIDE, CELLS), F32),
        vmem((2, WIDE, CELLS), F32),
        vmem((2, CELLS, CHANNELS), BF16),
        vmem((2, HEADS, 1, CELLS), F32),
        vmem((2, HEADS, CELLS, CELLS), F32),
        vmem((3, KEYS, CELLS), F32),
        vmem((3, KEYS, CELLS), F32),
        vmem((CELLS, CHANNELS), F32),
        vmem((CELLS, CHANNELS), F32),
        vmem((2, CELLS, HEADS * CELLS), BF16),
        vmem((KEYS, HEADS * CELLS), BF16),
        vmem((CELLS, HEADS * CELLS), BF16),
        vmem((KEYS, HEADS * CELLS), BF16),
        vmem((KEYS, WIDE), BF16),
        vmem((KEYS, WIDE), BF16),
        vmem((WIDE, KEYS), BF16),
        vmem((KEY_SIDE, 32, CHANNELS), F32),
        vmem((3, 192, CHANNELS), BF16),
        vmem((3, 192, CHANNELS), BF16),
        vmem((3, 64, CHANNELS), BF16),
        vmem((3, 64, CHANNELS), BF16),
        vmem((8, 128 * TILES_W), F32),
        vmem((3, 8, 128 * TILES_C), F32),
        tiles1,
        tiles2,
        rs1,
        rs2,
        ag1,
        ag2,
        far1,
        far2,
        fin1,
        fin2,
        pltpu.SemaphoreType.DMA,
        pltpu.SemaphoreType.DMA,
        pltpu.SemaphoreType.DMA,
        pltpu.SemaphoreType.DMA,
        pltpu.SemaphoreType.DMA,
        pltpu.SemaphoreType.DMA,
        pltpu.SemaphoreType.DMA((8,)),
        pltpu.SemaphoreType.DMA((8,)),
    ]
    whole = pl.BlockSpec(memory_space=pltpu.VMEM)
    return pl.pallas_call(
        functools.partial(kernel, n_lat, n_lon),
        out_shape=(
            jax.ShapeDtypeStruct((16, 16, CHANNELS), F32),
            jax.ShapeDtypeStruct((HEADS, SPAN * SPAN), F32),
            jax.ShapeDtypeStruct((HEADS, CROSS * CROSS), F32),
        ),
        in_specs=[pl.BlockSpec(memory_space=pltpu.HBM)] * 10,
        out_specs=(whole, whole, whole),
        scratch_shapes=scratch,
        compiler_params=pltpu.CompilerParams(
            collective_id=0, has_side_effects=True, vmem_limit_bytes=63 * 1024 * 1024
        ),
    )(*operands)


def solution(mesh):
    def local(
        features,
        cotangent,
        first_gain,
        window_qkv,
        window_proj,
        window_table,
        second_gain,
        cross_qkv,
        cross_proj,
        cross_table,
    ):
        return body(
            mesh.shape["lat"],
            mesh.shape["lon"],
            features,
            cotangent,
            first_gain.reshape(1, CHANNELS),
            window_qkv,
            window_proj,
            window_table,
            second_gain.reshape(1, CHANNELS),
            cross_qkv,
            cross_proj,
            cross_table,
        )

    return jax.shard_map(
        local,
        mesh=mesh,
        in_specs=(
            P("lat", "lon", None),
            P("lat", "lon", None),
            P(),
            P(),
            P(),
            P(),
            P(),
            P(),
            P(),
            P(),
        ),
        out_specs=(P("lat", "lon", None), P(), P()),
        check_vma=False,
    )
```

```python
import functools

import jax
import jax.numpy as jnp
from jax import lax
from jax.experimental import pallas as pl
from jax.experimental.pallas import tpu as pltpu
from jax.sharding import PartitionSpec as P

CHANNELS = 180
HEADS = 6
HEAD_SIZE = 30
HEAD_PAD = 32
WIDE = 256
CELLS = 256
KEYS = 576
KEY_SIDE = 24
SPAN = 31
CROSS = 39
EPSILON = 1e-05
NEGATIVE = -1e30
LOG2E = 1.4426950408889634
SCALE = HEAD_SIZE**-0.5
TILES_W = 8
TILES_C = 12
LANES_W = 1024
LANES_C = 1280
USED_W = 640
USED_C = 896
MESH = pl.DeviceIdType.MESH
F32 = jnp.float32
BF16 = jnp.bfloat16


def iota(shape, dim):
    return lax.broadcasted_iota(jnp.int32, shape, dim)


def dot(a, b):
    return jnp.dot(a, b, preferred_element_type=F32)


def dot_nt(a, b):
    return lax.dot_general(a, b, (((1,), (1,)), ((), ())), preferred_element_type=F32)


def one_hot(mask):
    return jnp.where(mask, 1.0, 0.0).astype(BF16)


def roll(x, shift):
    size = x.shape[-1]
    return pltpu.roll(x, shift % size, x.ndim - 1)


def norm_parts(values):
    centre = jnp.mean(values, axis=-1, keepdims=True)
    offset = values - centre
    spread = jnp.mean(offset * offset, axis=-1, keepdims=True)
    inverse = lax.rsqrt(spread + EPSILON)
    return offset * inverse, inverse


def norm_back(unit, inverse, gain, grads):
    scaled = grads * gain
    first = jnp.mean(scaled, axis=-1, keepdims=True)
    second = jnp.mean(scaled * unit, axis=-1, keepdims=True)
    return inverse * (scaled - first - unit * second)


OWN = [(sy, sx, 2 * sy + sx, (1 - sy) * 2 + (1 - sx)) for sy in (0, 1) for sx in (0, 1)]


def spread_rows(base, stride, ways):
    rows = iota(base.shape, 0)
    for bit in (1, 2, 4):
        base = jnp.where((rows & bit) != 0, roll(base, stride * bit), base)
    upper = (iota(base.shape, 1) & 16) != 0
    base = jnp.where(upper, roll(base, -240), base)
    return [base if r == 0 else roll(base, -32 * r) for r in range(ways)]


def gather_rows(parts, stride):
    total = parts[0]
    for r in range(1, len(parts)):
        total = total + roll(parts[r], 32 * r)
    upper = (iota(total.shape, 1) & 16) != 0
    total = jnp.where(upper, 0.0, total) + roll(jnp.where(upper, total, 0.0), 240)
    rows = iota(total.shape, 0)
    for bit in (1, 2, 4):
        total = jnp.where((rows & bit) != 0, roll(total, -stride * bit), total)
    return jnp.sum(total, axis=0, keepdims=True)


def kernel(
    n_lat,
    n_lon,
    feat_in,
    cot_in_hbm,
    gain1_in,
    qkv1_in,
    proj1_in,
    tab1_in,
    gain2_in,
    qkv2_in,
    proj2_in,
    tab2_in,
    out_hbm,
    out1_hbm,
    out2_hbm,
    out_ref,
    out1_ref,
    out2_ref,
    feat_ref,
    cot_ref,
    gain1_ref,
    qkv1_ref,
    proj1_ref,
    tab1_ref,
    gain2_ref,
    qkv2_ref,
    proj2_ref,
    tab2_ref,
    load_sem,
    region,
    flat1,
    flat2,
    wt1,
    wt2,
    pp1,
    pp2,
    turn,
    z1,
    z2,
    acc1,
    acc2,
    feats,
    middles,
    units,
    inverses,
    kk,
    vt,
    vv,
    kt,
    qm,
    dom,
    qmt,
    gt,
    ot,
    normed,
    inverse1,
    s1,
    s2,
    g2,
    grad_mid,
    grad_first,
    p1,
    p2,
    ds1,
    ds2,
    k2,
    v2,
    k2t,
    lin,
    mid_out,
    mid_in,
    back_out,
    back_in,
    dense1,
    dense2,
    tiles1,
    tiles2,
    rs1,
    rs2,
    ag1,
    ag2,
    far1,
    far2,
    fin1,
    fin2,
    halo_send,
    halo_recv,
    mid_send,
    mid_recv,
    back_send,
    back_recv,
    sum_send,
    sum_recv,
):
    lat = lax.axis_index("lat")
    lon = lax.axis_index("lon")

    def wrapped(value, count):
        value = jnp.where(value >= count, value - count, value)
        return jnp.where(value < 0, value + count, value)

    def at(dy, dx):
        return (wrapped(lon + dx, n_lon), wrapped(lat + dy, n_lat))

    loads = [
        pltpu.make_async_copy(src, dst, load_sem.at[i])
        for i, (src, dst) in enumerate(
            (
                (feat_in, feat_ref),
                (qkv1_in, qkv1_ref),
                (proj1_in, proj1_ref),
                (qkv2_in, qkv2_ref),
                (proj2_in, proj2_ref),
                (tab1_in, tab1_ref),
                (tab2_in, tab2_ref),
                (gain1_in, gain1_ref),
                (gain2_in, gain2_ref),
                (cot_in_hbm, cot_ref),
            )
        )
    ]
    for load in loads:
        load.start()

    barrier = pltpu.get_barrier_semaphore()

    def greet(dy, dx):
        pl.semaphore_signal(barrier, inc=1, device_id=at(dy, dx), device_id_type=MESH)

    for dy in (-1, 0, 1):
        for dx in (-1, 0, 1):
            if dy or dx:
                greet(dy, dx)
    for j in range(2, n_lat - 1):
        greet(j, 0)
    inner, outer = lon_plan(n_lon)
    spot = lax.rem(lon, inner)

    def inner_peer(j):
        return (lon - spot + wrapped(spot + j, inner), lat)

    def greet_at(device):
        pl.semaphore_signal(barrier, inc=1, device_id=device, device_id_type=MESH)

    for j in range(1, inner):
        greet_at(inner_peer(j))
    for j in range(1, outer):
        greet(0, j * inner)

    loads[0].wait()
    own = feat_ref[...].astype(F32)
    for sy, sx, w, s in OWN:
        quarter = own[8 * sy : 8 * sy + 8, 8 * sx : 8 * sx + 8, :].reshape(64, CHANNELS)
        region[1 + sy, 1 + sx] = quarter.astype(BF16)

    for load in loads[1:7]:
        load.wait()

    def pad_weights(i, _):
        lane = iota((WIDE, 1), 0)
        real = (lane < 192) & ((lane & 31) < HEAD_SIZE)
        source = jnp.where(real, CHANNELS * i + lane - 2 * (lane >> 5), -1)
        pick = one_hot(iota((WIDE, 3 * CHANNELS), 1) == source)
        rows = pl.ds(pl.multiple_of(i * WIDE, WIDE), WIDE)
        wt1[rows, :] = dot_nt(pick, qkv1_ref[...]).astype(BF16)
        wt2[rows, :] = dot_nt(pick, qkv2_ref[...]).astype(BF16)

        @pl.when(i == 0)
        def _():
            pick_proj = pick[:, :CHANNELS]
            pp1[...] = dot(pick_proj, proj1_ref[...]).astype(BF16)
            pp2[...] = dot(pick_proj, proj2_ref[...]).astype(BF16)

        return 0

    lax.fori_loop(0, 3, pad_weights, 0)

    pl.semaphore_wait(barrier, 8 + n_lat - 3 + inner - 1 + outer - 1)

    def side(step):
        here = {-1: 1, 0: pl.ds(1, 2), 1: 2}[step]
        there = {-1: 3, 0: pl.ds(1, 2), 1: 0}[step]
        return here, there

    for dy in (-1, 0, 1):
        for dx in (-1, 0, 1):
            if dy == 0 and dx == 0:
                continue
            (a, a_there), (b, b_there) = side(dy), side(dx)
            pltpu.make_async_remote_copy(
                src_ref=region.at[a, b],
                dst_ref=region.at[a_there, b_there],
                send_sem=halo_send,
                recv_sem=halo_recv,
                device_id=at(dy, dx),
                device_id_type=MESH,
            ).start()

    for load in loads[7:]:
        load.wait()

    def turned(c):
        r = 255 - c
        return ((r >> 3) & 7) * 32 + ((r >> 7) & 1) * 16 + ((r >> 6) & 1) * 8 + (r & 7)

    turn[0] = one_hot(iota((CELLS, CELLS), 0) == turned(iota((1, CELLS), 1)))
    turn[1] = one_hot(iota((CELLS, CELLS), 1) == turned(iota((CELLS, 1), 0)))

    flat1[...] = jnp.zeros(flat1.shape, F32)
    flat2[...] = jnp.zeros(flat2.shape, F32)
    for dy in range(SPAN):
        flat1[:, dy * 32 : dy * 32 + SPAN] = tab1_ref[:, dy * SPAN : (dy + 1) * SPAN]
    for dy in range(CROSS):
        for s in range(3):
            start = dy * CROSS + 8 * s
            flat2[s, :, dy * 32 : dy * 32 + 23] = tab2_ref[:, start : start + 23]
    def spread(pair, _):
        for i in range(2):
            h = 2 * pair + i
            row = pl.ds(h, 1)
            for s in range(2):
                base = jnp.broadcast_to(flat1[row, :] * LOG2E, (8, LANES_W))
                for r, part in enumerate(spread_rows(roll(base, 8 * s - 15), 1, 4)):
                    z1[s, r, h] = part[:, :USED_W]
            for s in range(3):
                base = jnp.broadcast_to(flat2[s, row, :] * LOG2E, (8, LANES_C))
                for r, part in enumerate(spread_rows(base, -1, 4)):
                    z2[s, r, h] = part[:, :USED_C]
        return 0

    lax.fori_loop(0, HEADS // 2, spread, 0)
    query_half = (iota((1, CELLS), 1) >> 4) & 1

    def window_bias(h, y8):
        pieces = []
        for sy in range(2):
            t, r = divmod(15 - (8 * sy + y8), 4)
            for sx in range(2):
                pieces.append(z1[sx, r, h, :, 128 * t : 128 * t + CELLS])
        return jnp.concatenate(pieces, axis=0)

    def cross_bias(h, ky):
        t, r = divmod(ky, 4)
        pieces = [z2[s, r, h, :, 128 * t : 128 * t + CELLS] for s in range(3)]
        return jnp.concatenate(pieces, axis=0)

    def by_eight(values):
        return values.reshape(values.shape[0] // 8, 8, CELLS)

    def add_bias(scores, step, count, bias):
        peak = None
        for c in range(count):
            rows = slice(c * step, (c + 1) * step)
            part = scores[rows, :] * (SCALE * LOG2E) + bias(c)
            scores[rows, :] = part
            part = jnp.max(by_eight(part), axis=0)
            peak = part if peak is None else jnp.maximum(peak, part)
        return jnp.max(peak, axis=0, keepdims=True)

    def raise_all(scores, step, count, peak, probs, columns, keep):
        total = None
        for c in range(count):
            rows = slice(c * step, (c + 1) * step)
            part = jnp.exp2(scores[rows, :] - peak)
            probs[rows, columns] = part.astype(BF16)
            if keep:
                scores[rows, :] = part
            part = jnp.sum(by_eight(part), axis=0)
            total = part if total is None else total + part
        return 1.0 / jnp.sum(total, axis=0, keepdims=True)

    def weigh_all(raised, grads, step, count, inverse):
        total = None
        for c in range(count):
            rows = slice(c * step, (c + 1) * step)
            part = raised(rows) * grads[rows, :]
            grads[rows, :] = part
            part = jnp.sum(by_eight(part), axis=0)
            total = part if total is None else total + part
        return jnp.sum(total, axis=0, keepdims=True) * inverse

    def slope_all(raised, grads, step, count, total, slopes, packed, columns):
        for c in range(count):
            rows = slice(c * step, (c + 1) * step)
            part = grads[rows, :] - raised(rows) * total
            slopes[rows, :] = part
            packed[rows, columns] = part.astype(BF16)

    def collect(acc, h, s, count, group_of, slopes):
        for r in range(4):
            for t in range(count // 4 + 1):
                parts = []
                if t < count // 4:
                    group = group_of(4 * t + r)
                    parts.append(slopes[group : group + 8, 0:128])
                if t > 0:
                    group = group_of(4 * t - 4 + r)
                    parts.append(slopes[group : group + 8, 128:256])
                acc[s, r, h, :, 128 * t : 128 * t + 128] = sum(parts[1:], parts[0])

    def head_rows(rows, h):
        before = h % 4 * HEAD_PAD
        pieces = [rows]
        if before:
            pieces = [jnp.zeros((before, CELLS), rows.dtype)] + pieces
        if before + HEAD_PAD < 128:
            pieces.append(jnp.zeros((128 - HEAD_PAD - before, CELLS), rows.dtype))
        return jnp.concatenate(pieces, axis=0) if len(pieces) > 1 else rows

    def head_block(rows, h):
        four = jnp.concatenate([rows] * 4, axis=0)
        return jnp.where((iota((128, CELLS), 0) >> 5) == lax.rem(h, 4), four, 0.0).astype(BF16)

    def head_lanes(values, into):
        zeros = jnp.zeros((CELLS, 128), BF16)
        for h in range(HEADS):
            half = h // 4 * 128
            lanes = iota((CELLS, 128), 1) >> 5
            own_lanes = jnp.where(lanes == h % 4, values[:, half : half + 128], 0.0).astype(BF16)
            rows = slice(h * CELLS, (h + 1) * CELLS)
            into[rows, half : half + 128] = own_lanes
            into[rows, 128 - half : 256 - half] = zeros

    every = region.at[pl.ds(0, 3)]
    pltpu.make_async_copy(every, every, halo_recv).wait()

    gain1 = gain1_ref[...]
    gain2 = gain2_ref[...]

    key_half = 30 + ((iota((CELLS, 1), 0) >> 4) & 1)
    lane_row = iota((1, WIDE), 1)
    marks = key_half == jnp.where(lane_row < 192, lane_row & 31, 0)
    pad_row = iota((HEAD_PAD, CELLS), 0)

    def own_columns(h):
        return slice(h * CELLS, (h + 1) * CELLS)

    def own_rows(h):
        return slice(h * HEAD_PAD, (h + 1) * HEAD_PAD)

    def window_row(wy, _):
        for wx in range(2):
            w = 2 * wy + wx
            for c in range(4):
                parts = [
                    region[2 * wy + s // 2, 2 * wx + s % 2, 16 * c : 16 * c + 16, :]
                    .astype(F32)
                    .reshape(2, 1, 8, CHANNELS)
                    for s in range(4)
                ]
                values = jnp.concatenate(parts, axis=1).reshape(64, CHANNELS)
                rows = slice(64 * c, 64 * c + 64)
                feats[wx, rows, :] = values
                unit, _ = norm_parts(values)
                normed[wx, rows, :] = (unit * gain1).astype(BF16)
        edge = lat == jnp.where(wy == 0, 0, n_lat - 1)
        floor = jnp.where(edge, NEGATIVE, 0.0)
        hidden = jnp.where(pad_row - 30 == 1 - query_half, floor, 0.0)
        hidden = jnp.where(pad_row >= 30, hidden, 0.0)
        for wx in range(2):
            queries = dot_nt(wt1[0:WIDE, :], normed[wx])
            for h in range(HEADS):
                qmt[wx, h] = head_rows((queries[own_rows(h), :] + hidden).astype(BF16), h)
            keys = dot_nt(normed[wx], wt1[WIDE : 2 * WIDE, :])
            kk[wx] = jnp.where(marks, 1.0, keys).astype(BF16)
            vt[wx] = dot_nt(wt1[2 * WIDE :, :], normed[wx]).astype(BF16)
        for wx in range(2):
            for h in range(HEADS):
                half = h // 4 * 128
                s1[wx, h] = dot(kk[wx, :, half : half + 128], qmt[wx, h])
        for wx in range(2):
            for h in range(HEADS):
                scores = s1.at[wx, h]
                peak = add_bias(scores, 32, 8, functools.partial(window_bias, h))
                inverse = raise_all(scores, 32, 8, peak, p1.at[wx], own_columns(h), False)
                inverse1[wx, h] = inverse
        for wx in range(2):
            for h in range(HEADS):
                rows = own_rows(h)
                heads_t = dot(vt[wx, rows, :], p1[wx, :, own_columns(h)])
                ot[wx, rows, :] = heads_t * inverse1[wx, h]
        for wx in range(2):
            heads_out = jnp.transpose(ot[wx]).astype(BF16)
            middle = feats[wx] + dot(heads_out, pp1[...])
            middles[2 * wy + wx] = middle.reshape(8, 2, 2, 8, CHANNELS)
        return 0

    ot[...] = jnp.zeros(ot.shape, F32)
    lax.fori_loop(0, 2, window_row, 0)

    y_runs = ((0, 0, 4, 8, 0), (0, 1, 0, 8, 4), (1, 0, 0, 8, 12), (1, 1, 0, 4, 20))
    for wy, sy, first, last, place in y_runs:
        for wx in range(2):
            for sx in range(2):
                start = (2 * wx + sx) * 8
                lin[place : place + last - first, start : start + 8, :] = middles[
                    2 * wy + wx, first:last, sy, sx
                ]

    def second_norm(step, _):
        for k in range(4):
            i = 4 * step + k
            lines, rows = pl.ds(2 * i, 2), pl.ds(pl.multiple_of(64 * i, 64), 64)
            unit, inverse = norm_parts(lin[lines].reshape(64, CHANNELS))
            units[rows, :] = unit
            inverses[rows, :] = inverse
            normal = (unit * gain2).astype(BF16).astype(F32)
            lin[lines] = normal.reshape(2, 32, CHANNELS)
        return 0

    lax.fori_loop(0, KEY_SIDE // 8, second_norm, 0)
    inside_low = jnp.where(lat > 0, 1.0, 0.0)
    inside_high = jnp.where(lat < n_lat - 1, 1.0, 0.0)
    lin[0:4] = lin[0:4] * inside_low
    lin[20:24] = lin[20:24] * inside_high
    keys_in = lin[:, 4:28, :].reshape(KEYS, CHANNELS).astype(BF16)
    k2[...] = dot_nt(keys_in, wt2[WIDE : 2 * WIDE, :]).astype(BF16)
    v2[...] = dot_nt(keys_in, wt2[2 * WIDE :, :]).astype(BF16)
    k2t[...] = dot_nt(wt2[WIDE : 2 * WIDE, :], keys_in).astype(BF16)

    def own_part(sy, sx):
        return slice(4 + 8 * sy, 12 + 8 * sy), slice(8 + 8 * sx, 16 + 8 * sx)

    own_second = jnp.concatenate(
        [lin[(*own_part(sy, sx), slice(None))].reshape(64, CHANNELS) for sy, sx, w, s in OWN],
        axis=0,
    )
    queries_in = dot(turn[0], own_second.astype(BF16)).astype(BF16)
    cot = cot_ref[...].astype(F32)
    cot_own = [
        cot[8 * sy : 8 * sy + 8, 8 * sx : 8 * sx + 8, :].reshape(64, CHANNELS)
        for sy, sx, w, s in OWN
    ]
    cot_in = dot(turn[0], jnp.concatenate(cot_own, axis=0).astype(BF16)).astype(BF16)
    queries_t = dot_nt(wt2[0:WIDE, :], queries_in).astype(BF16)
    gt[...] = dot_nt(pp2[...], cot_in)
    for h in range(HEADS):
        qmt[0, h] = head_rows(queries_t[h * HEAD_PAD : (h + 1) * HEAD_PAD, :], h)
    head_lanes(dot_nt(queries_in, wt2[0:WIDE, :]), qm)

    def cross_heads(group, _):
        heads = [3 * group + i for i in range(3)]

        def half(h):
            return pl.ds(pl.multiple_of(h // 4 * 128, 128), 128)

        def columns(h):
            return pl.ds(pl.multiple_of(h * CELLS, CELLS), CELLS)

        def rows(h):
            return pl.ds(pl.multiple_of(h * HEAD_PAD, HEAD_PAD), HEAD_PAD)

        def bias(h, c):
            return jnp.concatenate([cross_bias(h, 2 * c), cross_bias(h, 2 * c + 1)], axis=0)

        for i, h in enumerate(heads):
            s2[i] = dot(k2[:, half(h)], qmt[0, h])
        inverse = []
        for i, h in enumerate(heads):
            peak = add_bias(s2.at[i], 48, 12, functools.partial(bias, h))
            inverse.append(raise_all(s2.at[i], 48, 12, peak, p2, columns(h), True))
            scaled = gt[rows(h), :] * inverse[i]
            gt[rows(h), :] = scaled
            g2[i] = dot(v2[:, half(h)], head_block(scaled, h))
        for i, h in enumerate(heads):
            scores, grads = s2.at[i], g2.at[i]

            def raised(part):
                return scores[part, :]

            total = weigh_all(raised, grads, 48, 12, inverse[i])
            slope_all(raised, grads, 48, 12, total, scores, ds2, columns(h))
            for s in range(3):
                collect(acc2, h, s, KEY_SIDE, lambda m: (m * 3 + s) * 8, scores)
        for h in heads:
            ot[0, rows(h), :] = dot(k2t[rows(h), :], ds2[:, columns(h)])
        return 0

    lax.fori_loop(0, HEADS // 3, cross_heads, 0)
    head_lanes(jnp.transpose(gt[...]), dom)
    grad_queries = (jnp.transpose(ot[0]) * SCALE).astype(BF16)
    grad_keys = (dot(ds2[...], qm[...]) * SCALE).astype(BF16)
    grad_values = dot(p2[...], dom[...]).astype(BF16)
    grad_second = dot(grad_keys, wt2[WIDE : 2 * WIDE, :]) + dot(grad_values, wt2[2 * WIDE :, :])
    grad_own = dot(turn[1], dot(grad_queries, wt2[0:WIDE, :]).astype(BF16))

    lin[...] = jnp.zeros(lin.shape, F32)
    lin[:, 4:28, :] = grad_second.reshape(KEY_SIDE, KEY_SIDE, CHANNELS)
    lin[0:4] = lin[0:4] * inside_low
    lin[20:24] = lin[20:24] * inside_high
    for i, (sy, sx, w, s) in enumerate(OWN):
        place = (*own_part(sy, sx), slice(None))
        lin[place] = lin[place] + grad_own[64 * i : 64 * i + 64, :].reshape(8, 8, CHANNELS)

    def second_back(step, _):
        for k in range(4):
            i = 4 * step + k
            lines, rows = pl.ds(2 * i, 2), pl.ds(pl.multiple_of(64 * i, 64), 64)
            grad = lin[lines].reshape(64, CHANNELS)
            grad = norm_back(units[rows, :], inverses[rows, :], gain2, grad)
            lin[lines] = grad.reshape(2, 32, CHANNELS)
        return 0

    lax.fori_loop(0, KEY_SIDE // 8, second_back, 0)
    for i, (sy, sx, w, s) in enumerate(OWN):
        place = (*own_part(sy, sx), slice(None))
        lin[place] = lin[place] + cot_own[i].reshape(8, 8, CHANNELS)
    for w in range(3):
        rows, cols = 12 * (w // 2), 16 * (w % 2)
        piece = lin[rows : rows + 12, cols : cols + 16, :]
        mid_out[w] = piece.reshape(192, CHANNELS).astype(BF16)
        pltpu.make_async_remote_copy(
            src_ref=mid_out.at[w],
            dst_ref=mid_in.at[w],
            send_sem=mid_send,
            recv_sem=mid_recv,
            device_id=at(w // 2 - 1, w % 2 - 1),
            device_id_type=MESH,
        ).start()

    def sum_scatter(kind, tiles, buffer):
        chunks, depth = buffer_plan(tiles, n_lat)
        for c in range(chunks):

            @pl.when(lat != c)
            def _():
                pltpu.make_async_remote_copy(
                    src_ref=tiles.at[pl.ds(c * depth, depth)],
                    dst_ref=buffer.at[wrapped(lat - c, n_lat) - 1],
                    send_sem=sum_send.at[kind],
                    recv_sem=sum_recv.at[kind],
                    device_id=(lon, c),
                    device_id_type=MESH,
                ).start()

    def drain(sem, ref):
        pltpu.make_async_copy(ref, ref, sem).wait()

    def sum_spread(kind, tiles, buffer, rows):
        chunks, depth = buffer_plan(tiles, n_lat)

        @pl.when(lat < chunks)
        def _():
            drain(sum_recv.at[kind], buffer)
            total = tiles[pl.ds(lat * depth, depth)]
            for i in range(n_lat - 1):
                total = total + buffer[i]
            rows[spot] = total
            for j in range(1, inner):
                pltpu.make_async_remote_copy(
                    src_ref=rows.at[spot],
                    dst_ref=rows.at[spot],
                    send_sem=sum_send.at[kind + 1],
                    recv_sem=sum_recv.at[kind + 1],
                    device_id=inner_peer(j),
                    device_id_type=MESH,
                ).start()

    def sum_cross(kind, tiles, rows, far):
        chunks, depth = buffer_plan(tiles, n_lat)
        block = lax.div(lon, inner)

        @pl.when(lat < chunks)
        def _():
            drain(sum_recv.at[kind + 1], rows.at[pl.ds(0, inner - 1)])
            total = rows[0]
            for i in range(1, inner):
                total = total + rows[i]
            far[block] = total
            for j in range(1, outer):
                pltpu.make_async_remote_copy(
                    src_ref=far.at[block],
                    dst_ref=far.at[block],
                    send_sem=sum_send.at[kind + 2],
                    recv_sem=sum_recv.at[kind + 2],
                    device_id=at(0, j * inner),
                    device_id_type=MESH,
                ).start()

    def sum_gather(kind, tiles, far, result):
        chunks, depth = buffer_plan(tiles, n_lat)

        @pl.when(lat < chunks)
        def _():
            if outer > 1:
                drain(sum_recv.at[kind + 2], far.at[pl.ds(0, outer - 1)])
            total = far[0]
            for i in range(1, outer):
                total = total + far[i]
            result[lat] = total
            for j in range(1, n_lat):
                pltpu.make_async_remote_copy(
                    src_ref=result.at[lat],
                    dst_ref=result.at[lat],
                    send_sem=sum_send.at[kind + 3],
                    recv_sem=sum_recv.at[kind + 3],
                    device_id=at(j, 0),
                    device_id_type=MESH,
                ).start()

    def sum_end(kind, tiles, buffer, rows, far, result):
        chunks, depth = buffer_plan(tiles, n_lat)

        @pl.when(lat < chunks)
        def _():
            if chunks > 1:
                drain(sum_recv.at[kind + 3], result.at[pl.ds(0, chunks - 1)])
                drain(sum_send.at[kind], result.at[pl.ds(0, chunks - 1)])
            drain(sum_send.at[kind + 1], rows.at[pl.ds(0, inner - 1)])
            if outer > 1:
                drain(sum_send.at[kind + 2], far.at[pl.ds(0, outer - 1)])
            drain(sum_send.at[kind + 3], buffer)

        @pl.when(lat >= chunks)
        def _():
            drain(sum_recv.at[kind + 3], result)
            drain(sum_send.at[kind], result)

    def joined(result, count):
        chunks, depth = result.shape[0], result.shape[1]
        whole = jnp.concatenate(
            [result[c, d] for c in range(chunks) for d in range(depth)], axis=1
        )
        return whole[:, :count]

    def widened(part, width):
        return jnp.concatenate([part, jnp.zeros((8, width - part.shape[1]), F32)], axis=1)

    def gather_cross(pair, _):
        for i in range(2):
            h = 2 * pair + i
            for s in range(3):
                parts = [widened(acc2[s, r, h], LANES_C) for r in range(4)]
                flat2[s, pl.ds(h, 1), :] = gather_rows(parts, -1)
        return 0

    lax.fori_loop(0, HEADS // 2, gather_cross, 0)
    dense2[...] = jnp.zeros(dense2.shape, F32)
    for dy in range(CROSS):
        for s in range(3):
            start = dy * CROSS + 8 * s
            dense2[s, 0:HEADS, start : start + 23] = flat2[s, :, dy * 32 : dy * 32 + 23]
    for t in range(TILES_C):
        part = pl.ds(128 * t, 128)
        whole = dense2[0, :, part] + dense2[1, :, part] + dense2[2, :, part]
        tiles2[t] = whole[:HEADS]
    sum_scatter(0, tiles2, rs2)

    vv[...] = dot_nt(normed[1], wt1[2 * WIDE :, :]).astype(BF16)
    kt[...] = dot_nt(wt1[WIDE : 2 * WIDE, :], normed[1]).astype(BF16)
    head_lanes(dot_nt(normed[1], wt1[0:WIDE, :]), qm)

    drain(mid_recv, mid_in)
    total = lin[12:24, 16:32, :] + mid_in[2].astype(F32).reshape(12, 16, CHANNELS)
    below = (mid_in[0].astype(F32) + mid_in[1].astype(F32)).reshape(12, 16, CHANNELS)
    total = jnp.concatenate([total[0:4], total[4:12] + below[0:8], below[8:12]], axis=0)
    pair = [total[8 * sy : 8 * sy + 8].reshape(8, 1, 16, CHANNELS) for sy in range(2)]
    grad_mid[...] = jnp.concatenate(pair, axis=1).reshape(CELLS, CHANNELS)

    grads_t = dot_nt(pp1[...], grad_mid[...].astype(BF16))
    for h in range(HEADS):
        scaled = grads_t[own_rows(h), :] * inverse1[1, h]
        gt[own_rows(h), :] = scaled
        half = h // 4 * 128
        s1[1, h] = dot(vv[:, half : half + 128], head_rows(scaled.astype(BF16), h))
    for h in range(HEADS):

        def raised(part):
            return p1[1, part, own_columns(h)].astype(F32)

        total = weigh_all(raised, s1.at[1, h], 32, 8, inverse1[1, h])
        slope_all(raised, s1.at[1, h], 32, 8, total, s1.at[0, h], ds1, own_columns(h))
        for sx in range(2):

            def group_of(m):
                ky = 15 - m
                return (ky % 8 * 4 + ky // 8 * 2 + sx) * 8

            collect(acc1, h, sx, 16, group_of, s1.at[0, h])

    for h in range(HEADS):
        total = None
        for s in range(2):
            parts = [widened(acc1[s, r, h], LANES_W) for r in range(4)]
            piece = roll(gather_rows(parts, 1), 15 - 8 * s)
            total = piece if total is None else total + piece
        flat1[h : h + 1, :] = total
    dense1[...] = jnp.zeros(dense1.shape, F32)
    for dy in range(SPAN):
        dense1[0:HEADS, dy * SPAN : (dy + 1) * SPAN] = flat1[:, dy * 32 : dy * 32 + SPAN]
    for t in range(TILES_W):
        tiles1[t] = dense1[:HEADS, 128 * t : 128 * t + 128]
    sum_scatter(4, tiles1, rs1)
    sum_spread(0, tiles2, rs2, ag2)

    for h in range(HEADS):
        ot[0, own_rows(h), :] = dot(kt[own_rows(h), :], ds1[:, own_columns(h)])
    head_lanes(jnp.transpose(gt[...]), dom)
    grad_queries = (jnp.transpose(ot[0]) * SCALE).astype(BF16)
    grad_keys = (dot(ds1[...], qm[...]) * SCALE).astype(BF16)
    grad_values = dot(p1[1], dom[...])
    sum_spread(4, tiles1, rs1, ag1)
    sum_cross(0, tiles2, ag2, far2)
    grad_first[...] = (
        dot(grad_queries, wt1[0:WIDE, :])
        + dot(grad_keys, wt1[WIDE : 2 * WIDE, :])
        + dot(grad_values.astype(BF16), wt1[2 * WIDE :, :])
    )
    for c in range(4):
        rows = slice(64 * c, 64 * c + 64)
        unit, inverse = norm_parts(feats[1, rows, :])
        grad = grad_mid[rows, :] + norm_back(unit, inverse, gain1, grad_first[rows, :])
        quarters = grad.reshape(2, 2, 2, 8, CHANNELS)
        out_ref[8 + 2 * c : 10 + 2 * c, 8:16, :] = quarters[:, 0, 0]
        for s in (1, 2, 3):
            piece = quarters[:, s // 2, s % 2].reshape(16, CHANNELS)
            back_out[s - 1, 16 * c : 16 * c + 16, :] = piece.astype(BF16)
    for s in (1, 2, 3):
        pltpu.make_async_remote_copy(
            src_ref=back_out.at[s - 1],
            dst_ref=back_in.at[s - 1],
            send_sem=back_send,
            recv_sem=back_recv,
            device_id=at(s // 2, s % 2),
            device_id_type=MESH,
        ).start()
    sum_cross(4, tiles1, ag1, far1)
    sum_gather(0, tiles2, far2, fin2)
    drain(back_recv, back_in)
    out_ref[8:16, 0:8, :] = back_in[0].astype(F32).reshape(8, 8, CHANNELS)
    out_ref[0:8, 8:16, :] = back_in[1].astype(F32).reshape(8, 8, CHANNELS)
    out_ref[0:8, 0:8, :] = back_in[2].astype(F32).reshape(8, 8, CHANNELS)
    store = pltpu.make_async_copy(out_ref, out_hbm, load_sem.at[0])
    store.start()
    sum_gather(4, tiles1, far1, fin1)
    sum_end(0, tiles2, rs2, ag2, far2, fin2)
    out2_ref[...] = joined(fin2, CROSS * CROSS)
    store2 = pltpu.make_async_copy(out2_ref, out2_hbm, load_sem.at[1])
    store2.start()
    sum_end(4, tiles1, rs1, ag1, far1, fin1)
    out1_ref[...] = joined(fin1, SPAN * SPAN)
    store1 = pltpu.make_async_copy(out1_ref, out1_hbm, load_sem.at[2])
    store1.start()
    pltpu.make_async_copy(every, every, halo_send).wait()
    drain(mid_send, mid_out)
    drain(back_send, back_out)
    store.wait()
    store2.wait()
    store1.wait()


def lon_plan(n_lon):
    inner = 8 if n_lon % 8 == 0 else 2 if n_lon % 2 == 0 else n_lon
    return inner, n_lon // inner


def buffer_plan(tiles, n_lat):
    count = tiles.shape[0]
    chunks = min(n_lat, count)
    return chunks, count // chunks


def body(n_lat, n_lon, *operands):
    vmem = pltpu.VMEM
    inner, outer = lon_plan(n_lon)

    def sums(count):
        chunks = min(n_lat, count)
        depth = count // chunks
        return (
            vmem((count, HEADS, 128), F32),
            vmem((n_lat - 1, depth, HEADS, 128), F32),
            vmem((inner, depth, HEADS, 128), F32),
            vmem((outer, depth, HEADS, 128), F32),
            vmem((chunks, depth, HEADS, 128), F32),
        )

    tiles1, rs1, ag1, far1, fin1 = sums(TILES_W)
    tiles2, rs2, ag2, far2, fin2 = sums(TILES_C)
    scratch = [
        vmem((16, 16, CHANNELS), F32),
        vmem((HEADS, SPAN * SPAN), F32),
        vmem((HEADS, CROSS * CROSS), F32),
        vmem((16, 16, CHANNELS), BF16),
        vmem((16, 16, CHANNELS), BF16),
        vmem((1, CHANNELS), F32),
        vmem((CHANNELS, 3 * CHANNELS), BF16),
        vmem((CHANNELS, CHANNELS), BF16),
        vmem((HEADS, SPAN * SPAN), F32),
        vmem((1, CHANNELS), F32),
        vmem((CHANNELS, 3 * CHANNELS), BF16),
        vmem((CHANNELS, CHANNELS), BF16),
        vmem((HEADS, CROSS * CROSS), F32),
        pltpu.SemaphoreType.DMA((10,)),
        vmem((4, 4, 64, CHANNELS), BF16),
        vmem((HEADS, LANES_W), F32),
        vmem((3, HEADS, LANES_C), F32),
        vmem((3 * WIDE, CHANNELS), BF16),
        vmem((3 * WIDE, CHANNELS), BF16),
        vmem((WIDE, CHANNELS), BF16),
        vmem((WIDE, CHANNELS), BF16),
        vmem((2, CELLS, CELLS), BF16),
        vmem((2, 4, HEADS, 8, USED_W), F32),
        vmem((3, 4, HEADS, 8, USED_C), F32),
        vmem((2, 4, HEADS, 8, USED_W), F32),
        vmem((3, 4, HEADS, 8, USED_C), F32),
        vmem((2, CELLS, CHANNELS), F32),
        vmem((4, 8, 2, 2, 8, CHANNELS), F32),
        vmem((KEY_SIDE * 32, CHANNELS), F32),
        vmem((KEY_SIDE * 32, 1), F32),
        vmem((2, CELLS, WIDE), BF16),
        vmem((2, WIDE, CELLS), BF16),
        vmem((CELLS, WIDE), BF16),
        vmem((WIDE, CELLS), BF16),
        vmem((HEADS * CELLS, WIDE), BF16),
        vmem((HEADS * CELLS, WIDE), BF16),
        vmem((2, HEADS, 128, CELLS), BF16),
        vmem((WIDE, CELLS), F32),
        vmem((2, WIDE, CELLS), F32),
        vmem((2, CELLS, CHANNELS), BF16),
        vmem((2, HEADS, 1, CELLS), F32),
        vmem((2, HEADS, CELLS, CELLS), F32),
        vmem((3, KEYS, CELLS), F32),
        vmem((3, KEYS, CELLS), F32),
        vmem((CELLS, CHANNELS), F32),
        vmem((CELLS, CHANNELS), F32),
        vmem((2, CELLS, HEADS * CELLS), BF16),
        vmem((KEYS, HEADS * CELLS), BF16),
        vmem((CELLS, HEADS * CELLS), BF16),
        vmem((KEYS, HEADS * CELLS), BF16),
        vmem((KEYS, WIDE), BF16),
        vmem((KEYS, WIDE), BF16),
        vmem((WIDE, KEYS), BF16),
        vmem((KEY_SIDE, 32, CHANNELS), F32),
        vmem((3, 192, CHANNELS), BF16),
        vmem((3, 192, CHANNELS), BF16),
        vmem((3, 64, CHANNELS), BF16),
        vmem((3, 64, CHANNELS), BF16),
        vmem((8, 128 * TILES_W), F32),
        vmem((3, 8, 128 * TILES_C), F32),
        tiles1,
        tiles2,
        rs1,
        rs2,
        ag1,
        ag2,
        far1,
        far2,
        fin1,
        fin2,
        pltpu.SemaphoreType.DMA,
        pltpu.SemaphoreType.DMA,
        pltpu.SemaphoreType.DMA,
        pltpu.SemaphoreType.DMA,
        pltpu.SemaphoreType.DMA,
        pltpu.SemaphoreType.DMA,
        pltpu.SemaphoreType.DMA((8,)),
        pltpu.SemaphoreType.DMA((8,)),
    ]
    hbm = pl.BlockSpec(memory_space=pltpu.HBM)
    limit = 63 * 1024 * 1024
    shapes = (
        jax.ShapeDtypeStruct((16, 16, CHANNELS), F32),
        jax.ShapeDtypeStruct((HEADS, SPAN * SPAN), F32),
        jax.ShapeDtypeStruct((HEADS, CROSS * CROSS), F32),
    )
    results = pl.pallas_call(
        functools.partial(kernel, n_lat, n_lon),
        out_shape=shapes,
        in_specs=[hbm] * 10,
        out_specs=(hbm,) * 3,
        scratch_shapes=scratch,
        compiler_params=pltpu.CompilerParams(
            collective_id=0, has_side_effects=True, vmem_limit_bytes=limit
        ),
    )(*operands)
    return pl.pallas_call(
        hand_over,
        out_shape=shapes,
        in_specs=[hbm] * 3,
        out_specs=(hbm,) * 3,
        scratch_shapes=[pltpu.SemaphoreType.DMA((3,))],
        compiler_params=pltpu.CompilerParams(vmem_limit_bytes=limit),
    )(*results)


def hand_over(a, b, c, a_out, b_out, c_out, sems):
    copies = [
        pltpu.make_async_copy(src, dst, sems.at[i])
        for i, (src, dst) in enumerate(((a, a_out), (b, b_out), (c, c_out)))
    ]
    for copy in copies:
        copy.start()
    for copy in copies:
        copy.wait()


def solution(mesh):
    def local(
        features,
        cotangent,
        first_gain,
        window_qkv,
        window_proj,
        window_table,
        second_gain,
        cross_qkv,
        cross_proj,
        cross_table,
    ):
        return body(
            mesh.shape["lat"],
            mesh.shape["lon"],
            features,
            cotangent,
            first_gain.reshape(1, CHANNELS),
            window_qkv,
            window_proj,
            window_table,
            second_gain.reshape(1, CHANNELS),
            cross_qkv,
            cross_proj,
            cross_table,
        )

    return jax.shard_map(
        local,
        mesh=mesh,
        in_specs=(
            P("lat", "lon", None),
            P("lat", "lon", None),
            P(),
            P(),
            P(),
            P(),
            P(),
            P(),
            P(),
            P(),
        ),
        out_specs=(P("lat", "lon", None), P(), P()),
        check_vma=False,
    )
```

```python
import functools

import jax
import jax.numpy as jnp
from jax import lax
from jax.experimental import pallas as pl
from jax.experimental.pallas import tpu as pltpu
from jax.sharding import PartitionSpec as P

CHANNELS = 180
HEADS = 6
HEAD_SIZE = 30
HEAD_PAD = 32
WIDE = 256
CELLS = 256
KEYS = 576
KEY_SIDE = 24
SPAN = 31
CROSS = 39
EPSILON = 1e-05
NEGATIVE = -1e30
LOG2E = 1.4426950408889634
SCALE = HEAD_SIZE**-0.5
TILES_W = 8
TILES_C = 12
LANES_W = 1024
LANES_C = 1280
USED_W = 640
USED_C = 896
MESH = pl.DeviceIdType.MESH
F32 = jnp.float32
BF16 = jnp.bfloat16


def iota(shape, dim):
    return lax.broadcasted_iota(jnp.int32, shape, dim)


def dot(a, b):
    return jnp.dot(a, b, preferred_element_type=F32)


def dot_nt(a, b):
    return lax.dot_general(a, b, (((1,), (1,)), ((), ())), preferred_element_type=F32)


def one_hot(mask):
    return jnp.where(mask, 1.0, 0.0).astype(BF16)


def roll(x, shift):
    size = x.shape[-1]
    return pltpu.roll(x, shift % size, x.ndim - 1)


def norm_parts(values):
    centre = jnp.mean(values, axis=-1, keepdims=True)
    offset = values - centre
    spread = jnp.mean(offset * offset, axis=-1, keepdims=True)
    inverse = lax.rsqrt(spread + EPSILON)
    return offset * inverse, inverse


def norm_back(unit, inverse, gain, grads):
    scaled = grads * gain
    first = jnp.mean(scaled, axis=-1, keepdims=True)
    second = jnp.mean(scaled * unit, axis=-1, keepdims=True)
    return inverse * (scaled - first - unit * second)


OWN = [(sy, sx, 2 * sy + sx, (1 - sy) * 2 + (1 - sx)) for sy in (0, 1) for sx in (0, 1)]


def spread_rows(base, stride, ways):
    rows = iota(base.shape, 0)
    for bit in (1, 2, 4):
        base = jnp.where((rows & bit) != 0, roll(base, stride * bit), base)
    upper = (iota(base.shape, 1) & 16) != 0
    base = jnp.where(upper, roll(base, -240), base)
    return [base if r == 0 else roll(base, -32 * r) for r in range(ways)]


def gather_rows(parts, stride):
    total = parts[0]
    for r in range(1, len(parts)):
        total = total + roll(parts[r], 32 * r)
    upper = (iota(total.shape, 1) & 16) != 0
    total = jnp.where(upper, 0.0, total) + roll(jnp.where(upper, total, 0.0), 240)
    rows = iota(total.shape, 0)
    for bit in (1, 2, 4):
        total = jnp.where((rows & bit) != 0, roll(total, -stride * bit), total)
    return jnp.sum(total, axis=0, keepdims=True)


def kernel(
    n_lat,
    n_lon,
    feat_in,
    cot_in_hbm,
    gain1_in,
    qkv1_in,
    proj1_in,
    tab1_in,
    gain2_in,
    qkv2_in,
    proj2_in,
    tab2_in,
    out_hbm,
    out1_hbm,
    out2_hbm,
    out_ref,
    out1_ref,
    out2_ref,
    feat_ref,
    cot_ref,
    gain1_ref,
    qkv1_ref,
    proj1_ref,
    tab1_ref,
    gain2_ref,
    qkv2_ref,
    proj2_ref,
    tab2_ref,
    load_sem,
    region,
    flat1,
    flat2,
    wt1,
    wt2,
    pp1,
    pp2,
    turn,
    z1,
    z2,
    acc1,
    acc2,
    feats,
    middles,
    units,
    inverses,
    kk,
    vt,
    vv,
    kt,
    qm,
    dom,
    qmt,
    gt,
    ot,
    normed,
    inverse1,
    s1,
    s2,
    g2,
    grad_mid,
    grad_first,
    p1,
    p2,
    ds1,
    ds2,
    k2,
    v2,
    k2t,
    lin,
    mid_out,
    mid_in,
    back_out,
    back_in,
    dense1,
    dense2,
    tiles1,
    tiles2,
    rs1,
    rs2,
    ag1,
    ag2,
    far1,
    far2,
    fin1,
    fin2,
    halo_send,
    halo_recv,
    mid_send,
    mid_recv,
    back_send,
    back_recv,
    sum_send,
    sum_recv,
):
    lat = lax.axis_index("lat")
    lon = lax.axis_index("lon")

    def wrapped(value, count):
        value = jnp.where(value >= count, value - count, value)
        return jnp.where(value < 0, value + count, value)

    def at(dy, dx):
        return (wrapped(lon + dx, n_lon), wrapped(lat + dy, n_lat))

    loads = [
        pltpu.make_async_copy(src, dst, load_sem.at[i])
        for i, (src, dst) in enumerate(
            (
                (feat_in, feat_ref),
                (qkv1_in, qkv1_ref),
                (proj1_in, proj1_ref),
                (qkv2_in, qkv2_ref),
                (proj2_in, proj2_ref),
                (tab1_in, tab1_ref),
                (tab2_in, tab2_ref),
                (gain1_in, gain1_ref),
                (gain2_in, gain2_ref),
                (cot_in_hbm, cot_ref),
            )
        )
    ]
    for load in loads:
        load.start()

    barrier = pltpu.get_barrier_semaphore()

    def greet(dy, dx):
        pl.semaphore_signal(barrier, inc=1, device_id=at(dy, dx), device_id_type=MESH)

    for dy in (-1, 0, 1):
        for dx in (-1, 0, 1):
            if dy or dx:
                greet(dy, dx)
    for j in range(2, n_lat - 1):
        greet(j, 0)
    inner, outer = lon_plan(n_lon)
    spot = lax.rem(lon, inner)

    def inner_peer(j):
        return (lon - spot + wrapped(spot + j, inner), lat)

    def greet_at(device):
        pl.semaphore_signal(barrier, inc=1, device_id=device, device_id_type=MESH)

    for j in range(1, inner):
        greet_at(inner_peer(j))
    for j in range(1, outer):
        greet(0, j * inner)

    loads[0].wait()
    own = feat_ref[...].astype(F32)
    for sy, sx, w, s in OWN:
        quarter = own[8 * sy : 8 * sy + 8, 8 * sx : 8 * sx + 8, :].reshape(64, CHANNELS)
        region[1 + sy, 1 + sx, :, :CHANNELS] = quarter.astype(BF16)

    for load in loads[1:7]:
        load.wait()

    def pad_weights(i, _):
        lane = iota((WIDE, 1), 0)
        real = (lane < 192) & ((lane & 31) < HEAD_SIZE)
        source = jnp.where(real, CHANNELS * i + lane - 2 * (lane >> 5), -1)
        pick = one_hot(iota((WIDE, 3 * CHANNELS), 1) == source)
        rows = pl.ds(pl.multiple_of(i * WIDE, WIDE), WIDE)
        wt1[rows, :] = dot_nt(pick, qkv1_ref[...]).astype(BF16)
        wt2[rows, :] = dot_nt(pick, qkv2_ref[...]).astype(BF16)

        @pl.when(i == 0)
        def _():
            pick_proj = pick[:, :CHANNELS]
            pp1[...] = dot(pick_proj, proj1_ref[...]).astype(BF16)
            pp2[...] = dot(pick_proj, proj2_ref[...]).astype(BF16)

        return 0

    lax.fori_loop(0, 3, pad_weights, 0)

    pl.semaphore_wait(barrier, 8 + n_lat - 3 + inner - 1 + outer - 1)

    def side(step):
        here = {-1: 1, 0: pl.ds(1, 2), 1: 2}[step]
        there = {-1: 3, 0: pl.ds(1, 2), 1: 0}[step]
        return here, there

    for dy in (-1, 0, 1):
        for dx in (-1, 0, 1):
            if dy == 0 and dx == 0:
                continue
            (a, a_there), (b, b_there) = side(dy), side(dx)
            pltpu.make_async_remote_copy(
                src_ref=region.at[a, b],
                dst_ref=region.at[a_there, b_there],
                send_sem=halo_send,
                recv_sem=halo_recv,
                device_id=at(dy, dx),
                device_id_type=MESH,
            ).start()

    for load in loads[7:]:
        load.wait()

    def turned(c):
        r = 255 - c
        return ((r >> 3) & 7) * 32 + ((r >> 7) & 1) * 16 + ((r >> 6) & 1) * 8 + (r & 7)

    turn[0] = one_hot(iota((CELLS, CELLS), 0) == turned(iota((1, CELLS), 1)))
    turn[1] = one_hot(iota((CELLS, CELLS), 1) == turned(iota((CELLS, 1), 0)))

    flat1[...] = jnp.zeros(flat1.shape, F32)
    flat2[...] = jnp.zeros(flat2.shape, F32)
    for dy in range(SPAN):
        flat1[:, dy * 32 : dy * 32 + SPAN] = tab1_ref[:, dy * SPAN : (dy + 1) * SPAN]
    for dy in range(CROSS):
        for s in range(3):
            start = dy * CROSS + 8 * s
            flat2[s, :, dy * 32 : dy * 32 + 23] = tab2_ref[:, start : start + 23]
    def spread(pair, _):
        for i in range(2):
            h = 2 * pair + i
            row = pl.ds(h, 1)
            for s in range(2):
                base = jnp.broadcast_to(flat1[row, :] * LOG2E, (8, LANES_W))
                for r, part in enumerate(spread_rows(roll(base, 8 * s - 15), 1, 4)):
                    z1[s, r, h] = part[:, :USED_W]
            for s in range(3):
                base = jnp.broadcast_to(flat2[s, row, :] * LOG2E, (8, LANES_C))
                for r, part in enumerate(spread_rows(base, -1, 4)):
                    z2[s, r, h] = part[:, :USED_C]
        return 0

    lax.fori_loop(0, HEADS // 2, spread, 0)
    query_half = (iota((1, CELLS), 1) >> 4) & 1

    def window_bias(h, y8):
        pieces = []
        for sy in range(2):
            t, r = divmod(15 - (8 * sy + y8), 4)
            for sx in range(2):
                pieces.append(z1[sx, r, h, :, 128 * t : 128 * t + CELLS])
        return jnp.concatenate(pieces, axis=0)

    def cross_bias(h, ky):
        t, r = divmod(ky, 4)
        pieces = [z2[s, r, h, :, 128 * t : 128 * t + CELLS] for s in range(3)]
        return jnp.concatenate(pieces, axis=0)

    def by_eight(values):
        return values.reshape(values.shape[0] // 8, 8, CELLS)

    def add_bias(scores, step, count, bias):
        peak = None
        for c in range(count):
            rows = slice(c * step, (c + 1) * step)
            part = scores[rows, :] * (SCALE * LOG2E) + bias(c)
            scores[rows, :] = part
            part = jnp.max(by_eight(part), axis=0)
            peak = part if peak is None else jnp.maximum(peak, part)
        return jnp.max(peak, axis=0, keepdims=True)

    def raise_all(scores, step, count, peak, probs, columns, keep):
        total = None
        for c in range(count):
            rows = slice(c * step, (c + 1) * step)
            part = jnp.exp2(scores[rows, :] - peak)
            probs[rows, columns] = part.astype(BF16)
            if keep:
                scores[rows, :] = part
            part = jnp.sum(by_eight(part), axis=0)
            total = part if total is None else total + part
        return 1.0 / jnp.sum(total, axis=0, keepdims=True)

    def weigh_all(raised, grads, step, count, inverse):
        total = None
        for c in range(count):
            rows = slice(c * step, (c + 1) * step)
            part = raised(rows) * grads[rows, :]
            grads[rows, :] = part
            part = jnp.sum(by_eight(part), axis=0)
            total = part if total is None else total + part
        return jnp.sum(total, axis=0, keepdims=True) * inverse

    def slope_all(raised, grads, step, count, total, slopes, packed, columns):
        for c in range(count):
            rows = slice(c * step, (c + 1) * step)
            part = grads[rows, :] - raised(rows) * total
            slopes[rows, :] = part
            packed[rows, columns] = part.astype(BF16)

    def collect(acc, h, s, count, group_of, slopes):
        for r in range(4):
            for t in range(count // 4 + 1):
                parts = []
                if t < count // 4:
                    group = group_of(4 * t + r)
                    parts.append(slopes[group : group + 8, 0:128])
                if t > 0:
                    group = group_of(4 * t - 4 + r)
                    parts.append(slopes[group : group + 8, 128:256])
                acc[s, r, h, :, 128 * t : 128 * t + 128] = sum(parts[1:], parts[0])

    def head_rows(rows, h):
        before = h % 4 * HEAD_PAD
        pieces = [rows]
        if before:
            pieces = [jnp.zeros((before, CELLS), rows.dtype)] + pieces
        if before + HEAD_PAD < 128:
            pieces.append(jnp.zeros((128 - HEAD_PAD - before, CELLS), rows.dtype))
        return jnp.concatenate(pieces, axis=0) if len(pieces) > 1 else rows

    def head_block(rows, h):
        four = jnp.concatenate([rows] * 4, axis=0)
        return jnp.where((iota((128, CELLS), 0) >> 5) == lax.rem(h, 4), four, 0.0).astype(BF16)

    def head_lanes(values, into):
        zeros = jnp.zeros((CELLS, 128), BF16)
        for h in range(HEADS):
            half = h // 4 * 128
            lanes = iota((CELLS, 128), 1) >> 5
            own_lanes = jnp.where(lanes == h % 4, values[:, half : half + 128], 0.0).astype(BF16)
            rows = slice(h * CELLS, (h + 1) * CELLS)
            into[rows, half : half + 128] = own_lanes
            into[rows, 128 - half : 256 - half] = zeros

    every = region.at[pl.ds(0, 3)]
    pltpu.make_async_copy(every, every, halo_recv).wait()

    gain1 = gain1_ref[...]
    gain2 = gain2_ref[...]

    key_half = 30 + ((iota((CELLS, 1), 0) >> 4) & 1)
    lane_row = iota((1, WIDE), 1)
    marks = key_half == jnp.where(lane_row < 192, lane_row & 31, 0)
    pad_row = iota((HEAD_PAD, CELLS), 0)

    def own_columns(h):
        return slice(h * CELLS, (h + 1) * CELLS)

    def own_rows(h):
        return slice(h * HEAD_PAD, (h + 1) * HEAD_PAD)

    def window_row(wy, _):
        for wx in range(2):
            w = 2 * wy + wx
            for c in range(4):
                parts = [
                    region[2 * wy + s // 2, 2 * wx + s % 2, 16 * c : 16 * c + 16, :CHANNELS]
                    .astype(F32)
                    .reshape(2, 1, 8, CHANNELS)
                    for s in range(4)
                ]
                values = jnp.concatenate(parts, axis=1).reshape(64, CHANNELS)
                rows = slice(64 * c, 64 * c + 64)
                feats[wx, rows, :] = values
                unit, _ = norm_parts(values)
                normed[wx, rows, :] = (unit * gain1).astype(BF16)
        edge = lat == jnp.where(wy == 0, 0, n_lat - 1)
        floor = jnp.where(edge, NEGATIVE, 0.0)
        hidden = jnp.where(pad_row - 30 == 1 - query_half, floor, 0.0)
        hidden = jnp.where(pad_row >= 30, hidden, 0.0)
        for wx in range(2):
            queries = dot_nt(wt1[0:WIDE, :], normed[wx])
            for h in range(HEADS):
                qmt[wx, h] = head_rows((queries[own_rows(h), :] + hidden).astype(BF16), h)
            keys = dot_nt(normed[wx], wt1[WIDE : 2 * WIDE, :])
            kk[wx] = jnp.where(marks, 1.0, keys).astype(BF16)
            vt[wx] = dot_nt(wt1[2 * WIDE :, :], normed[wx]).astype(BF16)
        for wx in range(2):
            for h in range(HEADS):
                half = h // 4 * 128
                s1[wx, h] = dot(kk[wx, :, half : half + 128], qmt[wx, h])
        for wx in range(2):
            for h in range(HEADS):
                scores = s1.at[wx, h]
                peak = add_bias(scores, 32, 8, functools.partial(window_bias, h))
                inverse = raise_all(scores, 32, 8, peak, p1.at[wx], own_columns(h), False)
                inverse1[wx, h] = inverse
        for wx in range(2):
            for h in range(HEADS):
                rows = own_rows(h)
                heads_t = dot(vt[wx, rows, :], p1[wx, :, own_columns(h)])
                ot[wx, rows, :] = heads_t * inverse1[wx, h]
        for wx in range(2):
            heads_out = jnp.transpose(ot[wx]).astype(BF16)
            middle = feats[wx] + dot(heads_out, pp1[...])
            middles[2 * wy + wx] = middle.reshape(8, 2, 2, 8, CHANNELS)
        return 0

    ot[...] = jnp.zeros(ot.shape, F32)
    lax.fori_loop(0, 2, window_row, 0)

    y_runs = ((0, 0, 4, 8, 0), (0, 1, 0, 8, 4), (1, 0, 0, 8, 12), (1, 1, 0, 4, 20))
    for wy, sy, first, last, place in y_runs:
        for wx in range(2):
            for sx in range(2):
                start = (2 * wx + sx) * 8
                lin[place : place + last - first, start : start + 8, :] = middles[
                    2 * wy + wx, first:last, sy, sx
                ]

    def second_norm(step, _):
        for k in range(4):
            i = 4 * step + k
            lines, rows = pl.ds(2 * i, 2), pl.ds(pl.multiple_of(64 * i, 64), 64)
            unit, inverse = norm_parts(lin[lines].reshape(64, CHANNELS))
            units[rows, :] = unit
            inverses[rows, :] = inverse
            normal = (unit * gain2).astype(BF16).astype(F32)
            lin[lines] = normal.reshape(2, 32, CHANNELS)
        return 0

    lax.fori_loop(0, KEY_SIDE // 8, second_norm, 0)
    inside_low = jnp.where(lat > 0, 1.0, 0.0)
    inside_high = jnp.where(lat < n_lat - 1, 1.0, 0.0)
    lin[0:4] = lin[0:4] * inside_low
    lin[20:24] = lin[20:24] * inside_high
    keys_in = lin[:, 4:28, :].reshape(KEYS, CHANNELS).astype(BF16)
    k2[...] = dot_nt(keys_in, wt2[WIDE : 2 * WIDE, :]).astype(BF16)
    v2[...] = dot_nt(keys_in, wt2[2 * WIDE :, :]).astype(BF16)
    k2t[...] = dot_nt(wt2[WIDE : 2 * WIDE, :], keys_in).astype(BF16)

    def own_part(sy, sx):
        return slice(4 + 8 * sy, 12 + 8 * sy), slice(8 + 8 * sx, 16 + 8 * sx)

    own_second = jnp.concatenate(
        [lin[(*own_part(sy, sx), slice(None))].reshape(64, CHANNELS) for sy, sx, w, s in OWN],
        axis=0,
    )
    queries_in = dot(turn[0], own_second.astype(BF16)).astype(BF16)
    cot = cot_ref[...].astype(F32)
    cot_own = [
        cot[8 * sy : 8 * sy + 8, 8 * sx : 8 * sx + 8, :].reshape(64, CHANNELS)
        for sy, sx, w, s in OWN
    ]
    cot_in = dot(turn[0], jnp.concatenate(cot_own, axis=0).astype(BF16)).astype(BF16)
    queries_t = dot_nt(wt2[0:WIDE, :], queries_in).astype(BF16)
    gt[...] = dot_nt(pp2[...], cot_in)
    for h in range(HEADS):
        qmt[0, h] = head_rows(queries_t[h * HEAD_PAD : (h + 1) * HEAD_PAD, :], h)
    head_lanes(dot_nt(queries_in, wt2[0:WIDE, :]), qm)

    def cross_heads(group, _):
        heads = [3 * group + i for i in range(3)]

        def half(h):
            return pl.ds(pl.multiple_of(h // 4 * 128, 128), 128)

        def columns(h):
            return pl.ds(pl.multiple_of(h * CELLS, CELLS), CELLS)

        def rows(h):
            return pl.ds(pl.multiple_of(h * HEAD_PAD, HEAD_PAD), HEAD_PAD)

        def bias(h, c):
            return jnp.concatenate([cross_bias(h, 2 * c), cross_bias(h, 2 * c + 1)], axis=0)

        for i, h in enumerate(heads):
            s2[i] = dot(k2[:, half(h)], qmt[0, h])
        inverse = []
        for i, h in enumerate(heads):
            peak = add_bias(s2.at[i], 48, 12, functools.partial(bias, h))
            inverse.append(raise_all(s2.at[i], 48, 12, peak, p2, columns(h), True))
            scaled = gt[rows(h), :] * inverse[i]
            gt[rows(h), :] = scaled
            g2[i] = dot(v2[:, half(h)], head_block(scaled, h))
        for i, h in enumerate(heads):
            scores, grads = s2.at[i], g2.at[i]

            def raised(part):
                return scores[part, :]

            total = weigh_all(raised, grads, 48, 12, inverse[i])
            slope_all(raised, grads, 48, 12, total, scores, ds2, columns(h))
            for s in range(3):
                collect(acc2, h, s, KEY_SIDE, lambda m: (m * 3 + s) * 8, scores)
        for h in heads:
            ot[0, rows(h), :] = dot(k2t[rows(h), :], ds2[:, columns(h)])
        return 0

    lax.fori_loop(0, HEADS // 3, cross_heads, 0)
    head_lanes(jnp.transpose(gt[...]), dom)
    grad_queries = (jnp.transpose(ot[0]) * SCALE).astype(BF16)
    grad_keys = (dot(ds2[...], qm[...]) * SCALE).astype(BF16)
    grad_values = dot(p2[...], dom[...]).astype(BF16)
    grad_second = dot(grad_keys, wt2[WIDE : 2 * WIDE, :]) + dot(grad_values, wt2[2 * WIDE :, :])
    grad_own = dot(turn[1], dot(grad_queries, wt2[0:WIDE, :]).astype(BF16))

    lin[...] = jnp.zeros(lin.shape, F32)
    lin[:, 4:28, :] = grad_second.reshape(KEY_SIDE, KEY_SIDE, CHANNELS)
    lin[0:4] = lin[0:4] * inside_low
    lin[20:24] = lin[20:24] * inside_high
    for i, (sy, sx, w, s) in enumerate(OWN):
        place = (*own_part(sy, sx), slice(None))
        lin[place] = lin[place] + grad_own[64 * i : 64 * i + 64, :].reshape(8, 8, CHANNELS)

    def second_back(step, _):
        for k in range(4):
            i = 4 * step + k
            lines, rows = pl.ds(2 * i, 2), pl.ds(pl.multiple_of(64 * i, 64), 64)
            grad = lin[lines].reshape(64, CHANNELS)
            grad = norm_back(units[rows, :], inverses[rows, :], gain2, grad)
            lin[lines] = grad.reshape(2, 32, CHANNELS)
        return 0

    lax.fori_loop(0, KEY_SIDE // 8, second_back, 0)
    for i, (sy, sx, w, s) in enumerate(OWN):
        place = (*own_part(sy, sx), slice(None))
        lin[place] = lin[place] + cot_own[i].reshape(8, 8, CHANNELS)
    for w in range(3):
        rows, cols = 12 * (w // 2), 16 * (w % 2)
        piece = lin[rows : rows + 12, cols : cols + 16, :]
        mid_out[w, :, :CHANNELS] = piece.reshape(192, CHANNELS).astype(BF16)
        pltpu.make_async_remote_copy(
            src_ref=mid_out.at[w],
            dst_ref=mid_in.at[w],
            send_sem=mid_send,
            recv_sem=mid_recv,
            device_id=at(w // 2 - 1, w % 2 - 1),
            device_id_type=MESH,
        ).start()

    def sum_scatter(kind, tiles, buffer):
        chunks, depth = buffer_plan(tiles, n_lat)
        for c in range(chunks):

            @pl.when(lat != c)
            def _():
                pltpu.make_async_remote_copy(
                    src_ref=tiles.at[pl.ds(c * depth, depth)],
                    dst_ref=buffer.at[wrapped(lat - c, n_lat) - 1],
                    send_sem=sum_send.at[kind],
                    recv_sem=sum_recv.at[kind],
                    device_id=(lon, c),
                    device_id_type=MESH,
                ).start()

    def drain(sem, ref):
        pltpu.make_async_copy(ref, ref, sem).wait()

    def sum_spread(kind, tiles, buffer, rows):
        chunks, depth = buffer_plan(tiles, n_lat)

        @pl.when(lat < chunks)
        def _():
            drain(sum_recv.at[kind], buffer)
            total = tiles[pl.ds(lat * depth, depth)]
            for i in range(n_lat - 1):
                total = total + buffer[i]
            rows[spot] = total
            for j in range(1, inner):
                pltpu.make_async_remote_copy(
                    src_ref=rows.at[spot],
                    dst_ref=rows.at[spot],
                    send_sem=sum_send.at[kind + 1],
                    recv_sem=sum_recv.at[kind + 1],
                    device_id=inner_peer(j),
                    device_id_type=MESH,
                ).start()

    def sum_cross(kind, tiles, rows, far):
        chunks, depth = buffer_plan(tiles, n_lat)
        block = lax.div(lon, inner)

        @pl.when(lat < chunks)
        def _():
            drain(sum_recv.at[kind + 1], rows.at[pl.ds(0, inner - 1)])
            total = rows[0]
            for i in range(1, inner):
                total = total + rows[i]
            far[block] = total
            for j in range(1, outer):
                pltpu.make_async_remote_copy(
                    src_ref=far.at[block],
                    dst_ref=far.at[block],
                    send_sem=sum_send.at[kind + 2],
                    recv_sem=sum_recv.at[kind + 2],
                    device_id=at(0, j * inner),
                    device_id_type=MESH,
                ).start()

    def sum_gather(kind, tiles, far, result):
        chunks, depth = buffer_plan(tiles, n_lat)

        @pl.when(lat < chunks)
        def _():
            if outer > 1:
                drain(sum_recv.at[kind + 2], far.at[pl.ds(0, outer - 1)])
            total = far[0]
            for i in range(1, outer):
                total = total + far[i]
            result[lat] = total
            for j in range(1, n_lat):
                pltpu.make_async_remote_copy(
                    src_ref=result.at[lat],
                    dst_ref=result.at[lat],
                    send_sem=sum_send.at[kind + 3],
                    recv_sem=sum_recv.at[kind + 3],
                    device_id=at(j, 0),
                    device_id_type=MESH,
                ).start()

    def sum_end(kind, tiles, buffer, rows, far, result):
        chunks, depth = buffer_plan(tiles, n_lat)

        @pl.when(lat < chunks)
        def _():
            if chunks > 1:
                drain(sum_recv.at[kind + 3], result.at[pl.ds(0, chunks - 1)])
                drain(sum_send.at[kind], result.at[pl.ds(0, chunks - 1)])
            drain(sum_send.at[kind + 1], rows.at[pl.ds(0, inner - 1)])
            if outer > 1:
                drain(sum_send.at[kind + 2], far.at[pl.ds(0, outer - 1)])
            drain(sum_send.at[kind + 3], buffer)

        @pl.when(lat >= chunks)
        def _():
            drain(sum_recv.at[kind + 3], result)
            drain(sum_send.at[kind], result)

    def joined(result):
        chunks, depth = result.shape[0], result.shape[1]
        return jnp.concatenate(
            [result[c, d] for c in range(chunks) for d in range(depth)], axis=1
        )

    def widened(part, width):
        return jnp.concatenate([part, jnp.zeros((8, width - part.shape[1]), F32)], axis=1)

    def gather_cross(pair, _):
        for i in range(2):
            h = 2 * pair + i
            for s in range(3):
                parts = [widened(acc2[s, r, h], LANES_C) for r in range(4)]
                flat2[s, pl.ds(h, 1), :] = gather_rows(parts, -1)
        return 0

    lax.fori_loop(0, HEADS // 2, gather_cross, 0)
    dense2[...] = jnp.zeros(dense2.shape, F32)
    for dy in range(CROSS):
        for s in range(3):
            start = dy * CROSS + 8 * s
            dense2[s, 0:HEADS, start : start + 23] = flat2[s, :, dy * 32 : dy * 32 + 23]
    for t in range(TILES_C):
        part = pl.ds(128 * t, 128)
        whole = dense2[0, :, part] + dense2[1, :, part] + dense2[2, :, part]
        tiles2[t] = whole
    sum_scatter(0, tiles2, rs2)

    vv[...] = dot_nt(normed[1], wt1[2 * WIDE :, :]).astype(BF16)
    kt[...] = dot_nt(wt1[WIDE : 2 * WIDE, :], normed[1]).astype(BF16)
    head_lanes(dot_nt(normed[1], wt1[0:WIDE, :]), qm)

    drain(mid_recv, mid_in)
    total = lin[12:24, 16:32, :] + mid_in[2, :, :CHANNELS].astype(F32).reshape(12, 16, CHANNELS)
    below = (mid_in[0, :, :CHANNELS].astype(F32) + mid_in[1, :, :CHANNELS].astype(F32)).reshape(12, 16, CHANNELS)
    total = jnp.concatenate([total[0:4], total[4:12] + below[0:8], below[8:12]], axis=0)
    pair = [total[8 * sy : 8 * sy + 8].reshape(8, 1, 16, CHANNELS) for sy in range(2)]
    grad_mid[...] = jnp.concatenate(pair, axis=1).reshape(CELLS, CHANNELS)

    grads_t = dot_nt(pp1[...], grad_mid[...].astype(BF16))
    for h in range(HEADS):
        scaled = grads_t[own_rows(h), :] * inverse1[1, h]
        gt[own_rows(h), :] = scaled
        half = h // 4 * 128
        s1[1, h] = dot(vv[:, half : half + 128], head_rows(scaled.astype(BF16), h))
    for h in range(HEADS):

        def raised(part):
            return p1[1, part, own_columns(h)].astype(F32)

        total = weigh_all(raised, s1.at[1, h], 32, 8, inverse1[1, h])
        slope_all(raised, s1.at[1, h], 32, 8, total, s1.at[0, h], ds1, own_columns(h))
        for sx in range(2):

            def group_of(m):
                ky = 15 - m
                return (ky % 8 * 4 + ky // 8 * 2 + sx) * 8

            collect(acc1, h, sx, 16, group_of, s1.at[0, h])

    for h in range(HEADS):
        total = None
        for s in range(2):
            parts = [widened(acc1[s, r, h], LANES_W) for r in range(4)]
            piece = roll(gather_rows(parts, 1), 15 - 8 * s)
            total = piece if total is None else total + piece
        flat1[h : h + 1, :] = total
    dense1[...] = jnp.zeros(dense1.shape, F32)
    for dy in range(SPAN):
        dense1[0:HEADS, dy * SPAN : (dy + 1) * SPAN] = flat1[:, dy * 32 : dy * 32 + SPAN]
    for t in range(TILES_W):
        tiles1[t] = dense1[:, 128 * t : 128 * t + 128]
    sum_scatter(4, tiles1, rs1)
    sum_spread(0, tiles2, rs2, ag2)

    for h in range(HEADS):
        ot[0, own_rows(h), :] = dot(kt[own_rows(h), :], ds1[:, own_columns(h)])
    head_lanes(jnp.transpose(gt[...]), dom)
    grad_queries = (jnp.transpose(ot[0]) * SCALE).astype(BF16)
    grad_keys = (dot(ds1[...], qm[...]) * SCALE).astype(BF16)
    grad_values = dot(p1[1], dom[...])
    sum_spread(4, tiles1, rs1, ag1)
    sum_cross(0, tiles2, ag2, far2)
    grad_first[...] = (
        dot(grad_queries, wt1[0:WIDE, :])
        + dot(grad_keys, wt1[WIDE : 2 * WIDE, :])
        + dot(grad_values.astype(BF16), wt1[2 * WIDE :, :])
    )
    for c in range(4):
        rows = slice(64 * c, 64 * c + 64)
        unit, inverse = norm_parts(feats[1, rows, :])
        grad = grad_mid[rows, :] + norm_back(unit, inverse, gain1, grad_first[rows, :])
        quarters = grad.reshape(2, 2, 2, 8, CHANNELS)
        out_ref[8 + 2 * c : 10 + 2 * c, 8:16, :CHANNELS] = quarters[:, 0, 0]
        for s in (1, 2, 3):
            piece = quarters[:, s // 2, s % 2].reshape(16, CHANNELS)
            back_out[s - 1, 16 * c : 16 * c + 16, :CHANNELS] = piece.astype(BF16)
    for s in (1, 2, 3):
        pltpu.make_async_remote_copy(
            src_ref=back_out.at[s - 1],
            dst_ref=back_in.at[s - 1],
            send_sem=back_send,
            recv_sem=back_recv,
            device_id=at(s // 2, s % 2),
            device_id_type=MESH,
        ).start()
    sum_cross(4, tiles1, ag1, far1)
    sum_gather(0, tiles2, far2, fin2)
    drain(back_recv, back_in)
    out_ref[8:16, 0:8, :CHANNELS] = back_in[0, :, :CHANNELS].astype(F32).reshape(8, 8, CHANNELS)
    out_ref[0:8, 8:16, :CHANNELS] = back_in[1, :, :CHANNELS].astype(F32).reshape(8, 8, CHANNELS)
    out_ref[0:8, 0:8, :CHANNELS] = back_in[2, :, :CHANNELS].astype(F32).reshape(8, 8, CHANNELS)
    store = pltpu.make_async_copy(out_ref, out_hbm, load_sem.at[0])
    store.start()
    sum_gather(4, tiles1, far1, fin1)
    sum_end(0, tiles2, rs2, ag2, far2, fin2)
    out2_ref[...] = joined(fin2)
    store2 = pltpu.make_async_copy(out2_ref, out2_hbm, load_sem.at[1])
    store2.start()
    sum_end(4, tiles1, rs1, ag1, far1, fin1)
    out1_ref[...] = joined(fin1)
    store1 = pltpu.make_async_copy(out1_ref, out1_hbm, load_sem.at[2])
    store1.start()
    pltpu.make_async_copy(every, every, halo_send).wait()
    drain(mid_send, mid_out)
    drain(back_send, back_out)
    store.wait()
    store2.wait()
    store1.wait()


def lon_plan(n_lon):
    inner = 8 if n_lon % 8 == 0 else 2 if n_lon % 2 == 0 else n_lon
    return inner, n_lon // inner


def buffer_plan(tiles, n_lat):
    count = tiles.shape[0]
    chunks = min(n_lat, count)
    return chunks, count // chunks


def body(n_lat, n_lon, *operands):
    vmem = pltpu.VMEM
    inner, outer = lon_plan(n_lon)

    def sums(count):
        chunks = min(n_lat, count)
        depth = count // chunks
        return (
            vmem((count, 8, 128), F32),
            vmem((n_lat - 1, depth, 8, 128), F32),
            vmem((inner, depth, 8, 128), F32),
            vmem((outer, depth, 8, 128), F32),
            vmem((chunks, depth, 8, 128), F32),
        )

    tiles1, rs1, ag1, far1, fin1 = sums(TILES_W)
    tiles2, rs2, ag2, far2, fin2 = sums(TILES_C)
    scratch = [
        vmem((16, 16, WIDE), F32),
        vmem((8, 128 * TILES_W), F32),
        vmem((8, 128 * TILES_C), F32),
        vmem((16, 16, CHANNELS), BF16),
        vmem((16, 16, CHANNELS), BF16),
        vmem((1, CHANNELS), F32),
        vmem((CHANNELS, 3 * CHANNELS), BF16),
        vmem((CHANNELS, CHANNELS), BF16),
        vmem((HEADS, SPAN * SPAN), F32),
        vmem((1, CHANNELS), F32),
        vmem((CHANNELS, 3 * CHANNELS), BF16),
        vmem((CHANNELS, CHANNELS), BF16),
        vmem((HEADS, CROSS * CROSS), F32),
        pltpu.SemaphoreType.DMA((10,)),
        vmem((4, 4, 64, WIDE), BF16),
        vmem((HEADS, LANES_W), F32),
        vmem((3, HEADS, LANES_C), F32),
        vmem((3 * WIDE, CHANNELS), BF16),
        vmem((3 * WIDE, CHANNELS), BF16),
        vmem((WIDE, CHANNELS), BF16),
        vmem((WIDE, CHANNELS), BF16),
        vmem((2, CELLS, CELLS), BF16),
        vmem((2, 4, HEADS, 8, USED_W), F32),
        vmem((3, 4, HEADS, 8, USED_C), F32),
        vmem((2, 4, HEADS, 8, USED_W), F32),
        vmem((3, 4, HEADS, 8, USED_C), F32),
        vmem((2, CELLS, CHANNELS), F32),
        vmem((4, 8, 2, 2, 8, CHANNELS), F32),
        vmem((KEY_SIDE * 32, CHANNELS), F32),
        vmem((KEY_SIDE * 32, 1), F32),
        vmem((2, CELLS, WIDE), BF16),
        vmem((2, WIDE, CELLS), BF16),
        vmem((CELLS, WIDE), BF16),
        vmem((WIDE, CELLS), BF16),
        vmem((HEADS * CELLS, WIDE), BF16),
        vmem((HEADS * CELLS, WIDE), BF16),
        vmem((2, HEADS, 128, CELLS), BF16),
        vmem((WIDE, CELLS), F32),
        vmem((2, WIDE, CELLS), F32),
        vmem((2, CELLS, CHANNELS), BF16),
        vmem((2, HEADS, 1, CELLS), F32),
        vmem((2, HEADS, CELLS, CELLS), F32),
        vmem((3, KEYS, CELLS), F32),
        vmem((3, KEYS, CELLS), F32),
        vmem((CELLS, CHANNELS), F32),
        vmem((CELLS, CHANNELS), F32),
        vmem((2, CELLS, HEADS * CELLS), BF16),
        vmem((KEYS, HEADS * CELLS), BF16),
        vmem((CELLS, HEADS * CELLS), BF16),
        vmem((KEYS, HEADS * CELLS), BF16),
        vmem((KEYS, WIDE), BF16),
        vmem((KEYS, WIDE), BF16),
        vmem((WIDE, KEYS), BF16),
        vmem((KEY_SIDE, 32, CHANNELS), F32),
        vmem((3, 192, WIDE), BF16),
        vmem((3, 192, WIDE), BF16),
        vmem((3, 64, WIDE), BF16),
        vmem((3, 64, WIDE), BF16),
        vmem((8, 128 * TILES_W), F32),
        vmem((3, 8, 128 * TILES_C), F32),
        tiles1,
        tiles2,
        rs1,
        rs2,
        ag1,
        ag2,
        far1,
        far2,
        fin1,
        fin2,
        pltpu.SemaphoreType.DMA,
        pltpu.SemaphoreType.DMA,
        pltpu.SemaphoreType.DMA,
        pltpu.SemaphoreType.DMA,
        pltpu.SemaphoreType.DMA,
        pltpu.SemaphoreType.DMA,
        pltpu.SemaphoreType.DMA((8,)),
        pltpu.SemaphoreType.DMA((8,)),
    ]
    hbm = pl.BlockSpec(memory_space=pltpu.HBM)
    limit = 63 * 1024 * 1024
    shapes = (
        jax.ShapeDtypeStruct((16, 16, WIDE), F32),
        jax.ShapeDtypeStruct((8, 128 * TILES_W), F32),
        jax.ShapeDtypeStruct((8, 128 * TILES_C), F32),
    )
    grads, grad1, grad2 = pl.pallas_call(
        functools.partial(kernel, n_lat, n_lon),
        out_shape=shapes,
        in_specs=[hbm] * 10,
        out_specs=(hbm,) * 3,
        scratch_shapes=scratch,
        compiler_params=pltpu.CompilerParams(
            collective_id=0, has_side_effects=True, vmem_limit_bytes=limit
        ),
    )(*operands)
    return (
        grads[:, :, :CHANNELS],
        grad1[:HEADS, : SPAN * SPAN],
        grad2[:HEADS, : CROSS * CROSS],
    )


def solution(mesh):
    def local(
        features,
        cotangent,
        first_gain,
        window_qkv,
        window_proj,
        window_table,
        second_gain,
        cross_qkv,
        cross_proj,
        cross_table,
    ):
        return body(
            mesh.shape["lat"],
            mesh.shape["lon"],
            features,
            cotangent,
            first_gain.reshape(1, CHANNELS),
            window_qkv,
            window_proj,
            window_table,
            second_gain.reshape(1, CHANNELS),
            cross_qkv,
            cross_proj,
            cross_table,
        )

    return jax.shard_map(
        local,
        mesh=mesh,
        in_specs=(
            P("lat", "lon", None),
            P("lat", "lon", None),
            P(),
            P(),
            P(),
            P(),
            P(),
            P(),
            P(),
            P(),
        ),
        out_specs=(P("lat", "lon", None), P(), P()),
        check_vma=False,
    )
```

```python
import functools

import jax
import jax.numpy as jnp
from jax import lax
from jax.experimental import pallas as pl
from jax.experimental.pallas import tpu as pltpu
from jax.sharding import PartitionSpec as P

CHANNELS = 180
HEADS = 6
HEAD_SIZE = 30
HEAD_PAD = 32
WIDE = 256
CELLS = 256
KEYS = 576
KEY_SIDE = 24
SPAN = 31
CROSS = 39
EPSILON = 1e-05
NEGATIVE = -1e30
LOG2E = 1.4426950408889634
SCALE = HEAD_SIZE**-0.5
TILES_W = 8
TILES_C = 12
LANES_W = 1024
LANES_C = 1280
USED_W = 640
USED_C = 896
MESH = pl.DeviceIdType.MESH
F32 = jnp.float32
BF16 = jnp.bfloat16


def iota(shape, dim):
    return lax.broadcasted_iota(jnp.int32, shape, dim)


def dot(a, b):
    return jnp.dot(a, b, preferred_element_type=F32)


def dot_nt(a, b):
    return lax.dot_general(a, b, (((1,), (1,)), ((), ())), preferred_element_type=F32)


def one_hot(mask):
    return jnp.where(mask, 1.0, 0.0).astype(BF16)


def roll(x, shift):
    size = x.shape[-1]
    return pltpu.roll(x, shift % size, x.ndim - 1)


def norm_parts(values):
    centre = jnp.mean(values, axis=-1, keepdims=True)
    offset = values - centre
    spread = jnp.mean(offset * offset, axis=-1, keepdims=True)
    inverse = lax.rsqrt(spread + EPSILON)
    return offset * inverse, inverse


def norm_back(unit, inverse, gain, grads):
    scaled = grads * gain
    first = jnp.mean(scaled, axis=-1, keepdims=True)
    second = jnp.mean(scaled * unit, axis=-1, keepdims=True)
    return inverse * (scaled - first - unit * second)


OWN = [(sy, sx, 2 * sy + sx, (1 - sy) * 2 + (1 - sx)) for sy in (0, 1) for sx in (0, 1)]


def spread_rows(base, stride, ways):
    rows = iota(base.shape, 0)
    for bit in (1, 2, 4):
        base = jnp.where((rows & bit) != 0, roll(base, stride * bit), base)
    upper = (iota(base.shape, 1) & 16) != 0
    base = jnp.where(upper, roll(base, -240), base)
    return [base if r == 0 else roll(base, -32 * r) for r in range(ways)]


def gather_rows(parts, stride):
    total = parts[0]
    for r in range(1, len(parts)):
        total = total + roll(parts[r], 32 * r)
    upper = (iota(total.shape, 1) & 16) != 0
    total = jnp.where(upper, 0.0, total) + roll(jnp.where(upper, total, 0.0), 240)
    rows = iota(total.shape, 0)
    for bit in (1, 2, 4):
        total = jnp.where((rows & bit) != 0, roll(total, -stride * bit), total)
    return jnp.sum(total, axis=0, keepdims=True)


def kernel(
    n_lat,
    n_lon,
    feat_in,
    cot_in_hbm,
    gain1_in,
    qkv1_in,
    proj1_in,
    tab1_in,
    gain2_in,
    qkv2_in,
    proj2_in,
    tab2_in,
    out_hbm,
    out1_hbm,
    out2_hbm,
    out_ref,
    out1_ref,
    out2_ref,
    feat_ref,
    cot_ref,
    gain1_ref,
    qkv1_ref,
    proj1_ref,
    tab1_ref,
    gain2_ref,
    qkv2_ref,
    proj2_ref,
    tab2_ref,
    load_sem,
    region,
    flat1,
    flat2,
    wt1,
    wt2,
    pp1,
    pp2,
    turn,
    z1,
    z2,
    acc1,
    acc2,
    feats,
    middles,
    units,
    inverses,
    kk,
    vt,
    vv,
    kt,
    qm,
    dom,
    qmt,
    gt,
    ot,
    normed,
    inverse1,
    s1,
    s2,
    g2,
    grad_mid,
    grad_first,
    p1,
    p2,
    ds1,
    ds2,
    k2,
    v2,
    k2t,
    lin,
    mid_out,
    mid_in,
    back_out,
    back_in,
    dense1,
    dense2,
    tiles1,
    tiles2,
    rs1,
    rs2,
    ag1,
    ag2,
    far1,
    far2,
    fin1,
    fin2,
    halo_send,
    halo_recv,
    mid_send,
    mid_recv,
    back_send,
    back_recv,
    sum_send,
    sum_recv,
):
    lat = lax.axis_index("lat")
    lon = lax.axis_index("lon")

    def wrapped(value, count):
        value = jnp.where(value >= count, value - count, value)
        return jnp.where(value < 0, value + count, value)

    def at(dy, dx):
        return (wrapped(lon + dx, n_lon), wrapped(lat + dy, n_lat))

    loads = [
        pltpu.make_async_copy(src, dst, load_sem.at[i])
        for i, (src, dst) in enumerate(
            (
                (feat_in, feat_ref),
                (qkv1_in, qkv1_ref),
                (proj1_in, proj1_ref),
                (qkv2_in, qkv2_ref),
                (proj2_in, proj2_ref),
                (tab1_in, tab1_ref),
                (tab2_in, tab2_ref),
                (gain1_in, gain1_ref),
                (gain2_in, gain2_ref),
                (cot_in_hbm, cot_ref),
            )
        )
    ]
    for load in loads:
        load.start()

    barrier = pltpu.get_barrier_semaphore()

    def greet(dy, dx):
        pl.semaphore_signal(barrier, inc=1, device_id=at(dy, dx), device_id_type=MESH)

    for dy in (-1, 0, 1):
        for dx in (-1, 0, 1):
            if dy or dx:
                greet(dy, dx)
    for j in range(2, n_lat - 1):
        greet(j, 0)
    inner, outer = lon_plan(n_lon)
    spot = lax.rem(lon, inner)

    def inner_peer(j):
        return (lon - spot + wrapped(spot + j, inner), lat)

    def greet_at(device):
        pl.semaphore_signal(barrier, inc=1, device_id=device, device_id_type=MESH)

    for j in range(1, inner):
        greet_at(inner_peer(j))
    for j in range(1, outer):
        greet(0, j * inner)

    loads[0].wait()
    own = feat_ref[...].astype(F32)
    for sy, sx, w, s in OWN:
        quarter = own[8 * sy : 8 * sy + 8, 8 * sx : 8 * sx + 8, :].reshape(64, CHANNELS)
        region[1 + sy, 1 + sx, :, :CHANNELS] = quarter.astype(BF16)

    for load in loads[1:7]:
        load.wait()

    def pad_weights(i, _):
        lane = iota((WIDE, 1), 0)
        real = (lane < 192) & ((lane & 31) < HEAD_SIZE)
        source = jnp.where(real, CHANNELS * i + lane - 2 * (lane >> 5), -1)
        pick = one_hot(iota((WIDE, 3 * CHANNELS), 1) == source)
        rows = pl.ds(pl.multiple_of(i * WIDE, WIDE), WIDE)
        wt1[rows, :] = dot_nt(pick, qkv1_ref[...]).astype(BF16)
        wt2[rows, :] = dot_nt(pick, qkv2_ref[...]).astype(BF16)

        @pl.when(i == 0)
        def _():
            pick_proj = pick[:, :CHANNELS]
            pp1[...] = dot(pick_proj, proj1_ref[...]).astype(BF16)
            pp2[...] = dot(pick_proj, proj2_ref[...]).astype(BF16)

        return 0

    lax.fori_loop(0, 3, pad_weights, 0)

    pl.semaphore_wait(barrier, 8 + n_lat - 3 + inner - 1 + outer - 1)

    def side(step):
        here = {-1: 1, 0: pl.ds(1, 2), 1: 2}[step]
        there = {-1: 3, 0: pl.ds(1, 2), 1: 0}[step]
        return here, there

    for dy in (-1, 0, 1):
        for dx in (-1, 0, 1):
            if dy == 0 and dx == 0:
                continue
            (a, a_there), (b, b_there) = side(dy), side(dx)
            pltpu.make_async_remote_copy(
                src_ref=region.at[a, b],
                dst_ref=region.at[a_there, b_there],
                send_sem=halo_send,
                recv_sem=halo_recv,
                device_id=at(dy, dx),
                device_id_type=MESH,
            ).start()

    for load in loads[7:]:
        load.wait()

    def turned(c):
        r = 255 - c
        return ((r >> 3) & 7) * 32 + ((r >> 7) & 1) * 16 + ((r >> 6) & 1) * 8 + (r & 7)

    turn[0] = one_hot(iota((CELLS, CELLS), 0) == turned(iota((1, CELLS), 1)))
    turn[1] = one_hot(iota((CELLS, CELLS), 1) == turned(iota((CELLS, 1), 0)))

    flat1[...] = jnp.zeros(flat1.shape, F32)
    flat2[...] = jnp.zeros(flat2.shape, F32)
    for dy in range(SPAN):
        flat1[:, dy * 32 : dy * 32 + SPAN] = tab1_ref[:, dy * SPAN : (dy + 1) * SPAN]
    for dy in range(CROSS):
        for s in range(3):
            start = dy * CROSS + 8 * s
            flat2[s, :, dy * 32 : dy * 32 + 23] = tab2_ref[:, start : start + 23]
    def spread(group, _):
        for i in range(3):
            h = 3 * group + i
            row = pl.ds(h, 1)
            for s in range(2):
                base = jnp.broadcast_to(flat1[row, :] * LOG2E, (8, LANES_W))
                for r, part in enumerate(spread_rows(roll(base, 8 * s - 15), 1, 4)):
                    z1[s, r, h] = part[:, :USED_W]
            for s in range(3):
                base = jnp.broadcast_to(flat2[s, row, :] * LOG2E, (8, LANES_C))
                for r, part in enumerate(spread_rows(base, -1, 4)):
                    z2[s, r, h] = part[:, :USED_C]
        return 0

    lax.fori_loop(0, HEADS // 3, spread, 0)
    query_half = (iota((1, CELLS), 1) >> 4) & 1

    def window_bias(h, y8):
        pieces = []
        for sy in range(2):
            t, r = divmod(15 - (8 * sy + y8), 4)
            for sx in range(2):
                pieces.append(z1[sx, r, h, :, 128 * t : 128 * t + CELLS])
        return jnp.concatenate(pieces, axis=0)

    def cross_bias(h, ky):
        t, r = divmod(ky, 4)
        pieces = [z2[s, r, h, :, 128 * t : 128 * t + CELLS] for s in range(3)]
        return jnp.concatenate(pieces, axis=0)

    def by_eight(values):
        return values.reshape(values.shape[0] // 8, 8, CELLS)

    def add_bias(scores, step, count, bias):
        peak = None
        for c in range(count):
            rows = slice(c * step, (c + 1) * step)
            part = scores[rows, :] * (SCALE * LOG2E) + bias(c)
            scores[rows, :] = part
            part = jnp.max(by_eight(part), axis=0)
            peak = part if peak is None else jnp.maximum(peak, part)
        return jnp.max(peak, axis=0, keepdims=True)

    def raise_all(scores, step, count, peak, probs, columns, keep):
        total = None
        for c in range(count):
            rows = slice(c * step, (c + 1) * step)
            part = jnp.exp2(scores[rows, :] - peak)
            probs[rows, columns] = part.astype(BF16)
            if keep:
                scores[rows, :] = part
            part = jnp.sum(by_eight(part), axis=0)
            total = part if total is None else total + part
        return 1.0 / jnp.sum(total, axis=0, keepdims=True)

    def weigh_all(raised, grads, step, count, inverse):
        total = None
        for c in range(count):
            rows = slice(c * step, (c + 1) * step)
            part = raised(rows) * grads[rows, :]
            grads[rows, :] = part
            part = jnp.sum(by_eight(part), axis=0)
            total = part if total is None else total + part
        return jnp.sum(total, axis=0, keepdims=True) * inverse

    def slope_all(raised, grads, step, count, total, slopes, packed, columns):
        for c in range(count):
            rows = slice(c * step, (c + 1) * step)
            part = grads[rows, :] - raised(rows) * total
            slopes[rows, :] = part
            packed[rows, columns] = part.astype(BF16)

    def collect(acc, h, s, count, group_of, slopes):
        for r in range(4):
            for t in range(count // 4 + 1):
                parts = []
                if t < count // 4:
                    group = group_of(4 * t + r)
                    parts.append(slopes[group : group + 8, 0:128])
                if t > 0:
                    group = group_of(4 * t - 4 + r)
                    parts.append(slopes[group : group + 8, 128:256])
                acc[s, r, h, :, 128 * t : 128 * t + 128] = sum(parts[1:], parts[0])

    def head_rows(rows, h):
        before = h % 4 * HEAD_PAD
        pieces = [rows]
        if before:
            pieces = [jnp.zeros((before, CELLS), rows.dtype)] + pieces
        if before + HEAD_PAD < 128:
            pieces.append(jnp.zeros((128 - HEAD_PAD - before, CELLS), rows.dtype))
        return jnp.concatenate(pieces, axis=0) if len(pieces) > 1 else rows

    def head_lanes(values, into):
        zeros = jnp.zeros((CELLS, 128), BF16)
        for h in range(HEADS):
            half = h // 4 * 128
            lanes = iota((CELLS, 128), 1) >> 5
            own_lanes = jnp.where(lanes == h % 4, values[:, half : half + 128], 0.0).astype(BF16)
            rows = slice(h * CELLS, (h + 1) * CELLS)
            into[rows, half : half + 128] = own_lanes
            into[rows, 128 - half : 256 - half] = zeros

    every = region.at[pl.ds(0, 3)]
    pltpu.make_async_copy(every, every, halo_recv).wait()

    gain1 = gain1_ref[...]
    gain2 = gain2_ref[...]

    key_half = 30 + ((iota((CELLS, 1), 0) >> 4) & 1)
    lane_row = iota((1, WIDE), 1)
    marks = key_half == jnp.where(lane_row < 192, lane_row & 31, 0)
    pad_row = iota((HEAD_PAD, CELLS), 0)

    def own_columns(h):
        return slice(h * CELLS, (h + 1) * CELLS)

    def own_rows(h):
        return slice(h * HEAD_PAD, (h + 1) * HEAD_PAD)

    for w in range(4):
        for c in range(4):
            parts = [
                region[w // 2 * 2 + s // 2, w % 2 * 2 + s % 2, 16 * c : 16 * c + 16, :CHANNELS]
                .astype(F32)
                .reshape(2, 1, 8, CHANNELS)
                for s in range(4)
            ]
            values = jnp.concatenate(parts, axis=1).reshape(64, CHANNELS)
            rows = slice(64 * c, 64 * c + 64)
            feats[w, rows, :] = values
            unit, _ = norm_parts(values)
            normed[w, rows, :] = (unit * gain1).astype(BF16)
    for w in range(4):
        if w % 2 == 0:
            floor = jnp.where(lat == (0 if w == 0 else n_lat - 1), NEGATIVE, 0.0)
            hidden = jnp.where(pad_row - 30 == 1 - query_half, floor, 0.0)
            hidden = jnp.where(pad_row >= 30, hidden, 0.0)
        queries = dot_nt(wt1[0:WIDE, :], normed[w])
        for h in range(HEADS):
            qmt[w, h] = head_rows((queries[own_rows(h), :] + hidden).astype(BF16), h)
        keys = dot_nt(normed[w], wt1[WIDE : 2 * WIDE, :])
        kk[w] = jnp.where(marks, 1.0, keys).astype(BF16)
        vt[w] = dot_nt(wt1[2 * WIDE :, :], normed[w]).astype(BF16)
    for w in range(4):
        for h in range(HEADS):
            half = h // 4 * 128
            s1[w, h] = dot(kk[w, :, half : half + 128], qmt[w, h])
    for w in range(4):
        for h in range(HEADS):
            scores = s1.at[w, h]
            peak = add_bias(scores, 32, 8, functools.partial(window_bias, h))
            inverse1[w, h] = raise_all(scores, 32, 8, peak, p1.at[w], own_columns(h), False)
    for w in range(4):
        for h in range(HEADS):
            heads_t = dot(vt[w, own_rows(h), :], p1[w, :, own_columns(h)])
            ot[w, own_rows(h), :] = heads_t * inverse1[w, h]
        ot[w, HEADS * HEAD_PAD :, :] = jnp.zeros((WIDE - HEADS * HEAD_PAD, CELLS), F32)
    for w in range(4):
        heads_out = jnp.transpose(ot[w]).astype(BF16)
        middle = feats[w] + dot(heads_out, pp1[...])
        middles[w] = middle.reshape(8, 2, 2, 8, CHANNELS)

    y_runs = ((0, 0, 4, 8, 0), (0, 1, 0, 8, 4), (1, 0, 0, 8, 12), (1, 1, 0, 4, 20))
    for wy, sy, first, last, place in y_runs:
        for wx in range(2):
            for sx in range(2):
                start = (2 * wx + sx) * 8
                lin[place : place + last - first, start : start + 8, :] = middles[
                    2 * wy + wx, first:last, sy, sx
                ]

    for i in range(KEY_SIDE // 2):
        lines, rows = slice(2 * i, 2 * i + 2), slice(64 * i, 64 * i + 64)
        unit, inverse = norm_parts(lin[lines].reshape(64, CHANNELS))
        units[rows, :] = unit
        inverses[rows, :] = inverse
        normal = (unit * gain2).astype(BF16).astype(F32)
        lin[lines] = normal.reshape(2, 32, CHANNELS)
    inside_low = jnp.where(lat > 0, 1.0, 0.0)
    inside_high = jnp.where(lat < n_lat - 1, 1.0, 0.0)
    lin[0:4] = lin[0:4] * inside_low
    lin[20:24] = lin[20:24] * inside_high
    keys_in = lin[:, 4:28, :].reshape(KEYS, CHANNELS).astype(BF16)
    k2[...] = dot_nt(keys_in, wt2[WIDE : 2 * WIDE, :]).astype(BF16)
    v2[...] = dot_nt(keys_in, wt2[2 * WIDE :, :]).astype(BF16)
    k2t[...] = dot_nt(wt2[WIDE : 2 * WIDE, :], keys_in).astype(BF16)

    def own_part(sy, sx):
        return slice(4 + 8 * sy, 12 + 8 * sy), slice(8 + 8 * sx, 16 + 8 * sx)

    own_second = jnp.concatenate(
        [lin[(*own_part(sy, sx), slice(None))].reshape(64, CHANNELS) for sy, sx, w, s in OWN],
        axis=0,
    )
    queries_in = dot(turn[0], own_second.astype(BF16)).astype(BF16)
    cot = cot_ref[...].astype(F32)
    cot_own = [
        cot[8 * sy : 8 * sy + 8, 8 * sx : 8 * sx + 8, :].reshape(64, CHANNELS)
        for sy, sx, w, s in OWN
    ]
    cot_in = dot(turn[0], jnp.concatenate(cot_own, axis=0).astype(BF16)).astype(BF16)
    queries_t = dot_nt(wt2[0:WIDE, :], queries_in).astype(BF16)
    gt[...] = dot_nt(pp2[...], cot_in)
    for h in range(HEADS):
        qmt[0, h] = head_rows(queries_t[h * HEAD_PAD : (h + 1) * HEAD_PAD, :], h)
    head_lanes(dot_nt(queries_in, wt2[0:WIDE, :]), qm)

    def bias(h, c):
        return jnp.concatenate([cross_bias(h, 2 * c), cross_bias(h, 2 * c + 1)], axis=0)

    for h in range(HEADS):
        half = h // 4 * 128
        s2[h] = dot(k2[:, half : half + 128], qmt[0, h])
    inverse2 = []
    for h in range(HEADS):
        half = h // 4 * 128
        peak = add_bias(s2.at[h], 48, 12, functools.partial(bias, h))
        inverse2.append(raise_all(s2.at[h], 48, 12, peak, p2, own_columns(h), True))
        scaled = gt[own_rows(h), :] * inverse2[h]
        gt[own_rows(h), :] = scaled
        g2[h] = dot(v2[:, half : half + 128], head_rows(scaled.astype(BF16), h))
    for h in range(HEADS):

        def raised(part):
            return s2[h, part, :]

        total = weigh_all(raised, g2.at[h], 48, 12, inverse2[h])
        slope_all(raised, g2.at[h], 48, 12, total, s2.at[h], ds2, own_columns(h))
        for s in range(3):
            collect(acc2, h, s, KEY_SIDE, lambda m: (m * 3 + s) * 8, s2.at[h])
    for h in range(HEADS):
        ot[0, own_rows(h), :] = dot(k2t[own_rows(h), :], ds2[:, own_columns(h)])
    head_lanes(jnp.transpose(gt[...]), dom)
    grad_queries = (jnp.transpose(ot[0]) * SCALE).astype(BF16)
    grad_keys = (dot(ds2[...], qm[...]) * SCALE).astype(BF16)
    grad_values = dot(p2[...], dom[...]).astype(BF16)
    grad_second = dot(grad_keys, wt2[WIDE : 2 * WIDE, :]) + dot(grad_values, wt2[2 * WIDE :, :])
    grad_own = dot(turn[1], dot(grad_queries, wt2[0:WIDE, :]).astype(BF16))

    lin[...] = jnp.zeros(lin.shape, F32)
    lin[:, 4:28, :] = grad_second.reshape(KEY_SIDE, KEY_SIDE, CHANNELS)
    lin[0:4] = lin[0:4] * inside_low
    lin[20:24] = lin[20:24] * inside_high
    for i, (sy, sx, w, s) in enumerate(OWN):
        place = (*own_part(sy, sx), slice(None))
        lin[place] = lin[place] + grad_own[64 * i : 64 * i + 64, :].reshape(8, 8, CHANNELS)

    for i in range(KEY_SIDE // 2):
        lines, rows = slice(2 * i, 2 * i + 2), slice(64 * i, 64 * i + 64)
        grad = lin[lines].reshape(64, CHANNELS)
        grad = norm_back(units[rows, :], inverses[rows, :], gain2, grad)
        lin[lines] = grad.reshape(2, 32, CHANNELS)
    for i, (sy, sx, w, s) in enumerate(OWN):
        place = (*own_part(sy, sx), slice(None))
        lin[place] = lin[place] + cot_own[i].reshape(8, 8, CHANNELS)
    for w in range(3):
        rows, cols = 12 * (w // 2), 16 * (w % 2)
        piece = lin[rows : rows + 12, cols : cols + 16, :]
        mid_out[w, :, :CHANNELS] = piece.reshape(192, CHANNELS).astype(BF16)
        pltpu.make_async_remote_copy(
            src_ref=mid_out.at[w],
            dst_ref=mid_in.at[w],
            send_sem=mid_send,
            recv_sem=mid_recv,
            device_id=at(w // 2 - 1, w % 2 - 1),
            device_id_type=MESH,
        ).start()

    def sum_scatter(kind, tiles, buffer):
        chunks, depth = buffer_plan(tiles, n_lat)
        for c in range(chunks):

            @pl.when(lat != c)
            def _():
                pltpu.make_async_remote_copy(
                    src_ref=tiles.at[pl.ds(c * depth, depth)],
                    dst_ref=buffer.at[wrapped(lat - c, n_lat) - 1],
                    send_sem=sum_send.at[kind],
                    recv_sem=sum_recv.at[kind],
                    device_id=(lon, c),
                    device_id_type=MESH,
                ).start()

    def drain(sem, ref):
        pltpu.make_async_copy(ref, ref, sem).wait()

    def sum_spread(kind, tiles, buffer, rows):
        chunks, depth = buffer_plan(tiles, n_lat)

        @pl.when(lat < chunks)
        def _():
            drain(sum_recv.at[kind], buffer)
            total = tiles[pl.ds(lat * depth, depth)]
            for i in range(n_lat - 1):
                total = total + buffer[i]
            rows[spot] = total
            for j in range(1, inner):
                pltpu.make_async_remote_copy(
                    src_ref=rows.at[spot],
                    dst_ref=rows.at[spot],
                    send_sem=sum_send.at[kind + 1],
                    recv_sem=sum_recv.at[kind + 1],
                    device_id=inner_peer(j),
                    device_id_type=MESH,
                ).start()

    def sum_cross(kind, tiles, rows, far):
        chunks, depth = buffer_plan(tiles, n_lat)
        block = lax.div(lon, inner)

        @pl.when(lat < chunks)
        def _():
            drain(sum_recv.at[kind + 1], rows.at[pl.ds(0, inner - 1)])
            total = rows[0]
            for i in range(1, inner):
                total = total + rows[i]
            far[block] = total
            for j in range(1, outer):
                pltpu.make_async_remote_copy(
                    src_ref=far.at[block],
                    dst_ref=far.at[block],
                    send_sem=sum_send.at[kind + 2],
                    recv_sem=sum_recv.at[kind + 2],
                    device_id=at(0, j * inner),
                    device_id_type=MESH,
                ).start()

    def sum_gather(kind, tiles, far, result):
        chunks, depth = buffer_plan(tiles, n_lat)

        @pl.when(lat < chunks)
        def _():
            if outer > 1:
                drain(sum_recv.at[kind + 2], far.at[pl.ds(0, outer - 1)])
            total = far[0]
            for i in range(1, outer):
                total = total + far[i]
            result[lat] = total
            for j in range(1, n_lat):
                pltpu.make_async_remote_copy(
                    src_ref=result.at[lat],
                    dst_ref=result.at[lat],
                    send_sem=sum_send.at[kind + 3],
                    recv_sem=sum_recv.at[kind + 3],
                    device_id=at(j, 0),
                    device_id_type=MESH,
                ).start()

    def sum_end(kind, tiles, buffer, rows, far, result):
        chunks, depth = buffer_plan(tiles, n_lat)

        @pl.when(lat < chunks)
        def _():
            if chunks > 1:
                drain(sum_recv.at[kind + 3], result.at[pl.ds(0, chunks - 1)])
                drain(sum_send.at[kind], result.at[pl.ds(0, chunks - 1)])
            drain(sum_send.at[kind + 1], rows.at[pl.ds(0, inner - 1)])
            if outer > 1:
                drain(sum_send.at[kind + 2], far.at[pl.ds(0, outer - 1)])
            drain(sum_send.at[kind + 3], buffer)

        @pl.when(lat >= chunks)
        def _():
            drain(sum_recv.at[kind + 3], result)
            drain(sum_send.at[kind], result)

    def joined(result):
        chunks, depth = result.shape[0], result.shape[1]
        return jnp.concatenate(
            [result[c, d] for c in range(chunks) for d in range(depth)], axis=1
        )

    def widened(part, width):
        return jnp.concatenate([part, jnp.zeros((8, width - part.shape[1]), F32)], axis=1)

    def gather_cross(group, _):
        for i in range(3):
            h = 3 * group + i
            for s in range(3):
                parts = [widened(acc2[s, r, h], LANES_C) for r in range(4)]
                flat2[s, pl.ds(h, 1), :] = gather_rows(parts, -1)
        return 0

    lax.fori_loop(0, HEADS // 3, gather_cross, 0)
    dense2[...] = jnp.zeros(dense2.shape, F32)
    for dy in range(CROSS):
        for s in range(3):
            start = dy * CROSS + 8 * s
            dense2[s, 0:HEADS, start : start + 23] = flat2[s, :, dy * 32 : dy * 32 + 23]
    for t in range(TILES_C):
        part = pl.ds(128 * t, 128)
        whole = dense2[0, :, part] + dense2[1, :, part] + dense2[2, :, part]
        tiles2[t] = whole
    sum_scatter(0, tiles2, rs2)

    vv[...] = dot_nt(normed[3], wt1[2 * WIDE :, :]).astype(BF16)
    kt[...] = dot_nt(wt1[WIDE : 2 * WIDE, :], normed[3]).astype(BF16)
    head_lanes(dot_nt(normed[3], wt1[0:WIDE, :]), qm)

    drain(mid_recv, mid_in)
    total = lin[12:24, 16:32, :] + mid_in[2, :, :CHANNELS].astype(F32).reshape(12, 16, CHANNELS)
    below = (mid_in[0, :, :CHANNELS].astype(F32) + mid_in[1, :, :CHANNELS].astype(F32)).reshape(12, 16, CHANNELS)
    total = jnp.concatenate([total[0:4], total[4:12] + below[0:8], below[8:12]], axis=0)
    pair = [total[8 * sy : 8 * sy + 8].reshape(8, 1, 16, CHANNELS) for sy in range(2)]
    grad_mid[...] = jnp.concatenate(pair, axis=1).reshape(CELLS, CHANNELS)

    grads_t = dot_nt(pp1[...], grad_mid[...].astype(BF16))
    for h in range(HEADS):
        scaled = grads_t[own_rows(h), :] * inverse1[3, h]
        gt[own_rows(h), :] = scaled
        half = h // 4 * 128
        s1[1, h] = dot(vv[:, half : half + 128], head_rows(scaled.astype(BF16), h))
    for h in range(HEADS):

        def raised(part):
            return p1[3, part, own_columns(h)].astype(F32)

        total = weigh_all(raised, s1.at[1, h], 32, 8, inverse1[3, h])
        slope_all(raised, s1.at[1, h], 32, 8, total, s1.at[0, h], ds1, own_columns(h))
        for sx in range(2):

            def group_of(m):
                ky = 15 - m
                return (ky % 8 * 4 + ky // 8 * 2 + sx) * 8

            collect(acc1, h, sx, 16, group_of, s1.at[0, h])

    for h in range(HEADS):
        total = None
        for s in range(2):
            parts = [widened(acc1[s, r, h], LANES_W) for r in range(4)]
            piece = roll(gather_rows(parts, 1), 15 - 8 * s)
            total = piece if total is None else total + piece
        flat1[h : h + 1, :] = total
    dense1[...] = jnp.zeros(dense1.shape, F32)
    for dy in range(SPAN):
        dense1[0:HEADS, dy * SPAN : (dy + 1) * SPAN] = flat1[:, dy * 32 : dy * 32 + SPAN]
    for t in range(TILES_W):
        tiles1[t] = dense1[:, 128 * t : 128 * t + 128]
    sum_scatter(4, tiles1, rs1)
    sum_spread(0, tiles2, rs2, ag2)

    for h in range(HEADS):
        ot[0, own_rows(h), :] = dot(kt[own_rows(h), :], ds1[:, own_columns(h)])
    head_lanes(jnp.transpose(gt[...]), dom)
    grad_queries = (jnp.transpose(ot[0]) * SCALE).astype(BF16)
    grad_keys = (dot(ds1[...], qm[...]) * SCALE).astype(BF16)
    grad_values = dot(p1[3], dom[...])
    sum_spread(4, tiles1, rs1, ag1)
    sum_cross(0, tiles2, ag2, far2)
    grad_first[...] = (
        dot(grad_queries, wt1[0:WIDE, :])
        + dot(grad_keys, wt1[WIDE : 2 * WIDE, :])
        + dot(grad_values.astype(BF16), wt1[2 * WIDE :, :])
    )
    for c in range(4):
        rows = slice(64 * c, 64 * c + 64)
        unit, inverse = norm_parts(feats[3, rows, :])
        grad = grad_mid[rows, :] + norm_back(unit, inverse, gain1, grad_first[rows, :])
        quarters = grad.reshape(2, 2, 2, 8, CHANNELS)
        out_ref[8 + 2 * c : 10 + 2 * c, 8:16, :CHANNELS] = quarters[:, 0, 0]
        for s in (1, 2, 3):
            piece = quarters[:, s // 2, s % 2].reshape(16, CHANNELS)
            back_out[s - 1, 16 * c : 16 * c + 16, :CHANNELS] = piece.astype(BF16)
    for s in (1, 2, 3):
        pltpu.make_async_remote_copy(
            src_ref=back_out.at[s - 1],
            dst_ref=back_in.at[s - 1],
            send_sem=back_send,
            recv_sem=back_recv,
            device_id=at(s // 2, s % 2),
            device_id_type=MESH,
        ).start()
    sum_cross(4, tiles1, ag1, far1)
    sum_gather(0, tiles2, far2, fin2)
    drain(back_recv, back_in)
    out_ref[8:16, 0:8, :CHANNELS] = back_in[0, :, :CHANNELS].astype(F32).reshape(8, 8, CHANNELS)
    out_ref[0:8, 8:16, :CHANNELS] = back_in[1, :, :CHANNELS].astype(F32).reshape(8, 8, CHANNELS)
    out_ref[0:8, 0:8, :CHANNELS] = back_in[2, :, :CHANNELS].astype(F32).reshape(8, 8, CHANNELS)
    store = pltpu.make_async_copy(out_ref, out_hbm, load_sem.at[0])
    store.start()
    sum_gather(4, tiles1, far1, fin1)
    sum_end(0, tiles2, rs2, ag2, far2, fin2)
    out2_ref[...] = joined(fin2)
    store2 = pltpu.make_async_copy(out2_ref, out2_hbm, load_sem.at[1])
    store2.start()
    sum_end(4, tiles1, rs1, ag1, far1, fin1)
    out1_ref[...] = joined(fin1)
    store1 = pltpu.make_async_copy(out1_ref, out1_hbm, load_sem.at[2])
    store1.start()
    pltpu.make_async_copy(every, every, halo_send).wait()
    drain(mid_send, mid_out)
    drain(back_send, back_out)
    store.wait()
    store2.wait()
    store1.wait()


def lon_plan(n_lon):
    inner = 8 if n_lon % 8 == 0 else 2 if n_lon % 2 == 0 else n_lon
    return inner, n_lon // inner


def buffer_plan(tiles, n_lat):
    count = tiles.shape[0]
    chunks = min(n_lat, count)
    return chunks, count // chunks


def body(n_lat, n_lon, *operands):
    vmem = pltpu.VMEM
    inner, outer = lon_plan(n_lon)

    def sums(count):
        chunks = min(n_lat, count)
        depth = count // chunks
        return (
            vmem((count, 8, 128), F32),
            vmem((n_lat - 1, depth, 8, 128), F32),
            vmem((inner, depth, 8, 128), F32),
            vmem((outer, depth, 8, 128), F32),
            vmem((chunks, depth, 8, 128), F32),
        )

    tiles1, rs1, ag1, far1, fin1 = sums(TILES_W)
    tiles2, rs2, ag2, far2, fin2 = sums(TILES_C)
    scratch = [
        vmem((16, 16, WIDE), F32),
        vmem((8, 128 * TILES_W), F32),
        vmem((8, 128 * TILES_C), F32),
        vmem((16, 16, CHANNELS), BF16),
        vmem((16, 16, CHANNELS), BF16),
        vmem((1, CHANNELS), F32),
        vmem((CHANNELS, 3 * CHANNELS), BF16),
        vmem((CHANNELS, CHANNELS), BF16),
        vmem((HEADS, SPAN * SPAN), F32),
        vmem((1, CHANNELS), F32),
        vmem((CHANNELS, 3 * CHANNELS), BF16),
        vmem((CHANNELS, CHANNELS), BF16),
        vmem((HEADS, CROSS * CROSS), F32),
        pltpu.SemaphoreType.DMA((10,)),
        vmem((4, 4, 64, WIDE), BF16),
        vmem((HEADS, LANES_W), F32),
        vmem((3, HEADS, LANES_C), F32),
        vmem((3 * WIDE, CHANNELS), BF16),
        vmem((3 * WIDE, CHANNELS), BF16),
        vmem((WIDE, CHANNELS), BF16),
        vmem((WIDE, CHANNELS), BF16),
        vmem((2, CELLS, CELLS), BF16),
        vmem((2, 4, HEADS, 8, USED_W), F32),
        vmem((3, 4, HEADS, 8, USED_C), F32),
        vmem((2, 4, HEADS, 8, USED_W), F32),
        vmem((3, 4, HEADS, 8, USED_C), F32),
        vmem((4, CELLS, CHANNELS), F32),
        vmem((4, 8, 2, 2, 8, CHANNELS), F32),
        vmem((KEY_SIDE * 32, CHANNELS), F32),
        vmem((KEY_SIDE * 32, 1), F32),
        vmem((4, CELLS, WIDE), BF16),
        vmem((4, WIDE, CELLS), BF16),
        vmem((CELLS, WIDE), BF16),
        vmem((WIDE, CELLS), BF16),
        vmem((HEADS * CELLS, WIDE), BF16),
        vmem((HEADS * CELLS, WIDE), BF16),
        vmem((4, HEADS, 128, CELLS), BF16),
        vmem((WIDE, CELLS), F32),
        vmem((4, WIDE, CELLS), F32),
        vmem((4, CELLS, CHANNELS), BF16),
        vmem((4, HEADS, 1, CELLS), F32),
        vmem((4, HEADS, CELLS, CELLS), F32),
        vmem((HEADS, KEYS, CELLS), F32),
        vmem((HEADS, KEYS, CELLS), F32),
        vmem((CELLS, CHANNELS), F32),
        vmem((CELLS, CHANNELS), F32),
        vmem((4, CELLS, HEADS * CELLS), BF16),
        vmem((KEYS, HEADS * CELLS), BF16),
        vmem((CELLS, HEADS * CELLS), BF16),
        vmem((KEYS, HEADS * CELLS), BF16),
        vmem((KEYS, WIDE), BF16),
        vmem((KEYS, WIDE), BF16),
        vmem((WIDE, KEYS), BF16),
        vmem((KEY_SIDE, 32, CHANNELS), F32),
        vmem((3, 192, WIDE), BF16),
        vmem((3, 192, WIDE), BF16),
        vmem((3, 64, WIDE), BF16),
        vmem((3, 64, WIDE), BF16),
        vmem((8, 128 * TILES_W), F32),
        vmem((3, 8, 128 * TILES_C), F32),
        tiles1,
        tiles2,
        rs1,
        rs2,
        ag1,
        ag2,
        far1,
        far2,
        fin1,
        fin2,
        pltpu.SemaphoreType.DMA,
        pltpu.SemaphoreType.DMA,
        pltpu.SemaphoreType.DMA,
        pltpu.SemaphoreType.DMA,
        pltpu.SemaphoreType.DMA,
        pltpu.SemaphoreType.DMA,
        pltpu.SemaphoreType.DMA((8,)),
        pltpu.SemaphoreType.DMA((8,)),
    ]
    hbm = pl.BlockSpec(memory_space=pltpu.HBM)
    limit = 63 * 1024 * 1024
    shapes = (
        jax.ShapeDtypeStruct((16, 16, WIDE), F32),
        jax.ShapeDtypeStruct((8, 128 * TILES_W), F32),
        jax.ShapeDtypeStruct((8, 128 * TILES_C), F32),
    )
    grads, grad1, grad2 = pl.pallas_call(
        functools.partial(kernel, n_lat, n_lon),
        out_shape=shapes,
        in_specs=[hbm] * 10,
        out_specs=(hbm,) * 3,
        scratch_shapes=scratch,
        compiler_params=pltpu.CompilerParams(
            collective_id=0, has_side_effects=True, vmem_limit_bytes=limit
        ),
    )(*operands)
    return (
        grads[:, :, :CHANNELS],
        grad1[:HEADS, : SPAN * SPAN],
        grad2[:HEADS, : CROSS * CROSS],
    )


def solution(mesh):
    def local(
        features,
        cotangent,
        first_gain,
        window_qkv,
        window_proj,
        window_table,
        second_gain,
        cross_qkv,
        cross_proj,
        cross_table,
    ):
        return body(
            mesh.shape["lat"],
            mesh.shape["lon"],
            features,
            cotangent,
            first_gain.reshape(1, CHANNELS),
            window_qkv,
            window_proj,
            window_table,
            second_gain.reshape(1, CHANNELS),
            cross_qkv,
            cross_proj,
            cross_table,
        )

    return jax.shard_map(
        local,
        mesh=mesh,
        in_specs=(
            P("lat", "lon", None),
            P("lat", "lon", None),
            P(),
            P(),
            P(),
            P(),
            P(),
            P(),
            P(),
            P(),
        ),
        out_specs=(P("lat", "lon", None), P(), P()),
        check_vma=False,
    )
```

```python
import functools

import jax
import jax.numpy as jnp
from jax import lax
from jax.experimental import pallas as pl
from jax.experimental.pallas import tpu as pltpu
from jax.sharding import PartitionSpec as P

CHANNELS = 180
HEADS = 6
HEAD_SIZE = 30
HEAD_PAD = 32
WIDE = 256
CELLS = 256
KEYS = 576
KEY_SIDE = 24
SPAN = 31
CROSS = 39
EPSILON = 1e-05
NEGATIVE = -1e30
LOG2E = 1.4426950408889634
SCALE = HEAD_SIZE**-0.5
TILES_W = 8
TILES_C = 12
LANES_W = 1024
LANES_C = 1280
USED_W = 640
USED_C = 896
MESH = pl.DeviceIdType.MESH
F32 = jnp.float32
BF16 = jnp.bfloat16


def iota(shape, dim):
    return lax.broadcasted_iota(jnp.int32, shape, dim)


def dot(a, b):
    return jnp.dot(a, b, preferred_element_type=F32)


def dot_nt(a, b):
    return lax.dot_general(a, b, (((1,), (1,)), ((), ())), preferred_element_type=F32)


def one_hot(mask):
    return jnp.where(mask, 1.0, 0.0).astype(BF16)


def roll(x, shift):
    size = x.shape[-1]
    return pltpu.roll(x, shift % size, x.ndim - 1)


def norm_parts(values):
    centre = jnp.mean(values, axis=-1, keepdims=True)
    offset = values - centre
    spread = jnp.mean(offset * offset, axis=-1, keepdims=True)
    inverse = lax.rsqrt(spread + EPSILON)
    return offset * inverse, inverse


def norm_back(unit, inverse, gain, grads):
    scaled = grads * gain
    first = jnp.mean(scaled, axis=-1, keepdims=True)
    second = jnp.mean(scaled * unit, axis=-1, keepdims=True)
    return inverse * (scaled - first - unit * second)


OWN = [(sy, sx, 2 * sy + sx, (1 - sy) * 2 + (1 - sx)) for sy in (0, 1) for sx in (0, 1)]


def spread_rows(base, stride, ways):
    rows = iota(base.shape, 0)
    for bit in (1, 2, 4):
        base = jnp.where((rows & bit) != 0, roll(base, stride * bit), base)
    upper = (iota(base.shape, 1) & 16) != 0
    base = jnp.where(upper, roll(base, -240), base)
    return [base if r == 0 else roll(base, -32 * r) for r in range(ways)]


def gather_rows(parts, stride):
    total = parts[0]
    for r in range(1, len(parts)):
        total = total + roll(parts[r], 32 * r)
    upper = (iota(total.shape, 1) & 16) != 0
    total = jnp.where(upper, 0.0, total) + roll(jnp.where(upper, total, 0.0), 240)
    rows = iota(total.shape, 0)
    for bit in (1, 2, 4):
        total = jnp.where((rows & bit) != 0, roll(total, -stride * bit), total)
    return jnp.sum(total, axis=0, keepdims=True)


def kernel(
    n_lat,
    n_lon,
    feat_in,
    cot_in_hbm,
    gain1_in,
    qkv1_in,
    proj1_in,
    tab1_in,
    gain2_in,
    qkv2_in,
    proj2_in,
    tab2_in,
    out_hbm,
    out1_hbm,
    out2_hbm,
    out_ref,
    out1_ref,
    out2_ref,
    feat_ref,
    cot_ref,
    gain1_ref,
    qkv1_ref,
    proj1_ref,
    tab1_ref,
    gain2_ref,
    qkv2_ref,
    proj2_ref,
    tab2_ref,
    load_sem,
    region,
    flat1,
    flat2,
    wt1,
    wt2,
    pp1,
    pp2,
    turn,
    z1,
    z2,
    acc1,
    acc2,
    feats,
    middles,
    units,
    inverses,
    kk,
    vt,
    vv,
    kt,
    qm,
    dom,
    qmt,
    gt,
    ot,
    normed,
    inverse1,
    s1,
    s2,
    g2,
    grad_mid,
    grad_first,
    p1,
    p2,
    ds1,
    ds2,
    k2,
    v2,
    k2t,
    lin,
    mid_out,
    mid_in,
    back_out,
    back_in,
    dense1,
    dense2,
    tiles1,
    tiles2,
    rs1,
    rs2,
    ag1,
    ag2,
    far1,
    far2,
    fin1,
    fin2,
    halo_send,
    halo_recv,
    mid_send,
    mid_recv,
    back_send,
    back_recv,
    sum_send,
    sum_recv,
):
    lat = lax.axis_index("lat")
    lon = lax.axis_index("lon")

    def wrapped(value, count):
        value = jnp.where(value >= count, value - count, value)
        return jnp.where(value < 0, value + count, value)

    def at(dy, dx):
        return (wrapped(lon + dx, n_lon), wrapped(lat + dy, n_lat))

    loads = [
        pltpu.make_async_copy(src, dst, load_sem.at[i])
        for i, (src, dst) in enumerate(
            (
                (feat_in, feat_ref),
                (qkv1_in, qkv1_ref),
                (proj1_in, proj1_ref),
                (qkv2_in, qkv2_ref),
                (proj2_in, proj2_ref),
                (tab1_in, tab1_ref),
                (tab2_in, tab2_ref),
                (gain1_in, gain1_ref),
                (gain2_in, gain2_ref),
                (cot_in_hbm, cot_ref),
            )
        )
    ]
    for load in loads:
        load.start()

    barrier = pltpu.get_barrier_semaphore()

    def greet(dy, dx):
        pl.semaphore_signal(barrier, inc=1, device_id=at(dy, dx), device_id_type=MESH)

    for dy in (-1, 0, 1):
        for dx in (-1, 0, 1):
            if dy or dx:
                greet(dy, dx)
    for j in range(2, n_lat - 1):
        greet(j, 0)
    inner, outer = lon_plan(n_lon)
    spot = lax.rem(lon, inner)

    def inner_peer(j):
        return (lon - spot + wrapped(spot + j, inner), lat)

    def greet_at(device):
        pl.semaphore_signal(barrier, inc=1, device_id=device, device_id_type=MESH)

    for j in range(1, inner):
        greet_at(inner_peer(j))
    for j in range(1, outer):
        greet(0, j * inner)

    loads[0].wait()
    own = feat_ref[...].astype(F32)
    for sy, sx, w, s in OWN:
        quarter = own[8 * sy : 8 * sy + 8, 8 * sx : 8 * sx + 8, :].reshape(64, CHANNELS)
        region[1 + sy, 1 + sx, :, :CHANNELS] = quarter.astype(BF16)

    for load in loads[1:7]:
        load.wait()

    for i in range(3):
        lane = iota((WIDE, 1), 0)
        real = (lane < 192) & ((lane & 31) < HEAD_SIZE)
        source = jnp.where(real, CHANNELS * i + lane - 2 * (lane >> 5), -1)
        pick = one_hot(iota((WIDE, 3 * CHANNELS), 1) == source)
        rows = slice(i * WIDE, (i + 1) * WIDE)
        wt1[rows, :] = dot_nt(pick, qkv1_ref[...]).astype(BF16)
        wt2[rows, :] = dot_nt(pick, qkv2_ref[...]).astype(BF16)
        if i == 0:
            pp1[...] = dot(pick[:, :CHANNELS], proj1_ref[...]).astype(BF16)
            pp2[...] = dot(pick[:, :CHANNELS], proj2_ref[...]).astype(BF16)

    pl.semaphore_wait(barrier, 8 + n_lat - 3 + inner - 1 + outer - 1)

    def side(step):
        here = {-1: 1, 0: pl.ds(1, 2), 1: 2}[step]
        there = {-1: 3, 0: pl.ds(1, 2), 1: 0}[step]
        return here, there

    for dy in (-1, 0, 1):
        for dx in (-1, 0, 1):
            if dy == 0 and dx == 0:
                continue
            (a, a_there), (b, b_there) = side(dy), side(dx)
            pltpu.make_async_remote_copy(
                src_ref=region.at[a, b],
                dst_ref=region.at[a_there, b_there],
                send_sem=halo_send,
                recv_sem=halo_recv,
                device_id=at(dy, dx),
                device_id_type=MESH,
            ).start()

    for load in loads[7:]:
        load.wait()

    def turned(c):
        r = 255 - c
        return ((r >> 3) & 7) * 32 + ((r >> 7) & 1) * 16 + ((r >> 6) & 1) * 8 + (r & 7)

    turn[0] = one_hot(iota((CELLS, CELLS), 0) == turned(iota((1, CELLS), 1)))
    turn[1] = one_hot(iota((CELLS, CELLS), 1) == turned(iota((CELLS, 1), 0)))

    flat1[...] = jnp.zeros(flat1.shape, F32)
    flat2[...] = jnp.zeros(flat2.shape, F32)
    for dy in range(SPAN):
        flat1[:, dy * 32 : dy * 32 + SPAN] = tab1_ref[:, dy * SPAN : (dy + 1) * SPAN]
    for dy in range(CROSS):
        for s in range(3):
            start = dy * CROSS + 8 * s
            flat2[s, :, dy * 32 : dy * 32 + 23] = tab2_ref[:, start : start + 23]
    def spread(group, _):
        for i in range(3):
            h = 3 * group + i
            row = pl.ds(h, 1)
            for s in range(2):
                base = jnp.broadcast_to(flat1[row, :] * LOG2E, (8, LANES_W))
                for r, part in enumerate(spread_rows(roll(base, 8 * s - 15), 1, 4)):
                    z1[s, r, h] = part[:, :USED_W]
            for s in range(3):
                base = jnp.broadcast_to(flat2[s, row, :] * LOG2E, (8, LANES_C))
                for r, part in enumerate(spread_rows(base, -1, 4)):
                    z2[s, r, h] = part[:, :USED_C]
        return 0

    lax.fori_loop(0, HEADS // 3, spread, 0)
    query_half = (iota((1, CELLS), 1) >> 4) & 1

    def window_bias(h, y8):
        pieces = []
        for sy in range(2):
            t, r = divmod(15 - (8 * sy + y8), 4)
            for sx in range(2):
                pieces.append(z1[sx, r, h, :, 128 * t : 128 * t + CELLS])
        return jnp.concatenate(pieces, axis=0)

    def cross_bias(h, ky):
        t, r = divmod(ky, 4)
        pieces = [z2[s, r, h, :, 128 * t : 128 * t + CELLS] for s in range(3)]
        return jnp.concatenate(pieces, axis=0)

    def by_eight(values):
        return values.reshape(values.shape[0] // 8, 8, CELLS)

    def add_bias(scores, step, count, bias):
        peak = None
        for c in range(count):
            rows = slice(c * step, (c + 1) * step)
            part = scores[rows, :] * (SCALE * LOG2E) + bias(c)
            scores[rows, :] = part
            part = jnp.max(by_eight(part), axis=0)
            peak = part if peak is None else jnp.maximum(peak, part)
        return jnp.max(peak, axis=0, keepdims=True)

    def raise_all(scores, step, count, peak, probs, columns, keep):
        total = None
        for c in range(count):
            rows = slice(c * step, (c + 1) * step)
            part = jnp.exp2(scores[rows, :] - peak)
            probs[rows, columns] = part.astype(BF16)
            if keep:
                scores[rows, :] = part
            part = jnp.sum(by_eight(part), axis=0)
            total = part if total is None else total + part
        return 1.0 / jnp.sum(total, axis=0, keepdims=True)

    def weigh_all(raised, grads, step, count, inverse):
        total = None
        for c in range(count):
            rows = slice(c * step, (c + 1) * step)
            part = raised(rows) * grads[rows, :]
            grads[rows, :] = part
            part = jnp.sum(by_eight(part), axis=0)
            total = part if total is None else total + part
        return jnp.sum(total, axis=0, keepdims=True) * inverse

    def slope_all(raised, grads, step, count, total, slopes, packed, columns):
        for c in range(count):
            rows = slice(c * step, (c + 1) * step)
            part = grads[rows, :] - raised(rows) * total
            slopes[rows, :] = part
            packed[rows, columns] = part.astype(BF16)

    def collect(acc, h, s, count, group_of, slopes):
        for r in range(4):
            for t in range(count // 4 + 1):
                parts = []
                if t < count // 4:
                    group = group_of(4 * t + r)
                    parts.append(slopes[group : group + 8, 0:128])
                if t > 0:
                    group = group_of(4 * t - 4 + r)
                    parts.append(slopes[group : group + 8, 128:256])
                acc[s, r, h, :, 128 * t : 128 * t + 128] = sum(parts[1:], parts[0])

    def head_rows(rows, h):
        before = h % 4 * HEAD_PAD
        pieces = [rows]
        if before:
            pieces = [jnp.zeros((before, CELLS), rows.dtype)] + pieces
        if before + HEAD_PAD < 128:
            pieces.append(jnp.zeros((128 - HEAD_PAD - before, CELLS), rows.dtype))
        return jnp.concatenate(pieces, axis=0) if len(pieces) > 1 else rows

    def head_lanes(values, into):
        zeros = jnp.zeros((CELLS, 128), BF16)
        for h in range(HEADS):
            half = h // 4 * 128
            lanes = iota((CELLS, 128), 1) >> 5
            own_lanes = jnp.where(lanes == h % 4, values[:, half : half + 128], 0.0).astype(BF16)
            rows = slice(h * CELLS, (h + 1) * CELLS)
            into[rows, half : half + 128] = own_lanes
            into[rows, 128 - half : 256 - half] = zeros

    every = region.at[pl.ds(0, 3)]
    pltpu.make_async_copy(every, every, halo_recv).wait()

    gain1 = gain1_ref[...]
    gain2 = gain2_ref[...]

    key_half = 30 + ((iota((CELLS, 1), 0) >> 4) & 1)
    lane_row = iota((1, WIDE), 1)
    marks = key_half == jnp.where(lane_row < 192, lane_row & 31, 0)
    pad_row = iota((HEAD_PAD, CELLS), 0)

    def own_columns(h):
        return slice(h * CELLS, (h + 1) * CELLS)

    def own_rows(h):
        return slice(h * HEAD_PAD, (h + 1) * HEAD_PAD)

    for w in range(4):
        for c in range(4):
            parts = [
                region[w // 2 * 2 + s // 2, w % 2 * 2 + s % 2, 16 * c : 16 * c + 16, :CHANNELS]
                .astype(F32)
                .reshape(2, 1, 8, CHANNELS)
                for s in range(4)
            ]
            values = jnp.concatenate(parts, axis=1).reshape(64, CHANNELS)
            rows = slice(64 * c, 64 * c + 64)
            feats[w, rows, :] = values
            unit, _ = norm_parts(values)
            normed[w, rows, :] = (unit * gain1).astype(BF16)
    for w in range(4):
        if w % 2 == 0:
            floor = jnp.where(lat == (0 if w == 0 else n_lat - 1), NEGATIVE, 0.0)
            hidden = jnp.where(pad_row - 30 == 1 - query_half, floor, 0.0)
            hidden = jnp.where(pad_row >= 30, hidden, 0.0)
        queries = dot_nt(wt1[0:WIDE, :], normed[w])
        for h in range(HEADS):
            qmt[w, h] = head_rows((queries[own_rows(h), :] + hidden).astype(BF16), h)
        keys = dot_nt(normed[w], wt1[WIDE : 2 * WIDE, :])
        kk[w] = jnp.where(marks, 1.0, keys).astype(BF16)
        vt[w] = dot_nt(wt1[2 * WIDE :, :], normed[w]).astype(BF16)
    for w in range(4):
        for h in range(HEADS):
            half = h // 4 * 128
            s1[w, h] = dot(kk[w, :, half : half + 128], qmt[w, h])
    for w in range(4):
        for h in range(HEADS):
            scores = s1.at[w, h]
            peak = add_bias(scores, 32, 8, functools.partial(window_bias, h))
            inverse1[w, h] = raise_all(scores, 32, 8, peak, p1.at[w], own_columns(h), False)
    for w in range(4):
        for h in range(HEADS):
            heads_t = dot(vt[w, own_rows(h), :], p1[w, :, own_columns(h)])
            ot[w, own_rows(h), :] = heads_t * inverse1[w, h]
        ot[w, HEADS * HEAD_PAD :, :] = jnp.zeros((WIDE - HEADS * HEAD_PAD, CELLS), F32)
    for w in range(4):
        heads_out = jnp.transpose(ot[w]).astype(BF16)
        middle = feats[w] + dot(heads_out, pp1[...])
        middles[w] = middle.reshape(8, 2, 2, 8, CHANNELS)

    y_runs = ((0, 0, 4, 8, 0), (0, 1, 0, 8, 4), (1, 0, 0, 8, 12), (1, 1, 0, 4, 20))
    for wy, sy, first, last, place in y_runs:
        for wx in range(2):
            for sx in range(2):
                start = (2 * wx + sx) * 8
                lin[place : place + last - first, start : start + 8, :] = middles[
                    2 * wy + wx, first:last, sy, sx
                ]

    for i in range(KEY_SIDE // 2):
        lines, rows = slice(2 * i, 2 * i + 2), slice(64 * i, 64 * i + 64)
        unit, inverse = norm_parts(lin[lines].reshape(64, CHANNELS))
        units[rows, :] = unit
        inverses[rows, :] = inverse
        normal = (unit * gain2).astype(BF16).astype(F32)
        lin[lines] = normal.reshape(2, 32, CHANNELS)
    inside_low = jnp.where(lat > 0, 1.0, 0.0)
    inside_high = jnp.where(lat < n_lat - 1, 1.0, 0.0)
    lin[0:4] = lin[0:4] * inside_low
    lin[20:24] = lin[20:24] * inside_high
    keys_in = lin[:, 4:28, :].reshape(KEYS, CHANNELS).astype(BF16)
    k2[...] = dot_nt(keys_in, wt2[WIDE : 2 * WIDE, :]).astype(BF16)
    v2[...] = dot_nt(keys_in, wt2[2 * WIDE :, :]).astype(BF16)
    k2t[...] = dot_nt(wt2[WIDE : 2 * WIDE, :], keys_in).astype(BF16)

    def own_part(sy, sx):
        return slice(4 + 8 * sy, 12 + 8 * sy), slice(8 + 8 * sx, 16 + 8 * sx)

    own_second = jnp.concatenate(
        [lin[(*own_part(sy, sx), slice(None))].reshape(64, CHANNELS) for sy, sx, w, s in OWN],
        axis=0,
    )
    queries_in = dot(turn[0], own_second.astype(BF16)).astype(BF16)
    cot = cot_ref[...].astype(F32)
    cot_own = [
        cot[8 * sy : 8 * sy + 8, 8 * sx : 8 * sx + 8, :].reshape(64, CHANNELS)
        for sy, sx, w, s in OWN
    ]
    cot_in = dot(turn[0], jnp.concatenate(cot_own, axis=0).astype(BF16)).astype(BF16)
    queries_t = dot_nt(wt2[0:WIDE, :], queries_in).astype(BF16)
    gt[...] = dot_nt(pp2[...], cot_in)
    for h in range(HEADS):
        qmt[0, h] = head_rows(queries_t[h * HEAD_PAD : (h + 1) * HEAD_PAD, :], h)
    head_lanes(dot_nt(queries_in, wt2[0:WIDE, :]), qm)

    def bias(h, c):
        return jnp.concatenate([cross_bias(h, 2 * c), cross_bias(h, 2 * c + 1)], axis=0)

    for h in range(HEADS):
        half = h // 4 * 128
        s2[h] = dot(k2[:, half : half + 128], qmt[0, h])
    inverse2 = []
    for h in range(HEADS):
        half = h // 4 * 128
        peak = add_bias(s2.at[h], 48, 12, functools.partial(bias, h))
        inverse2.append(raise_all(s2.at[h], 48, 12, peak, p2, own_columns(h), True))
        scaled = gt[own_rows(h), :] * inverse2[h]
        gt[own_rows(h), :] = scaled
        g2[h] = dot(v2[:, half : half + 128], head_rows(scaled.astype(BF16), h))
    for h in range(HEADS):

        def raised(part):
            return s2[h, part, :]

        total = weigh_all(raised, g2.at[h], 48, 12, inverse2[h])
        slope_all(raised, g2.at[h], 48, 12, total, s2.at[h], ds2, own_columns(h))
    for h in range(HEADS):
        ot[0, own_rows(h), :] = dot(k2t[own_rows(h), :], ds2[:, own_columns(h)])
    head_lanes(jnp.transpose(gt[...]), dom)
    grad_queries = (jnp.transpose(ot[0]) * SCALE).astype(BF16)
    grad_keys = (dot(ds2[...], qm[...]) * SCALE).astype(BF16)
    grad_values = dot(p2[...], dom[...]).astype(BF16)
    grad_second = dot(grad_keys, wt2[WIDE : 2 * WIDE, :]) + dot(grad_values, wt2[2 * WIDE :, :])
    grad_own = dot(turn[1], dot(grad_queries, wt2[0:WIDE, :]).astype(BF16))

    lin[...] = jnp.zeros(lin.shape, F32)
    lin[:, 4:28, :] = grad_second.reshape(KEY_SIDE, KEY_SIDE, CHANNELS)
    lin[0:4] = lin[0:4] * inside_low
    lin[20:24] = lin[20:24] * inside_high
    for i, (sy, sx, w, s) in enumerate(OWN):
        place = (*own_part(sy, sx), slice(None))
        lin[place] = lin[place] + grad_own[64 * i : 64 * i + 64, :].reshape(8, 8, CHANNELS)

    for i in range(KEY_SIDE // 2):
        lines, rows = slice(2 * i, 2 * i + 2), slice(64 * i, 64 * i + 64)
        grad = lin[lines].reshape(64, CHANNELS)
        grad = norm_back(units[rows, :], inverses[rows, :], gain2, grad)
        lin[lines] = grad.reshape(2, 32, CHANNELS)
    for i, (sy, sx, w, s) in enumerate(OWN):
        place = (*own_part(sy, sx), slice(None))
        lin[place] = lin[place] + cot_own[i].reshape(8, 8, CHANNELS)
    for w in range(3):
        rows, cols = 12 * (w // 2), 16 * (w % 2)
        piece = lin[rows : rows + 12, cols : cols + 16, :]
        mid_out[w, :, :CHANNELS] = piece.reshape(192, CHANNELS).astype(BF16)
        pltpu.make_async_remote_copy(
            src_ref=mid_out.at[w],
            dst_ref=mid_in.at[w],
            send_sem=mid_send,
            recv_sem=mid_recv,
            device_id=at(w // 2 - 1, w % 2 - 1),
            device_id_type=MESH,
        ).start()

    def sum_scatter(kind, tiles, buffer):
        chunks, depth = buffer_plan(tiles, n_lat)
        for c in range(chunks):

            @pl.when(lat != c)
            def _():
                pltpu.make_async_remote_copy(
                    src_ref=tiles.at[pl.ds(c * depth, depth)],
                    dst_ref=buffer.at[wrapped(lat - c, n_lat) - 1],
                    send_sem=sum_send.at[kind],
                    recv_sem=sum_recv.at[kind],
                    device_id=(lon, c),
                    device_id_type=MESH,
                ).start()

    def drain(sem, ref):
        pltpu.make_async_copy(ref, ref, sem).wait()

    def sum_spread(kind, tiles, buffer, rows):
        chunks, depth = buffer_plan(tiles, n_lat)

        @pl.when(lat < chunks)
        def _():
            drain(sum_recv.at[kind], buffer)
            total = tiles[pl.ds(lat * depth, depth)]
            for i in range(n_lat - 1):
                total = total + buffer[i]
            rows[spot] = total
            for j in range(1, inner):
                pltpu.make_async_remote_copy(
                    src_ref=rows.at[spot],
                    dst_ref=rows.at[spot],
                    send_sem=sum_send.at[kind + 1],
                    recv_sem=sum_recv.at[kind + 1],
                    device_id=inner_peer(j),
                    device_id_type=MESH,
                ).start()

    def sum_cross(kind, tiles, rows, far):
        chunks, depth = buffer_plan(tiles, n_lat)
        block = lax.div(lon, inner)

        @pl.when(lat < chunks)
        def _():
            drain(sum_recv.at[kind + 1], rows.at[pl.ds(0, inner - 1)])
            total = rows[0]
            for i in range(1, inner):
                total = total + rows[i]
            far[block] = total
            for j in range(1, outer):
                pltpu.make_async_remote_copy(
                    src_ref=far.at[block],
                    dst_ref=far.at[block],
                    send_sem=sum_send.at[kind + 2],
                    recv_sem=sum_recv.at[kind + 2],
                    device_id=at(0, j * inner),
                    device_id_type=MESH,
                ).start()

    def sum_gather(kind, tiles, far, result):
        chunks, depth = buffer_plan(tiles, n_lat)

        @pl.when(lat < chunks)
        def _():
            if outer > 1:
                drain(sum_recv.at[kind + 2], far.at[pl.ds(0, outer - 1)])
            total = far[0]
            for i in range(1, outer):
                total = total + far[i]
            result[lat] = total
            for j in range(1, n_lat):
                pltpu.make_async_remote_copy(
                    src_ref=result.at[lat],
                    dst_ref=result.at[lat],
                    send_sem=sum_send.at[kind + 3],
                    recv_sem=sum_recv.at[kind + 3],
                    device_id=at(j, 0),
                    device_id_type=MESH,
                ).start()

    def sum_end(kind, tiles, buffer, rows, far, result):
        chunks, depth = buffer_plan(tiles, n_lat)

        @pl.when(lat < chunks)
        def _():
            if chunks > 1:
                drain(sum_recv.at[kind + 3], result.at[pl.ds(0, chunks - 1)])
                drain(sum_send.at[kind], result.at[pl.ds(0, chunks - 1)])
            drain(sum_send.at[kind + 1], rows.at[pl.ds(0, inner - 1)])
            if outer > 1:
                drain(sum_send.at[kind + 2], far.at[pl.ds(0, outer - 1)])
            drain(sum_send.at[kind + 3], buffer)

        @pl.when(lat >= chunks)
        def _():
            drain(sum_recv.at[kind + 3], result)
            drain(sum_send.at[kind], result)

    def joined(result):
        chunks, depth = result.shape[0], result.shape[1]
        return jnp.concatenate(
            [result[c, d] for c in range(chunks) for d in range(depth)], axis=1
        )

    def widened(part, width):
        return jnp.concatenate([part, jnp.zeros((8, width - part.shape[1]), F32)], axis=1)

    for h in range(HEADS):
        for s in range(3):
            collect(acc2, h, s, KEY_SIDE, lambda m: (m * 3 + s) * 8, s2.at[h])

    def gather_cross(group, _):
        for i in range(3):
            h = 3 * group + i
            for s in range(3):
                parts = [widened(acc2[s, r, h], LANES_C) for r in range(4)]
                flat2[s, pl.ds(h, 1), :] = gather_rows(parts, -1)
        return 0

    lax.fori_loop(0, HEADS // 3, gather_cross, 0)
    dense2[...] = jnp.zeros(dense2.shape, F32)
    for dy in range(CROSS):
        for s in range(3):
            start = dy * CROSS + 8 * s
            dense2[s, 0:HEADS, start : start + 23] = flat2[s, :, dy * 32 : dy * 32 + 23]
    for t in range(TILES_C):
        part = pl.ds(128 * t, 128)
        whole = dense2[0, :, part] + dense2[1, :, part] + dense2[2, :, part]
        tiles2[t] = whole
    sum_scatter(0, tiles2, rs2)

    vv[...] = dot_nt(normed[3], wt1[2 * WIDE :, :]).astype(BF16)
    drain(mid_recv, mid_in)
    total = lin[12:24, 16:32, :] + mid_in[2, :, :CHANNELS].astype(F32).reshape(12, 16, CHANNELS)
    below = (mid_in[0, :, :CHANNELS].astype(F32) + mid_in[1, :, :CHANNELS].astype(F32)).reshape(12, 16, CHANNELS)
    total = jnp.concatenate([total[0:4], total[4:12] + below[0:8], below[8:12]], axis=0)
    pair = [total[8 * sy : 8 * sy + 8].reshape(8, 1, 16, CHANNELS) for sy in range(2)]
    grad_mid[...] = jnp.concatenate(pair, axis=1).reshape(CELLS, CHANNELS)

    grads_t = dot_nt(pp1[...], grad_mid[...].astype(BF16))
    for h in range(HEADS):
        scaled = grads_t[own_rows(h), :] * inverse1[3, h]
        gt[own_rows(h), :] = scaled
        half = h // 4 * 128
        s1[1, h] = dot(vv[:, half : half + 128], head_rows(scaled.astype(BF16), h))
    for h in range(HEADS):

        def raised(part):
            return p1[3, part, own_columns(h)].astype(F32)

        total = weigh_all(raised, s1.at[1, h], 32, 8, inverse1[3, h])
        slope_all(raised, s1.at[1, h], 32, 8, total, s1.at[0, h], ds1, own_columns(h))
        for sx in range(2):

            def group_of(m):
                ky = 15 - m
                return (ky % 8 * 4 + ky // 8 * 2 + sx) * 8

            collect(acc1, h, sx, 16, group_of, s1.at[0, h])

    for h in range(HEADS):
        total = None
        for s in range(2):
            parts = [widened(acc1[s, r, h], LANES_W) for r in range(4)]
            piece = roll(gather_rows(parts, 1), 15 - 8 * s)
            total = piece if total is None else total + piece
        flat1[h : h + 1, :] = total
    dense1[...] = jnp.zeros(dense1.shape, F32)
    for dy in range(SPAN):
        dense1[0:HEADS, dy * SPAN : (dy + 1) * SPAN] = flat1[:, dy * 32 : dy * 32 + SPAN]
    for t in range(TILES_W):
        tiles1[t] = dense1[:, 128 * t : 128 * t + 128]
    sum_scatter(4, tiles1, rs1)
    sum_spread(0, tiles2, rs2, ag2)
    kt[...] = dot_nt(wt1[WIDE : 2 * WIDE, :], normed[3]).astype(BF16)
    head_lanes(dot_nt(normed[3], wt1[0:WIDE, :]), qm)

    for h in range(HEADS):
        ot[0, own_rows(h), :] = dot(kt[own_rows(h), :], ds1[:, own_columns(h)])
    head_lanes(jnp.transpose(gt[...]), dom)
    grad_queries = (jnp.transpose(ot[0]) * SCALE).astype(BF16)
    grad_keys = (dot(ds1[...], qm[...]) * SCALE).astype(BF16)
    grad_values = dot(p1[3], dom[...])
    sum_spread(4, tiles1, rs1, ag1)
    sum_cross(0, tiles2, ag2, far2)
    grad_first[...] = (
        dot(grad_queries, wt1[0:WIDE, :])
        + dot(grad_keys, wt1[WIDE : 2 * WIDE, :])
        + dot(grad_values.astype(BF16), wt1[2 * WIDE :, :])
    )
    for c in range(4):
        rows = slice(64 * c, 64 * c + 64)
        unit, inverse = norm_parts(feats[3, rows, :])
        grad = grad_mid[rows, :] + norm_back(unit, inverse, gain1, grad_first[rows, :])
        quarters = grad.reshape(2, 2, 2, 8, CHANNELS)
        out_ref[8 + 2 * c : 10 + 2 * c, 8:16, :CHANNELS] = quarters[:, 0, 0]
        for s in (1, 2, 3):
            piece = quarters[:, s // 2, s % 2].reshape(16, CHANNELS)
            back_out[s - 1, 16 * c : 16 * c + 16, :CHANNELS] = piece.astype(BF16)
    for s in (1, 2, 3):
        pltpu.make_async_remote_copy(
            src_ref=back_out.at[s - 1],
            dst_ref=back_in.at[s - 1],
            send_sem=back_send,
            recv_sem=back_recv,
            device_id=at(s // 2, s % 2),
            device_id_type=MESH,
        ).start()
    sum_cross(4, tiles1, ag1, far1)
    sum_gather(0, tiles2, far2, fin2)
    drain(back_recv, back_in)
    out_ref[8:16, 0:8, :CHANNELS] = back_in[0, :, :CHANNELS].astype(F32).reshape(8, 8, CHANNELS)
    out_ref[0:8, 8:16, :CHANNELS] = back_in[1, :, :CHANNELS].astype(F32).reshape(8, 8, CHANNELS)
    out_ref[0:8, 0:8, :CHANNELS] = back_in[2, :, :CHANNELS].astype(F32).reshape(8, 8, CHANNELS)
    store = pltpu.make_async_copy(out_ref, out_hbm, load_sem.at[0])
    store.start()
    sum_gather(4, tiles1, far1, fin1)
    sum_end(0, tiles2, rs2, ag2, far2, fin2)
    out2_ref[...] = joined(fin2)
    store2 = pltpu.make_async_copy(out2_ref, out2_hbm, load_sem.at[1])
    store2.start()
    sum_end(4, tiles1, rs1, ag1, far1, fin1)
    out1_ref[...] = joined(fin1)
    store1 = pltpu.make_async_copy(out1_ref, out1_hbm, load_sem.at[2])
    store1.start()
    pltpu.make_async_copy(every, every, halo_send).wait()
    drain(mid_send, mid_out)
    drain(back_send, back_out)
    store.wait()
    store2.wait()
    store1.wait()


def lon_plan(n_lon):
    inner = 8 if n_lon % 8 == 0 else 2 if n_lon % 2 == 0 else n_lon
    return inner, n_lon // inner


def buffer_plan(tiles, n_lat):
    count = tiles.shape[0]
    chunks = min(n_lat, count)
    return chunks, count // chunks


def body(n_lat, n_lon, *operands):
    vmem = pltpu.VMEM
    inner, outer = lon_plan(n_lon)

    def sums(count):
        chunks = min(n_lat, count)
        depth = count // chunks
        return (
            vmem((count, 8, 128), F32),
            vmem((n_lat - 1, depth, 8, 128), F32),
            vmem((inner, depth, 8, 128), F32),
            vmem((outer, depth, 8, 128), F32),
            vmem((chunks, depth, 8, 128), F32),
        )

    tiles1, rs1, ag1, far1, fin1 = sums(TILES_W)
    tiles2, rs2, ag2, far2, fin2 = sums(TILES_C)
    scratch = [
        vmem((16, 16, WIDE), F32),
        vmem((8, 128 * TILES_W), F32),
        vmem((8, 128 * TILES_C), F32),
        vmem((16, 16, CHANNELS), BF16),
        vmem((16, 16, CHANNELS), BF16),
        vmem((1, CHANNELS), F32),
        vmem((CHANNELS, 3 * CHANNELS), BF16),
        vmem((CHANNELS, CHANNELS), BF16),
        vmem((HEADS, SPAN * SPAN), F32),
        vmem((1, CHANNELS), F32),
        vmem((CHANNELS, 3 * CHANNELS), BF16),
        vmem((CHANNELS, CHANNELS), BF16),
        vmem((HEADS, CROSS * CROSS), F32),
        pltpu.SemaphoreType.DMA((10,)),
        vmem((4, 4, 64, WIDE), BF16),
        vmem((HEADS, LANES_W), F32),
        vmem((3, HEADS, LANES_C), F32),
        vmem((3 * WIDE, CHANNELS), BF16),
        vmem((3 * WIDE, CHANNELS), BF16),
        vmem((WIDE, CHANNELS), BF16),
        vmem((WIDE, CHANNELS), BF16),
        vmem((2, CELLS, CELLS), BF16),
        vmem((2, 4, HEADS, 8, USED_W), F32),
        vmem((3, 4, HEADS, 8, USED_C), F32),
        vmem((2, 4, HEADS, 8, USED_W), F32),
        vmem((3, 4, HEADS, 8, USED_C), F32),
        vmem((4, CELLS, CHANNELS), F32),
        vmem((4, 8, 2, 2, 8, CHANNELS), F32),
        vmem((KEY_SIDE * 32, CHANNELS), F32),
        vmem((KEY_SIDE * 32, 1), F32),
        vmem((4, CELLS, WIDE), BF16),
        vmem((4, WIDE, CELLS), BF16),
        vmem((CELLS, WIDE), BF16),
        vmem((WIDE, CELLS), BF16),
        vmem((HEADS * CELLS, WIDE), BF16),
        vmem((HEADS * CELLS, WIDE), BF16),
        vmem((4, HEADS, 128, CELLS), BF16),
        vmem((WIDE, CELLS), F32),
        vmem((4, WIDE, CELLS), F32),
        vmem((4, CELLS, CHANNELS), BF16),
        vmem((4, HEADS, 1, CELLS), F32),
        vmem((4, HEADS, CELLS, CELLS), F32),
        vmem((HEADS, KEYS, CELLS), F32),
        vmem((HEADS, KEYS, CELLS), F32),
        vmem((CELLS, CHANNELS), F32),
        vmem((CELLS, CHANNELS), F32),
        vmem((4, CELLS, HEADS * CELLS), BF16),
        vmem((KEYS, HEADS * CELLS), BF16),
        vmem((CELLS, HEADS * CELLS), BF16),
        vmem((KEYS, HEADS * CELLS), BF16),
        vmem((KEYS, WIDE), BF16),
        vmem((KEYS, WIDE), BF16),
        vmem((WIDE, KEYS), BF16),
        vmem((KEY_SIDE, 32, CHANNELS), F32),
        vmem((3, 192, WIDE), BF16),
        vmem((3, 192, WIDE), BF16),
        vmem((3, 64, WIDE), BF16),
        vmem((3, 64, WIDE), BF16),
        vmem((8, 128 * TILES_W), F32),
        vmem((3, 8, 128 * TILES_C), F32),
        tiles1,
        tiles2,
        rs1,
        rs2,
        ag1,
        ag2,
        far1,
        far2,
        fin1,
        fin2,
        pltpu.SemaphoreType.DMA,
        pltpu.SemaphoreType.DMA,
        pltpu.SemaphoreType.DMA,
        pltpu.SemaphoreType.DMA,
        pltpu.SemaphoreType.DMA,
        pltpu.SemaphoreType.DMA,
        pltpu.SemaphoreType.DMA((8,)),
        pltpu.SemaphoreType.DMA((8,)),
    ]
    hbm = pl.BlockSpec(memory_space=pltpu.HBM)
    limit = 63 * 1024 * 1024
    shapes = (
        jax.ShapeDtypeStruct((16, 16, WIDE), F32),
        jax.ShapeDtypeStruct((8, 128 * TILES_W), F32),
        jax.ShapeDtypeStruct((8, 128 * TILES_C), F32),
    )
    grads, grad1, grad2 = pl.pallas_call(
        functools.partial(kernel, n_lat, n_lon),
        out_shape=shapes,
        in_specs=[hbm] * 10,
        out_specs=(hbm,) * 3,
        scratch_shapes=scratch,
        compiler_params=pltpu.CompilerParams(
            collective_id=0, has_side_effects=True, vmem_limit_bytes=limit
        ),
    )(*operands)
    return (
        grads[:, :, :CHANNELS],
        grad1[:HEADS, : SPAN * SPAN],
        grad2[:HEADS, : CROSS * CROSS],
    )


def solution(mesh):
    def local(
        features,
        cotangent,
        first_gain,
        window_qkv,
        window_proj,
        window_table,
        second_gain,
        cross_qkv,
        cross_proj,
        cross_table,
    ):
        return body(
            mesh.shape["lat"],
            mesh.shape["lon"],
            features,
            cotangent,
            first_gain.reshape(1, CHANNELS),
            window_qkv,
            window_proj,
            window_table,
            second_gain.reshape(1, CHANNELS),
            cross_qkv,
            cross_proj,
            cross_table,
        )

    return jax.shard_map(
        local,
        mesh=mesh,
        in_specs=(
            P("lat", "lon", None),
            P("lat", "lon", None),
            P(),
            P(),
            P(),
            P(),
            P(),
            P(),
            P(),
            P(),
        ),
        out_specs=(P("lat", "lon", None), P(), P()),
        check_vma=False,
    )
```

```python
import functools

import jax
import jax.numpy as jnp
from jax import lax
from jax.experimental import pallas as pl
from jax.experimental.pallas import tpu as pltpu
from jax.sharding import PartitionSpec as P

CHANNELS = 180
HEADS = 6
HEAD_SIZE = 30
HEAD_PAD = 32
WIDE = 256
CELLS = 256
KEYS = 576
KEY_SIDE = 24
SPAN = 31
CROSS = 39
EPSILON = 1e-05
NEGATIVE = -1e30
LOG2E = 1.4426950408889634
SCALE = HEAD_SIZE**-0.5
TILES_W = 8
TILES_C = 12
LANES_W = 1024
LANES_C = 1280
USED_W = 640
USED_C = 896
MESH = pl.DeviceIdType.MESH
F32 = jnp.float32
BF16 = jnp.bfloat16


def iota(shape, dim):
    return lax.broadcasted_iota(jnp.int32, shape, dim)


def dot(a, b):
    return jnp.dot(a, b, preferred_element_type=F32)


def dot_nt(a, b):
    return lax.dot_general(a, b, (((1,), (1,)), ((), ())), preferred_element_type=F32)


def one_hot(mask):
    return jnp.where(mask, 1.0, 0.0).astype(BF16)


def roll(x, shift):
    size = x.shape[-1]
    return pltpu.roll(x, shift % size, x.ndim - 1)


def norm_parts(values):
    centre = jnp.mean(values, axis=-1, keepdims=True)
    offset = values - centre
    spread = jnp.mean(offset * offset, axis=-1, keepdims=True)
    inverse = lax.rsqrt(spread + EPSILON)
    return offset * inverse, inverse


def norm_back(unit, inverse, gain, grads):
    scaled = grads * gain
    first = jnp.mean(scaled, axis=-1, keepdims=True)
    second = jnp.mean(scaled * unit, axis=-1, keepdims=True)
    return inverse * (scaled - first - unit * second)


OWN = [(sy, sx, 2 * sy + sx, (1 - sy) * 2 + (1 - sx)) for sy in (0, 1) for sx in (0, 1)]


def spread_rows(base, stride, ways):
    rows = iota(base.shape, 0)
    for bit in (1, 2, 4):
        base = jnp.where((rows & bit) != 0, roll(base, stride * bit), base)
    upper = (iota(base.shape, 1) & 16) != 0
    base = jnp.where(upper, roll(base, -240), base)
    return [base if r == 0 else roll(base, -32 * r) for r in range(ways)]


def gather_rows(parts, stride):
    total = parts[0]
    for r in range(1, len(parts)):
        total = total + roll(parts[r], 32 * r)
    upper = (iota(total.shape, 1) & 16) != 0
    total = jnp.where(upper, 0.0, total) + roll(jnp.where(upper, total, 0.0), 240)
    rows = iota(total.shape, 0)
    for bit in (1, 2, 4):
        total = jnp.where((rows & bit) != 0, roll(total, -stride * bit), total)
    return jnp.sum(total, axis=0, keepdims=True)


def kernel(
    n_lat,
    n_lon,
    feat_in,
    cot_in_hbm,
    gain1_in,
    qkv1_in,
    proj1_in,
    tab1_in,
    gain2_in,
    qkv2_in,
    proj2_in,
    tab2_in,
    out_hbm,
    out1_hbm,
    out2_hbm,
    out_ref,
    out1_ref,
    out2_ref,
    feat_ref,
    cot_ref,
    gain1_ref,
    qkv1_ref,
    proj1_ref,
    tab1_ref,
    gain2_ref,
    qkv2_ref,
    proj2_ref,
    tab2_ref,
    load_sem,
    region,
    flat1,
    flat2,
    wt1,
    wt2,
    pp1,
    pp2,
    turn,
    z1,
    z2,
    acc1,
    acc2,
    feats,
    middles,
    units,
    inverses,
    kk,
    vt,
    vv,
    kt,
    qm,
    dom,
    qmt,
    gt,
    ot,
    normed,
    inverse1,
    s1,
    s2,
    g2,
    grad_mid,
    grad_first,
    p1,
    p2,
    ds1,
    ds2,
    k2,
    v2,
    k2t,
    lin,
    mid_out,
    mid_in,
    back_out,
    back_in,
    dense1,
    dense2,
    tiles1,
    tiles2,
    rs1,
    rs2,
    ag1,
    ag2,
    far1,
    far2,
    fin1,
    fin2,
    halo_send,
    halo_recv,
    mid_send,
    mid_recv,
    back_send,
    back_recv,
    sum_send,
    sum_recv,
):
    lat = lax.axis_index("lat")
    lon = lax.axis_index("lon")

    def wrapped(value, count):
        value = jnp.where(value >= count, value - count, value)
        return jnp.where(value < 0, value + count, value)

    def at(dy, dx):
        return (wrapped(lon + dx, n_lon), wrapped(lat + dy, n_lat))

    loads = [
        pltpu.make_async_copy(src, dst, load_sem.at[i])
        for i, (src, dst) in enumerate(
            (
                (feat_in, feat_ref),
                (qkv1_in, qkv1_ref),
                (proj1_in, proj1_ref),
                (qkv2_in, qkv2_ref),
                (proj2_in, proj2_ref),
                (tab1_in, tab1_ref),
                (tab2_in, tab2_ref),
                (gain1_in, gain1_ref),
                (gain2_in, gain2_ref),
                (cot_in_hbm, cot_ref),
            )
        )
    ]
    for load in loads:
        load.start()

    barrier = pltpu.get_barrier_semaphore()

    def greet(dy, dx):
        pl.semaphore_signal(barrier, inc=1, device_id=at(dy, dx), device_id_type=MESH)

    for dy in (-1, 0, 1):
        for dx in (-1, 0, 1):
            if dy or dx:
                greet(dy, dx)
    for j in range(2, n_lat - 1):
        greet(j, 0)
    inner, outer = lon_plan(n_lon)
    spot = lax.rem(lon, inner)

    def inner_peer(j):
        return (lon - spot + wrapped(spot + j, inner), lat)

    def greet_at(device):
        pl.semaphore_signal(barrier, inc=1, device_id=device, device_id_type=MESH)

    for j in range(1, inner):
        greet_at(inner_peer(j))
    for j in range(1, outer):
        greet(0, j * inner)

    loads[0].wait()
    own = feat_ref[...].astype(F32)
    for sy, sx, w, s in OWN:
        quarter = own[8 * sy : 8 * sy + 8, 8 * sx : 8 * sx + 8, :].reshape(64, CHANNELS)
        region[1 + sy, 1 + sx, :, :CHANNELS] = quarter.astype(BF16)

    for load in loads[1:7]:
        load.wait()

    for i in range(3):
        lane = iota((WIDE, 1), 0)
        real = (lane < 192) & ((lane & 31) < HEAD_SIZE)
        source = jnp.where(real, CHANNELS * i + lane - 2 * (lane >> 5), -1)
        pick = one_hot(iota((WIDE, 3 * CHANNELS), 1) == source)
        rows = slice(i * WIDE, (i + 1) * WIDE)
        wt1[rows, :] = dot_nt(pick, qkv1_ref[...]).astype(BF16)
        wt2[rows, :] = dot_nt(pick, qkv2_ref[...]).astype(BF16)
        if i == 0:
            pp1[...] = dot(pick[:, :CHANNELS], proj1_ref[...]).astype(BF16)
            pp2[...] = dot(pick[:, :CHANNELS], proj2_ref[...]).astype(BF16)

    pl.semaphore_wait(barrier, 8 + n_lat - 3 + inner - 1 + outer - 1)

    def side(step):
        here = {-1: 1, 0: pl.ds(1, 2), 1: 2}[step]
        there = {-1: 3, 0: pl.ds(1, 2), 1: 0}[step]
        return here, there

    for dy in (-1, 0, 1):
        for dx in (-1, 0, 1):
            if dy == 0 and dx == 0:
                continue
            (a, a_there), (b, b_there) = side(dy), side(dx)
            pltpu.make_async_remote_copy(
                src_ref=region.at[a, b],
                dst_ref=region.at[a_there, b_there],
                send_sem=halo_send,
                recv_sem=halo_recv,
                device_id=at(dy, dx),
                device_id_type=MESH,
            ).start()

    for load in loads[7:]:
        load.wait()

    def turned(c):
        r = 255 - c
        return ((r >> 3) & 7) * 32 + ((r >> 7) & 1) * 16 + ((r >> 6) & 1) * 8 + (r & 7)

    turn[0] = one_hot(iota((CELLS, CELLS), 0) == turned(iota((1, CELLS), 1)))
    turn[1] = one_hot(iota((CELLS, CELLS), 1) == turned(iota((CELLS, 1), 0)))

    flat1[...] = jnp.zeros(flat1.shape, F32)
    flat2[...] = jnp.zeros(flat2.shape, F32)
    for dy in range(SPAN):
        flat1[:, dy * 32 : dy * 32 + SPAN] = tab1_ref[:, dy * SPAN : (dy + 1) * SPAN]
    for dy in range(CROSS):
        for s in range(3):
            start = dy * CROSS + 8 * s
            flat2[s, :, dy * 32 : dy * 32 + 23] = tab2_ref[:, start : start + 23]
    def spread(group):
        for i in range(3):
            h = 3 * group + i
            row = pl.ds(h, 1)
            for s in range(2):
                base = jnp.broadcast_to(flat1[row, :] * LOG2E, (8, LANES_W))
                for r, part in enumerate(spread_rows(roll(base, 8 * s - 15), 1, 4)):
                    z1[s, r, h] = part[:, :USED_W]
            for s in range(3):
                base = jnp.broadcast_to(flat2[s, row, :] * LOG2E, (8, LANES_C))
                for r, part in enumerate(spread_rows(base, -1, 4)):
                    z2[s, r, h] = part[:, :USED_C]

    for group in range(HEADS // 3):
        spread(group)
    query_half = (iota((1, CELLS), 1) >> 4) & 1

    def window_bias(h, y8):
        pieces = []
        for sy in range(2):
            t, r = divmod(15 - (8 * sy + y8), 4)
            for sx in range(2):
                pieces.append(z1[sx, r, h, :, 128 * t : 128 * t + CELLS])
        return jnp.concatenate(pieces, axis=0)

    def cross_bias(h, ky):
        t, r = divmod(ky, 4)
        pieces = [z2[s, r, h, :, 128 * t : 128 * t + CELLS] for s in range(3)]
        return jnp.concatenate(pieces, axis=0)

    def by_eight(values):
        return values.reshape(values.shape[0] // 8, 8, CELLS)

    def add_bias(scores, step, count, bias):
        peak = None
        for c in range(count):
            rows = slice(c * step, (c + 1) * step)
            part = scores[rows, :] * (SCALE * LOG2E) + bias(c)
            scores[rows, :] = part
            part = jnp.max(by_eight(part), axis=0)
            peak = part if peak is None else jnp.maximum(peak, part)
        return jnp.max(peak, axis=0, keepdims=True)

    def raise_all(scores, step, count, peak, probs, columns, keep):
        total = None
        for c in range(count):
            rows = slice(c * step, (c + 1) * step)
            part = jnp.exp2(scores[rows, :] - peak)
            probs[rows, columns] = part.astype(BF16)
            if keep:
                scores[rows, :] = part
            part = jnp.sum(by_eight(part), axis=0)
            total = part if total is None else total + part
        return 1.0 / jnp.sum(total, axis=0, keepdims=True)

    def weigh_all(raised, grads, step, count, inverse):
        total = None
        for c in range(count):
            rows = slice(c * step, (c + 1) * step)
            part = raised(rows) * grads[rows, :]
            grads[rows, :] = part
            part = jnp.sum(by_eight(part), axis=0)
            total = part if total is None else total + part
        return jnp.sum(total, axis=0, keepdims=True) * inverse

    def slope_all(raised, grads, step, count, total, slopes, packed, columns):
        for c in range(count):
            rows = slice(c * step, (c + 1) * step)
            part = grads[rows, :] - raised(rows) * total
            slopes[rows, :] = part
            packed[rows, columns] = part.astype(BF16)

    def collect(acc, h, s, count, group_of, slopes):
        for r in range(4):
            for t in range(count // 4 + 1):
                parts = []
                if t < count // 4:
                    group = group_of(4 * t + r)
                    parts.append(slopes[group : group + 8, 0:128])
                if t > 0:
                    group = group_of(4 * t - 4 + r)
                    parts.append(slopes[group : group + 8, 128:256])
                acc[s, r, h, :, 128 * t : 128 * t + 128] = sum(parts[1:], parts[0])

    def head_rows(rows, h):
        before = h % 4 * HEAD_PAD
        pieces = [rows]
        if before:
            pieces = [jnp.zeros((before, CELLS), rows.dtype)] + pieces
        if before + HEAD_PAD < 128:
            pieces.append(jnp.zeros((128 - HEAD_PAD - before, CELLS), rows.dtype))
        return jnp.concatenate(pieces, axis=0) if len(pieces) > 1 else rows

    def head_lanes(values, into):
        zeros = jnp.zeros((CELLS, 128), BF16)
        for h in range(HEADS):
            half = h // 4 * 128
            lanes = iota((CELLS, 128), 1) >> 5
            own_lanes = jnp.where(lanes == h % 4, values[:, half : half + 128], 0.0).astype(BF16)
            rows = slice(h * CELLS, (h + 1) * CELLS)
            into[rows, half : half + 128] = own_lanes
            into[rows, 128 - half : 256 - half] = zeros

    cot = cot_ref[...].astype(F32)
    cot_own = [
        cot[8 * sy : 8 * sy + 8, 8 * sx : 8 * sx + 8, :].reshape(64, CHANNELS)
        for sy, sx, w, s in OWN
    ]
    cot_in = dot(turn[0], jnp.concatenate(cot_own, axis=0).astype(BF16)).astype(BF16)
    gt[...] = dot_nt(pp2[...], cot_in)

    every = region.at[pl.ds(0, 3)]
    pltpu.make_async_copy(every, every, halo_recv).wait()

    gain1 = gain1_ref[...]
    gain2 = gain2_ref[...]

    key_half = 30 + ((iota((CELLS, 1), 0) >> 4) & 1)
    lane_row = iota((1, WIDE), 1)
    marks = key_half == jnp.where(lane_row < 192, lane_row & 31, 0)
    pad_row = iota((HEAD_PAD, CELLS), 0)

    def own_columns(h):
        return slice(h * CELLS, (h + 1) * CELLS)

    def own_rows(h):
        return slice(h * HEAD_PAD, (h + 1) * HEAD_PAD)

    for w in range(4):
        for c in range(4):
            parts = [
                region[w // 2 * 2 + s // 2, w % 2 * 2 + s % 2, 16 * c : 16 * c + 16, :CHANNELS]
                .astype(F32)
                .reshape(2, 1, 8, CHANNELS)
                for s in range(4)
            ]
            values = jnp.concatenate(parts, axis=1).reshape(64, CHANNELS)
            rows = slice(64 * c, 64 * c + 64)
            feats[w, rows, :] = values
            unit, _ = norm_parts(values)
            normed[w, rows, :] = (unit * gain1).astype(BF16)
    for w in range(4):
        if w % 2 == 0:
            floor = jnp.where(lat == (0 if w == 0 else n_lat - 1), NEGATIVE, 0.0)
            hidden = jnp.where(pad_row - 30 == 1 - query_half, floor, 0.0)
            hidden = jnp.where(pad_row >= 30, hidden, 0.0)
        queries = dot_nt(wt1[0:WIDE, :], normed[w])
        for h in range(HEADS):
            qmt[w, h] = head_rows((queries[own_rows(h), :] + hidden).astype(BF16), h)
        keys = dot_nt(normed[w], wt1[WIDE : 2 * WIDE, :])
        kk[w] = jnp.where(marks, 1.0, keys).astype(BF16)
        vt[w] = dot_nt(wt1[2 * WIDE :, :], normed[w]).astype(BF16)
    for w in range(4):
        for h in range(HEADS):
            half = h // 4 * 128
            s1[w, h] = dot(kk[w, :, half : half + 128], qmt[w, h])
    for w in range(4):
        for h in range(HEADS):
            scores = s1.at[w, h]
            peak = add_bias(scores, 32, 8, functools.partial(window_bias, h))
            inverse1[w, h] = raise_all(scores, 32, 8, peak, p1.at[w], own_columns(h), False)
    for w in range(4):
        for h in range(HEADS):
            heads_t = dot(vt[w, own_rows(h), :], p1[w, :, own_columns(h)])
            ot[w, own_rows(h), :] = heads_t * inverse1[w, h]
        ot[w, HEADS * HEAD_PAD :, :] = jnp.zeros((WIDE - HEADS * HEAD_PAD, CELLS), F32)
    for w in range(4):
        heads_out = jnp.transpose(ot[w]).astype(BF16)
        middle = feats[w] + dot(heads_out, pp1[...])
        middles[w] = middle.reshape(8, 2, 2, 8, CHANNELS)

    y_runs = ((0, 0, 4, 8, 0), (0, 1, 0, 8, 4), (1, 0, 0, 8, 12), (1, 1, 0, 4, 20))
    for wy, sy, first, last, place in y_runs:
        for wx in range(2):
            for sx in range(2):
                start = (2 * wx + sx) * 8
                lin[place : place + last - first, start : start + 8, :] = middles[
                    2 * wy + wx, first:last, sy, sx
                ]

    for i in range(KEY_SIDE // 2):
        lines, rows = slice(2 * i, 2 * i + 2), slice(64 * i, 64 * i + 64)
        unit, inverse = norm_parts(lin[lines].reshape(64, CHANNELS))
        units[rows, :] = unit
        inverses[rows, :] = inverse
        normal = (unit * gain2).astype(BF16).astype(F32)
        lin[lines] = normal.reshape(2, 32, CHANNELS)
    inside_low = jnp.where(lat > 0, 1.0, 0.0)
    inside_high = jnp.where(lat < n_lat - 1, 1.0, 0.0)
    lin[0:4] = lin[0:4] * inside_low
    lin[20:24] = lin[20:24] * inside_high
    keys_in = lin[:, 4:28, :].reshape(KEYS, CHANNELS).astype(BF16)
    k2[...] = dot_nt(keys_in, wt2[WIDE : 2 * WIDE, :]).astype(BF16)
    v2[...] = dot_nt(keys_in, wt2[2 * WIDE :, :]).astype(BF16)
    k2t[...] = dot_nt(wt2[WIDE : 2 * WIDE, :], keys_in).astype(BF16)

    def own_part(sy, sx):
        return slice(4 + 8 * sy, 12 + 8 * sy), slice(8 + 8 * sx, 16 + 8 * sx)

    own_second = jnp.concatenate(
        [lin[(*own_part(sy, sx), slice(None))].reshape(64, CHANNELS) for sy, sx, w, s in OWN],
        axis=0,
    )
    queries_in = dot(turn[0], own_second.astype(BF16)).astype(BF16)
    queries_t = dot_nt(wt2[0:WIDE, :], queries_in).astype(BF16)
    for h in range(HEADS):
        qmt[0, h] = head_rows(queries_t[h * HEAD_PAD : (h + 1) * HEAD_PAD, :], h)
    head_lanes(dot_nt(queries_in, wt2[0:WIDE, :]), qm)

    def bias(h, c):
        return jnp.concatenate([cross_bias(h, 2 * c), cross_bias(h, 2 * c + 1)], axis=0)

    for h in range(HEADS):
        half = h // 4 * 128
        s2[h] = dot(k2[:, half : half + 128], qmt[0, h])
    inverse2 = []
    for h in range(HEADS):
        half = h // 4 * 128
        peak = add_bias(s2.at[h], 48, 12, functools.partial(bias, h))
        inverse2.append(raise_all(s2.at[h], 48, 12, peak, p2, own_columns(h), True))
        scaled = gt[own_rows(h), :] * inverse2[h]
        gt[own_rows(h), :] = scaled
        g2[h] = dot(v2[:, half : half + 128], head_rows(scaled.astype(BF16), h))
    for h in range(HEADS):

        def raised(part):
            return s2[h, part, :]

        total = weigh_all(raised, g2.at[h], 48, 12, inverse2[h])
        slope_all(raised, g2.at[h], 48, 12, total, s2.at[h], ds2, own_columns(h))
    for h in range(HEADS):
        ot[0, own_rows(h), :] = dot(k2t[own_rows(h), :], ds2[:, own_columns(h)])
    head_lanes(jnp.transpose(gt[...]), dom)
    grad_queries = (jnp.transpose(ot[0]) * SCALE).astype(BF16)
    grad_keys = (dot(ds2[...], qm[...]) * SCALE).astype(BF16)
    grad_values = dot(p2[...], dom[...]).astype(BF16)
    grad_second = dot(grad_keys, wt2[WIDE : 2 * WIDE, :]) + dot(grad_values, wt2[2 * WIDE :, :])
    grad_own = dot(turn[1], dot(grad_queries, wt2[0:WIDE, :]).astype(BF16))

    lin[...] = jnp.zeros(lin.shape, F32)
    lin[:, 4:28, :] = grad_second.reshape(KEY_SIDE, KEY_SIDE, CHANNELS)
    lin[0:4] = lin[0:4] * inside_low
    lin[20:24] = lin[20:24] * inside_high
    for i, (sy, sx, w, s) in enumerate(OWN):
        place = (*own_part(sy, sx), slice(None))
        lin[place] = lin[place] + grad_own[64 * i : 64 * i + 64, :].reshape(8, 8, CHANNELS)

    for i in range(KEY_SIDE // 2):
        lines, rows = slice(2 * i, 2 * i + 2), slice(64 * i, 64 * i + 64)
        grad = lin[lines].reshape(64, CHANNELS)
        grad = norm_back(units[rows, :], inverses[rows, :], gain2, grad)
        lin[lines] = grad.reshape(2, 32, CHANNELS)
    for i, (sy, sx, w, s) in enumerate(OWN):
        place = (*own_part(sy, sx), slice(None))
        lin[place] = lin[place] + cot_own[i].reshape(8, 8, CHANNELS)
    for w in range(3):
        rows, cols = 12 * (w // 2), 16 * (w % 2)
        piece = lin[rows : rows + 12, cols : cols + 16, :]
        mid_out[w, :, :CHANNELS] = piece.reshape(192, CHANNELS).astype(BF16)
        pltpu.make_async_remote_copy(
            src_ref=mid_out.at[w],
            dst_ref=mid_in.at[w],
            send_sem=mid_send,
            recv_sem=mid_recv,
            device_id=at(w // 2 - 1, w % 2 - 1),
            device_id_type=MESH,
        ).start()

    def sum_scatter(kind, tiles, buffer):
        chunks, depth = buffer_plan(tiles, n_lat)
        for c in range(chunks):

            @pl.when(lat != c)
            def _():
                pltpu.make_async_remote_copy(
                    src_ref=tiles.at[pl.ds(c * depth, depth)],
                    dst_ref=buffer.at[wrapped(lat - c, n_lat) - 1],
                    send_sem=sum_send.at[kind],
                    recv_sem=sum_recv.at[kind],
                    device_id=(lon, c),
                    device_id_type=MESH,
                ).start()

    def drain(sem, ref):
        pltpu.make_async_copy(ref, ref, sem).wait()

    def sum_spread(kind, tiles, buffer, rows):
        chunks, depth = buffer_plan(tiles, n_lat)

        @pl.when(lat < chunks)
        def _():
            drain(sum_recv.at[kind], buffer)
            total = tiles[pl.ds(lat * depth, depth)]
            for i in range(n_lat - 1):
                total = total + buffer[i]
            rows[spot] = total
            for j in range(1, inner):
                pltpu.make_async_remote_copy(
                    src_ref=rows.at[spot],
                    dst_ref=rows.at[spot],
                    send_sem=sum_send.at[kind + 1],
                    recv_sem=sum_recv.at[kind + 1],
                    device_id=inner_peer(j),
                    device_id_type=MESH,
                ).start()

    def sum_cross(kind, tiles, rows, far):
        chunks, depth = buffer_plan(tiles, n_lat)
        block = lax.div(lon, inner)

        @pl.when(lat < chunks)
        def _():
            drain(sum_recv.at[kind + 1], rows.at[pl.ds(0, inner - 1)])
            total = rows[0]
            for i in range(1, inner):
                total = total + rows[i]
            far[block] = total
            for j in range(1, outer):
                pltpu.make_async_remote_copy(
                    src_ref=far.at[block],
                    dst_ref=far.at[block],
                    send_sem=sum_send.at[kind + 2],
                    recv_sem=sum_recv.at[kind + 2],
                    device_id=at(0, j * inner),
                    device_id_type=MESH,
                ).start()

    def sum_gather(kind, tiles, far, result):
        chunks, depth = buffer_plan(tiles, n_lat)

        @pl.when(lat < chunks)
        def _():
            if outer > 1:
                drain(sum_recv.at[kind + 2], far.at[pl.ds(0, outer - 1)])
            total = far[0]
            for i in range(1, outer):
                total = total + far[i]
            result[lat] = total
            for j in range(1, n_lat):
                pltpu.make_async_remote_copy(
                    src_ref=result.at[lat],
                    dst_ref=result.at[lat],
                    send_sem=sum_send.at[kind + 3],
                    recv_sem=sum_recv.at[kind + 3],
                    device_id=at(j, 0),
                    device_id_type=MESH,
                ).start()

    def sum_end(kind, tiles, buffer, rows, far, result):
        chunks, depth = buffer_plan(tiles, n_lat)

        @pl.when(lat < chunks)
        def _():
            if chunks > 1:
                drain(sum_recv.at[kind + 3], result.at[pl.ds(0, chunks - 1)])
                drain(sum_send.at[kind], result.at[pl.ds(0, chunks - 1)])
            drain(sum_send.at[kind + 1], rows.at[pl.ds(0, inner - 1)])
            if outer > 1:
                drain(sum_send.at[kind + 2], far.at[pl.ds(0, outer - 1)])
            drain(sum_send.at[kind + 3], buffer)

        @pl.when(lat >= chunks)
        def _():
            drain(sum_recv.at[kind + 3], result)
            drain(sum_send.at[kind], result)

    def joined(result):
        chunks, depth = result.shape[0], result.shape[1]
        return jnp.concatenate(
            [result[c, d] for c in range(chunks) for d in range(depth)], axis=1
        )

    def widened(part, width):
        return jnp.concatenate([part, jnp.zeros((8, width - part.shape[1]), F32)], axis=1)

    for h in range(HEADS):
        for s in range(3):
            collect(acc2, h, s, KEY_SIDE, lambda m: (m * 3 + s) * 8, s2.at[h])

    def gather_cross(group):
        for i in range(3):
            h = 3 * group + i
            for s in range(3):
                parts = [widened(acc2[s, r, h], LANES_C) for r in range(4)]
                flat2[s, pl.ds(h, 1), :] = gather_rows(parts, -1)

    for group in range(HEADS // 3):
        gather_cross(group)
    dense2[...] = jnp.zeros(dense2.shape, F32)
    for dy in range(CROSS):
        for s in range(3):
            start = dy * CROSS + 8 * s
            dense2[s, 0:HEADS, start : start + 23] = flat2[s, :, dy * 32 : dy * 32 + 23]
    for t in range(TILES_C):
        part = pl.ds(128 * t, 128)
        whole = dense2[0, :, part] + dense2[1, :, part] + dense2[2, :, part]
        tiles2[t] = whole
    sum_scatter(0, tiles2, rs2)

    vv[...] = dot_nt(normed[3], wt1[2 * WIDE :, :]).astype(BF16)
    drain(mid_recv, mid_in)
    total = lin[12:24, 16:32, :] + mid_in[2, :, :CHANNELS].astype(F32).reshape(12, 16, CHANNELS)
    below = (mid_in[0, :, :CHANNELS].astype(F32) + mid_in[1, :, :CHANNELS].astype(F32)).reshape(12, 16, CHANNELS)
    total = jnp.concatenate([total[0:4], total[4:12] + below[0:8], below[8:12]], axis=0)
    pair = [total[8 * sy : 8 * sy + 8].reshape(8, 1, 16, CHANNELS) for sy in range(2)]
    grad_mid[...] = jnp.concatenate(pair, axis=1).reshape(CELLS, CHANNELS)

    grads_t = dot_nt(pp1[...], grad_mid[...].astype(BF16))
    for h in range(HEADS):
        scaled = grads_t[own_rows(h), :] * inverse1[3, h]
        gt[own_rows(h), :] = scaled
        half = h // 4 * 128
        s1[1, h] = dot(vv[:, half : half + 128], head_rows(scaled.astype(BF16), h))
    for h in range(HEADS):

        def raised(part):
            return p1[3, part, own_columns(h)].astype(F32)

        total = weigh_all(raised, s1.at[1, h], 32, 8, inverse1[3, h])
        slope_all(raised, s1.at[1, h], 32, 8, total, s1.at[0, h], ds1, own_columns(h))
        for sx in range(2):

            def group_of(m):
                ky = 15 - m
                return (ky % 8 * 4 + ky // 8 * 2 + sx) * 8

            collect(acc1, h, sx, 16, group_of, s1.at[0, h])

    for h in range(HEADS):
        total = None
        for s in range(2):
            parts = [widened(acc1[s, r, h], LANES_W) for r in range(4)]
            piece = roll(gather_rows(parts, 1), 15 - 8 * s)
            total = piece if total is None else total + piece
        flat1[h : h + 1, :] = total
    dense1[...] = jnp.zeros(dense1.shape, F32)
    for dy in range(SPAN):
        dense1[0:HEADS, dy * SPAN : (dy + 1) * SPAN] = flat1[:, dy * 32 : dy * 32 + SPAN]
    for t in range(TILES_W):
        tiles1[t] = dense1[:, 128 * t : 128 * t + 128]
    sum_scatter(4, tiles1, rs1)
    sum_spread(0, tiles2, rs2, ag2)
    kt[...] = dot_nt(wt1[WIDE : 2 * WIDE, :], normed[3]).astype(BF16)
    head_lanes(dot_nt(normed[3], wt1[0:WIDE, :]), qm)

    for h in range(HEADS):
        ot[0, own_rows(h), :] = dot(kt[own_rows(h), :], ds1[:, own_columns(h)])
    head_lanes(jnp.transpose(gt[...]), dom)
    grad_queries = (jnp.transpose(ot[0]) * SCALE).astype(BF16)
    grad_keys = (dot(ds1[...], qm[...]) * SCALE).astype(BF16)
    grad_values = dot(p1[3], dom[...])
    sum_spread(4, tiles1, rs1, ag1)
    sum_cross(0, tiles2, ag2, far2)
    grad_first[...] = (
        dot(grad_queries, wt1[0:WIDE, :])
        + dot(grad_keys, wt1[WIDE : 2 * WIDE, :])
        + dot(grad_values.astype(BF16), wt1[2 * WIDE :, :])
    )
    for c in range(4):
        rows = slice(64 * c, 64 * c + 64)
        unit, inverse = norm_parts(feats[3, rows, :])
        grad = grad_mid[rows, :] + norm_back(unit, inverse, gain1, grad_first[rows, :])
        quarters = grad.reshape(2, 2, 2, 8, CHANNELS)
        out_ref[8 + 2 * c : 10 + 2 * c, 8:16, :CHANNELS] = quarters[:, 0, 0]
        for s in (1, 2, 3):
            piece = quarters[:, s // 2, s % 2].reshape(16, CHANNELS)
            back_out[s - 1, 16 * c : 16 * c + 16, :CHANNELS] = piece.astype(BF16)
    for s in (1, 2, 3):
        pltpu.make_async_remote_copy(
            src_ref=back_out.at[s - 1],
            dst_ref=back_in.at[s - 1],
            send_sem=back_send,
            recv_sem=back_recv,
            device_id=at(s // 2, s % 2),
            device_id_type=MESH,
        ).start()
    sum_cross(4, tiles1, ag1, far1)
    sum_gather(0, tiles2, far2, fin2)
    drain(back_recv, back_in)
    out_ref[8:16, 0:8, :CHANNELS] = back_in[0, :, :CHANNELS].astype(F32).reshape(8, 8, CHANNELS)
    out_ref[0:8, 8:16, :CHANNELS] = back_in[1, :, :CHANNELS].astype(F32).reshape(8, 8, CHANNELS)
    out_ref[0:8, 0:8, :CHANNELS] = back_in[2, :, :CHANNELS].astype(F32).reshape(8, 8, CHANNELS)
    store = pltpu.make_async_copy(out_ref, out_hbm, load_sem.at[0])
    store.start()
    sum_gather(4, tiles1, far1, fin1)
    sum_end(0, tiles2, rs2, ag2, far2, fin2)
    out2_ref[...] = joined(fin2)
    store2 = pltpu.make_async_copy(out2_ref, out2_hbm, load_sem.at[1])
    store2.start()
    sum_end(4, tiles1, rs1, ag1, far1, fin1)
    out1_ref[...] = joined(fin1)
    store1 = pltpu.make_async_copy(out1_ref, out1_hbm, load_sem.at[2])
    store1.start()
    pltpu.make_async_copy(every, every, halo_send).wait()
    drain(mid_send, mid_out)
    drain(back_send, back_out)
    store.wait()
    store2.wait()
    store1.wait()


def lon_plan(n_lon):
    inner = 8 if n_lon % 8 == 0 else 2 if n_lon % 2 == 0 else n_lon
    return inner, n_lon // inner


def buffer_plan(tiles, n_lat):
    count = tiles.shape[0]
    chunks = min(n_lat, count)
    return chunks, count // chunks


def body(n_lat, n_lon, *operands):
    vmem = pltpu.VMEM
    inner, outer = lon_plan(n_lon)

    def sums(count):
        chunks = min(n_lat, count)
        depth = count // chunks
        return (
            vmem((count, 8, 128), F32),
            vmem((n_lat - 1, depth, 8, 128), F32),
            vmem((inner, depth, 8, 128), F32),
            vmem((outer, depth, 8, 128), F32),
            vmem((chunks, depth, 8, 128), F32),
        )

    tiles1, rs1, ag1, far1, fin1 = sums(TILES_W)
    tiles2, rs2, ag2, far2, fin2 = sums(TILES_C)
    scratch = [
        vmem((16, 16, WIDE), F32),
        vmem((8, 128 * TILES_W), F32),
        vmem((8, 128 * TILES_C), F32),
        vmem((16, 16, CHANNELS), BF16),
        vmem((16, 16, CHANNELS), BF16),
        vmem((1, CHANNELS), F32),
        vmem((CHANNELS, 3 * CHANNELS), BF16),
        vmem((CHANNELS, CHANNELS), BF16),
        vmem((HEADS, SPAN * SPAN), F32),
        vmem((1, CHANNELS), F32),
        vmem((CHANNELS, 3 * CHANNELS), BF16),
        vmem((CHANNELS, CHANNELS), BF16),
        vmem((HEADS, CROSS * CROSS), F32),
        pltpu.SemaphoreType.DMA((10,)),
        vmem((4, 4, 64, WIDE), BF16),
        vmem((HEADS, LANES_W), F32),
        vmem((3, HEADS, LANES_C), F32),
        vmem((3 * WIDE, CHANNELS), BF16),
        vmem((3 * WIDE, CHANNELS), BF16),
        vmem((WIDE, CHANNELS), BF16),
        vmem((WIDE, CHANNELS), BF16),
        vmem((2, CELLS, CELLS), BF16),
        vmem((2, 4, HEADS, 8, USED_W), F32),
        vmem((3, 4, HEADS, 8, USED_C), F32),
        vmem((2, 4, HEADS, 8, USED_W), F32),
        vmem((3, 4, HEADS, 8, USED_C), F32),
        vmem((4, CELLS, CHANNELS), F32),
        vmem((4, 8, 2, 2, 8, CHANNELS), F32),
        vmem((KEY_SIDE * 32, CHANNELS), F32),
        vmem((KEY_SIDE * 32, 1), F32),
        vmem((4, CELLS, WIDE), BF16),
        vmem((4, WIDE, CELLS), BF16),
        vmem((CELLS, WIDE), BF16),
        vmem((WIDE, CELLS), BF16),
        vmem((HEADS * CELLS, WIDE), BF16),
        vmem((HEADS * CELLS, WIDE), BF16),
        vmem((4, HEADS, 128, CELLS), BF16),
        vmem((WIDE, CELLS), F32),
        vmem((4, WIDE, CELLS), F32),
        vmem((4, CELLS, CHANNELS), BF16),
        vmem((4, HEADS, 1, CELLS), F32),
        vmem((4, HEADS, CELLS, CELLS), F32),
        vmem((HEADS, KEYS, CELLS), F32),
        vmem((HEADS, KEYS, CELLS), F32),
        vmem((CELLS, CHANNELS), F32),
        vmem((CELLS, CHANNELS), F32),
        vmem((4, CELLS, HEADS * CELLS), BF16),
        vmem((KEYS, HEADS * CELLS), BF16),
        vmem((CELLS, HEADS * CELLS), BF16),
        vmem((KEYS, HEADS * CELLS), BF16),
        vmem((KEYS, WIDE), BF16),
        vmem((KEYS, WIDE), BF16),
        vmem((WIDE, KEYS), BF16),
        vmem((KEY_SIDE, 32, CHANNELS), F32),
        vmem((3, 192, WIDE), BF16),
        vmem((3, 192, WIDE), BF16),
        vmem((3, 64, WIDE), BF16),
        vmem((3, 64, WIDE), BF16),
        vmem((8, 128 * TILES_W), F32),
        vmem((3, 8, 128 * TILES_C), F32),
        tiles1,
        tiles2,
        rs1,
        rs2,
        ag1,
        ag2,
        far1,
        far2,
        fin1,
        fin2,
        pltpu.SemaphoreType.DMA,
        pltpu.SemaphoreType.DMA,
        pltpu.SemaphoreType.DMA,
        pltpu.SemaphoreType.DMA,
        pltpu.SemaphoreType.DMA,
        pltpu.SemaphoreType.DMA,
        pltpu.SemaphoreType.DMA((8,)),
        pltpu.SemaphoreType.DMA((8,)),
    ]
    hbm = pl.BlockSpec(memory_space=pltpu.HBM)
    limit = 63 * 1024 * 1024
    shapes = (
        jax.ShapeDtypeStruct((16, 16, WIDE), F32),
        jax.ShapeDtypeStruct((8, 128 * TILES_W), F32),
        jax.ShapeDtypeStruct((8, 128 * TILES_C), F32),
    )
    grads, grad1, grad2 = pl.pallas_call(
        functools.partial(kernel, n_lat, n_lon),
        out_shape=shapes,
        in_specs=[hbm] * 10,
        out_specs=(hbm,) * 3,
        scratch_shapes=scratch,
        compiler_params=pltpu.CompilerParams(
            collective_id=0, has_side_effects=True, vmem_limit_bytes=limit
        ),
    )(*operands)
    return (
        grads[:, :, :CHANNELS],
        grad1[:HEADS, : SPAN * SPAN],
        grad2[:HEADS, : CROSS * CROSS],
    )


def solution(mesh):
    def local(
        features,
        cotangent,
        first_gain,
        window_qkv,
        window_proj,
        window_table,
        second_gain,
        cross_qkv,
        cross_proj,
        cross_table,
    ):
        return body(
            mesh.shape["lat"],
            mesh.shape["lon"],
            features,
            cotangent,
            first_gain.reshape(1, CHANNELS),
            window_qkv,
            window_proj,
            window_table,
            second_gain.reshape(1, CHANNELS),
            cross_qkv,
            cross_proj,
            cross_table,
        )

    return jax.shard_map(
        local,
        mesh=mesh,
        in_specs=(
            P("lat", "lon", None),
            P("lat", "lon", None),
            P(),
            P(),
            P(),
            P(),
            P(),
            P(),
            P(),
            P(),
        ),
        out_specs=(P("lat", "lon", None), P(), P()),
        check_vma=False,
    )
```
